256 devices in a mesh: gz: 64 (over z, y, x_lo), gy: 4 (over x_hi, core).
Axes of the slice: x: 4 (x_hi: 2, x_lo: 2; x = x_hi * 2 + x_lo), y: 4, z: 8, core: 2. Of those that a mesh axis runs over, the one named last changes fastest.
Arguments:
- point_feats: bfloat16 [16, 3670016], P(None, ('gz', 'gy')), may hold values from -6 to 6
- cell_index: int32 [3670016], P(('gz', 'gy')), may hold values from 0 to 2047, as said below
- send_slots: int32 [256, 2, 1792], P(('gz', 'gy')), may hold values from 0 to 14335, as said below
- send_count: int32 [256, 2], P(('gz', 'gy')), may hold values from 0 to 1792, as said below
- conv_weight: bfloat16 [16, 4, 3, 3, 3], replicated, may hold values from -0.625 to 0.625
- point_cot: bfloat16 [16, 4587520], P(None, ('gz', 'gy'))
Outputs:
- point_out: bfloat16 [16, 4587520], P(None, ('gz', 'gy'))
- point_grad: bfloat16 [16, 4587520], P(None, ('gz', 'gy'))
- weight_grad: float32 [16, 4, 3, 3, 3], replicated
The draws below stay inside these ranges and needn't reach their ends.
Inputs may be any that keep to these rules, and one draw needn't show every extreme that they name: `cell_index`: cells are numbered z-plane major, then y, then x within the owner's block; a point on a live list-0 entry lies in its new block's last z-plane, one on a live list-1 entry in its first z-plane. `send_slots`: slots of the device's own points; the live entries of one device are all distinct; entries that are not live are ignored. `send_count`: zero for list 0 of the lowest slab and list 1 of the highest; in every draw some device has 1792 live entries in list 0 and some device in list 1.
All inputs are finite; a program needn't handle non-finite values.
Results may differ from the reference program's by a relative error of at most 0.0056.
Values may be sent and summed in bfloat16 or wider, within the bound.
A program may use at most 64 MiB of HBM per device.

```python
import math
import jax
import jax.numpy as jnp
from jax import lax

CH = 16
GRP = 4
X = 128
CY = 8
CZ = 2
P_DEV = 14336
CAP = 1792
SLOTS_DEV = 17920
POINTS = 3670016
N_GZ = 64
N_GY = 4


def migration_plan(key):
    base_key = jax.random.fold_in(key, 7)
    count_key, pick_key, order_key = jax.random.split(base_key, 3)
    device_count = N_GZ * N_GY
    slab_ids = jnp.arange(device_count, dtype=jnp.int32) // N_GY
    counts = jax.random.randint(count_key, (device_count, 2), 0, CAP + 1, dtype=jnp.int32)
    counts = jnp.stack([jnp.where(slab_ids > 0, counts[:, 0], 0), jnp.where(slab_ids < N_GZ - 1, counts[:, 1], 0)], axis=1)
    picks = jax.random.randint(pick_key, (2,), 0, device_count - N_GY, dtype=jnp.int32)
    counts = counts.at[picks[0] + N_GY, 0].set(CAP).at[picks[1], 1].set(CAP)
    row_keys = jax.random.split(order_key, device_count)
    orders = jax.vmap(lambda row_key: jax.random.permutation(row_key, P_DEV))(row_keys)
    slot_lists = orders[:, :2 * CAP].reshape(device_count, 2, CAP)
    return (counts.astype(jnp.int32), slot_lists.astype(jnp.int32))


def draw_send_count(key, part):
    return migration_plan(key)[0]


def draw_send_slots(key, part):
    return migration_plan(key)[1]


def draw_cell_index(key, part):
    counts, slot_lists = migration_plan(key)
    device_count = N_GZ * N_GY
    plane_size = CY * X
    cells = jax.random.randint(jax.random.fold_in(key, 11), (device_count, P_DEV), 0, CZ * plane_size, dtype=jnp.int32)
    lane_ids = jnp.arange(CAP, dtype=jnp.int32)[None, :]
    dev_rows = jnp.arange(device_count, dtype=jnp.int32)[:, None]
    down_live = (lane_ids < counts[:, 0:1]).astype(jnp.int32)
    up_live = (lane_ids < counts[:, 1:2]).astype(jnp.int32)
    going_down = jnp.zeros((device_count, P_DEV), jnp.int32).at[dev_rows, slot_lists[:, 0]].max(down_live)
    going_up = jnp.zeros((device_count, P_DEV), jnp.int32).at[dev_rows, slot_lists[:, 1]].max(up_live)
    cells = jnp.where(going_down == 1, (CZ - 1) * plane_size + cells % plane_size, cells)
    cells = jnp.where(going_up == 1, cells % plane_size, cells)
    return cells.reshape(-1).astype(jnp.int32)


def draw_point_cot(key, part):
    column_count = SLOTS_DEV * N_GZ * N_GY
    ramp = 1.0 + 2.0 * jnp.arange(column_count, dtype=jnp.float32) / max(column_count - 1, 1)
    values = jnp.clip(jax.random.normal(key, (CH, column_count), jnp.float32), -6.0, 6.0)
    return (values * ramp[None, :]).astype(jnp.bfloat16)


def block_scale(key, shape, pieces, smallest, high):
    gain = 1.0
    for position, blocks in pieces:
        draws = jax.random.uniform(jax.random.fold_in(jax.random.fold_in(key, 6), position), (blocks,), jnp.float32, smallest / len(pieces), high / len(pieces))
        gain = gain * jnp.repeat(jnp.exp(draws), shape[position] // blocks).reshape((-1,) + (1,) * (len(shape) - 1 - position))
    return gain


def centred(key, shape, width, reach, pieces=(), held_as=jnp.bfloat16):
    gain = block_scale(key, shape, pieces, -0.22, 0.18) if pieces else 1.0
    values = jax.random.normal(key, shape, jnp.float32) * width * gain
    return jnp.minimum(jnp.maximum(values, -reach), reach).astype(held_as)


def setup_inputs(seed: int = 0) -> dict:
    key_list = jax.random.split(jax.random.key(seed), 7)
    return {
        "point_feats": centred(key_list[0], (CH, POINTS), 1.0, 6.0, ((1, 256),)),
        "cell_index": draw_cell_index(jax.random.fold_in(key_list[6], 71), 0),
        "send_slots": draw_send_slots(jax.random.fold_in(key_list[6], 71), 0),
        "send_count": draw_send_count(jax.random.fold_in(key_list[6], 71), 0),
        "conv_weight": centred(key_list[4], (CH, GRP, 3, 3, 3), (GRP * 27) ** -0.5, 0.625),
        "point_cot": draw_point_cot(jax.random.fold_in(key_list[6], 71), 0),
    }


def convolve(grid_wide, weight_wide):
    result = lax.conv_general_dilated(grid_wide[None], weight_wide, (1, 1, 1), [(1, 1), (1, 1), (1, 1)], dimension_numbers=('NCDHW', 'OIDHW', 'NCDHW'), feature_group_count=CH // GRP, precision=lax.Precision.HIGHEST)
    return result[0]

def reference(point_feats, cell_index, send_slots, send_count, conv_weight, point_cot):
    device_count = N_GZ * N_GY
    own_feats = point_feats.reshape(CH, device_count, P_DEV)
    own_cells = cell_index.reshape(device_count, P_DEV)
    lane_ids = jnp.arange(CAP, dtype=jnp.int32)
    listed = lane_ids[None, None, :] < send_count[:, :, None]
    dev_rows = jnp.arange(device_count, dtype=jnp.int32)[:, None]
    targets = jnp.where(listed, send_slots, P_DEV).astype(jnp.int32)
    leaving = jnp.zeros((device_count, P_DEV + 1), jnp.int32)
    leaving = leaving.at[dev_rows, targets[:, 0]].max(1).at[dev_rows, targets[:, 1]].max(1)[:, :P_DEV]
    staying = leaving == 0
    zero_feat = jnp.zeros((), own_feats.dtype)
    kept_feats = jnp.where(staying[None], own_feats, zero_feat)
    kept_cells = jnp.where(staying, own_cells, -1)
    dev_cube = jnp.arange(device_count, dtype=jnp.int32)[:, None, None]
    sent_feats = jnp.where(listed[None], own_feats[:, dev_cube, send_slots], zero_feat)
    sent_cells = jnp.where(listed, own_cells[dev_cube, send_slots], -1)
    sent_feats = sent_feats.reshape(CH, N_GZ, N_GY, 2, CAP)
    sent_cells = sent_cells.reshape(N_GZ, N_GY, 2, CAP)
    blank_feats = jnp.zeros((CH, 1, N_GY, CAP), own_feats.dtype)
    blank_cells = jnp.full((1, N_GY, CAP), -1, jnp.int32)
    below_feats = jnp.concatenate([blank_feats, sent_feats[:, :-1, :, 1]], axis=1)
    below_cells = jnp.concatenate([blank_cells, sent_cells[:-1, :, 1]], axis=0)
    above_feats = jnp.concatenate([sent_feats[:, 1:, :, 0], blank_feats], axis=1)
    above_cells = jnp.concatenate([sent_cells[1:, :, 0], blank_cells], axis=0)
    moved_feats = jnp.concatenate([kept_feats.reshape(CH, N_GZ, N_GY, P_DEV), below_feats, above_feats], axis=3)
    moved_cells = jnp.concatenate([kept_cells.reshape(N_GZ, N_GY, P_DEV), below_cells, above_cells], axis=2)
    present = moved_cells >= 0
    local_cell = jnp.maximum(moved_cells, 0)
    plane_z = local_cell // (CY * X)
    row_y = local_cell // X % CY
    col_x = local_cell % X
    slab_ids = jnp.arange(N_GZ, dtype=jnp.int32)[:, None, None]
    split_ids = jnp.arange(N_GY, dtype=jnp.int32)[None, :, None]
    cell_total = CZ * N_GZ * CY * N_GY * X
    flat_cell = ((slab_ids * CZ + plane_z) * (CY * N_GY) + split_ids * CY + row_y) * X + col_x
    flat_cell = jnp.where(present, flat_cell, cell_total).reshape(-1).astype(jnp.int32)
    present_flat = present.reshape(-1)
    counts = jnp.zeros((cell_total + 1,), jnp.float32).at[flat_cell].add(1.0)[:cell_total]
    sums = jnp.zeros((CH, cell_total + 1), jnp.float32).at[:, flat_cell].add(moved_feats.reshape(CH, -1).astype(jnp.float32))[:, :cell_total]
    cot_sums = jnp.zeros((CH, cell_total + 1), jnp.float32).at[:, flat_cell].add(point_cot.astype(jnp.float32))[:, :cell_total]
    divisor = jnp.maximum(counts, 1.0)
    grid_vals = (sums / divisor).astype(jnp.bfloat16).reshape(CH, CZ * N_GZ, CY * N_GY, X)
    grid_vals = lax.optimization_barrier(grid_vals)
    preact, pullback = jax.vjp(convolve, grid_vals.astype(jnp.float32), conv_weight.astype(jnp.float32))
    preact_flat = preact.reshape(CH, cell_total)
    activ = jax.nn.silu(preact_flat)
    safe_cell = jnp.minimum(flat_cell, cell_total - 1)
    point_out = jnp.where(present_flat[None], activ[:, safe_cell], 0.0).astype(jnp.bfloat16)
    sigma = jax.nn.sigmoid(preact_flat)
    grad_pre = (cot_sums * sigma * (1.0 + preact_flat * (1.0 - sigma))).astype(jnp.bfloat16)
    grad_pre = lax.optimization_barrier(grad_pre)
    grad_grid, grad_weight = pullback(grad_pre.astype(jnp.float32).reshape(preact.shape))
    weight_grad = grad_weight / math.sqrt(cell_total)
    grad_flat = grad_grid.reshape(CH, cell_total)
    point_grad = jnp.where(present_flat[None], grad_flat[:, safe_cell] / divisor[safe_cell][None], 0.0).astype(jnp.bfloat16)
    return (point_out, point_grad, weight_grad)
```

```python
import functools
import math

import jax
import jax.numpy as jnp
from jax import lax
from jax.experimental import pallas as pl
from jax.experimental.pallas import tpu as pltpu
from jax.sharding import PartitionSpec as P

CH = 16
GRP = 4
X = 128
CY = 8
CZ = 2
S = 1792
OWN = 8
ALL = OWN + 2
LO = 256
MESH = pl.DeviceIdType.MESH
f32 = jnp.float32
bf16 = jnp.bfloat16
NT = (((1,), (1,)), ((), ()))

UP_MSG = tuple(range(4, 12))
DOWN_MSG = (0, 1, 2, 3, 12, 13, 14, 15)
STAY = (0, 1, 2, 3, 8, 9, 10, 11)


def one_hot(row, count):
    ids = lax.broadcasted_iota(jnp.int32, (count, row.shape[1]), 0).astype(f32).astype(bf16)
    return jnp.where(ids == row, jnp.ones((), bf16), jnp.zeros((), bf16))


def masked_rows(row, values, codes):
    zero = jnp.zeros((), bf16)
    return [jnp.where(row == jnp.full((), code, bf16), values, zero) for code in codes]


def sigmoid(v):
    return 1.0 / (1.0 + jnp.exp(-v))


def kernel(
    feats_hbm, cot_hbm, cells_ref, slots_ref, count_ref, weight_ref,
    out_hbm, grad_hbm, wgrad_ref,
    feats, cot, out_buf, grad_buf, onehots, codes, lows, acc, acc_cot,
    list_send, list_recv,
    up_send, down_send, up_recv, down_recv,
    side_send, side_recv, corner_send, corner_recv,
    grid, gpad, patches, gp3, table, divisors, wmat, counts_in, pre,
    part, gather_1, total_1, gather_2,
    load_sem, store_sem, send_sem, recv_sem, send_2, recv_2, red_send, red_recv,
    *, comm,
):
    a = lax.axis_index("gz")
    b = lax.axis_index("gy")
    n_a = lax.axis_size("gz")
    n_b = lax.axis_size("gy")
    z_p = a // 8
    y_p = lax.rem(a // 2, 4)
    x_p = lax.rem(a, 2)

    load_feats = pltpu.make_async_copy(feats_hbm, feats, load_sem.at[0])
    load_cot = pltpu.make_async_copy(cot_hbm, cot, load_sem.at[1])
    load_feats.start()
    load_cot.start()

    def near(da, db):
        return (lax.rem(a + da + n_a, n_a), lax.rem(b + db + n_b, n_b))

    def peer_1(d):
        return (z_p * 8 + lax.rem(y_p + d // 4, 4) * 2 + x_p, lax.rem(b + lax.rem(d, 4), 4))

    def peer_2(d):
        return (lax.rem(z_p + d // 2, 8) * 8 + y_p * 2 + lax.rem(x_p + lax.rem(d, 2), 2), b)

    around = [(da, db) for da in (-1, 0, 1) for db in (-1, 0, 1) if (da, db) != (0, 0)]
    if comm:
        barrier = pltpu.get_barrier_semaphore()
        for da, db in around:
            pl.semaphore_signal(barrier, inc=1, device_id=near(da, db), device_id_type=MESH)

        def greet(d, carry):
            pl.semaphore_signal(barrier, inc=1, device_id=peer_1(d), device_id_type=MESH)
            pl.semaphore_signal(barrier, inc=1, device_id=peer_2(d), device_id_type=MESH)
            return carry

        lax.fori_loop(1, 16, greet, 0)

    tap_row = lax.broadcasted_iota(jnp.int32, (144, 128), 0)
    tap_col = lax.broadcasted_iota(jnp.int32, (144, 128), 1)
    tap_base = jnp.bitwise_and(tap_row, 3) * 27 + jnp.right_shift(tap_row, 4) * 3
    spread = [tap_base + col_k == tap_col for col_k in range(3)]
    out_ch = lax.broadcasted_iota(jnp.int32, (CH, 144), 0)
    in_ch = jnp.bitwise_and(lax.broadcasted_iota(jnp.int32, (CH, 144), 1), 15)
    same_group = jnp.right_shift(out_ch, 2) == jnp.right_shift(in_ch, 2)
    weight = weight_ref[...]
    for col_k in range(3):
        picked = lax.dot_general(
            weight, spread[col_k].astype(bf16), NT, preferred_element_type=f32
        )
        wmat[16 * col_k : 16 * col_k + 16, :] = jnp.where(same_group, picked, 0.0).astype(bf16)

    cells = jnp.concatenate(
        [cells_ref[pl.ds(0, 56, stride=2), :], cells_ref[pl.ds(1, 56, stride=2), :]], axis=1
    )
    cell_y = jnp.right_shift(jnp.bitwise_and(cells, 1023), 7) * 128
    cell_x = jnp.bitwise_and(cells, 127)
    pad = jnp.zeros((8, LO), f32)
    cell_table = jnp.concatenate(
        [cell_y.astype(f32), pad, cell_x.astype(f32), pad], axis=0
    ).astype(bf16)
    lane = lax.broadcasted_iota(jnp.int32, (1, S), 1)
    leaving = jnp.zeros((64, LO), f32)
    for side in range(2):
        listed = lane < count_ref[0, side]
        slot = slots_ref[0, side : side + 1, :]
        slot_hi = jnp.where(listed, jnp.right_shift(slot, 8), -1)
        hot_lo = one_hot(jnp.bitwise_and(slot, 255).astype(f32).astype(bf16), LO)
        hot_hi = lax.broadcasted_iota(jnp.int32, (64, S), 0) == slot_hi
        leaving += lax.dot_general(
            hot_hi.astype(f32).astype(bf16), hot_lo, NT, preferred_element_type=f32
        )
        found = jnp.dot(cell_table, hot_lo, preferred_element_type=f32)
        place = jnp.sum(jnp.where(hot_hi, found[:64] + found[64:], 0.0), axis=0, keepdims=True)
        list_send[side] = jnp.where(listed, place, -1.0)
    code = (
        jnp.bitwise_and(jnp.right_shift(cells, 8), 3) + jnp.right_shift(cells, 10) * 8
    ).astype(f32) + 4.0 * leaving[:56]
    low = jnp.bitwise_and(cells, 255).astype(f32)
    for row in range(7 * OWN):
        k, j = divmod(row, 7)
        codes[k, :, LO * j : LO * (j + 1)] = code[row : row + 1]
        lows[k, :, LO * j : LO * (j + 1)] = low[row : row + 1]

    load_feats.wait()
    acc[...] = jnp.zeros_like(acc)

    def splat_own(k, carry):
        hot = one_hot(lows[k].astype(bf16), LO)
        onehots[k] = hot
        row = codes[k].astype(bf16)
        values = feats[:, pl.ds(pl.multiple_of(k * S, 128), S)]
        rows = masked_rows(row, values, range(16)) + [one_hot(row, 16)]
        acc[...] += lax.dot_general(
            jnp.concatenate(rows, axis=0), hot, NT, preferred_element_type=f32
        )
        return carry

    lax.fori_loop(0, OWN, splat_own, 0)

    counts = acc[256:272, :]
    count_hi = jnp.floor(counts * (1.0 / 256.0))
    count_lo = (counts - 256.0 * count_hi).astype(bf16)
    count_hi = count_hi.astype(bf16)

    def block(number, row):
        lanes = slice(128 * (row % 2), 128 * (row % 2) + 128)
        return acc[16 * number : 16 * number + 16, lanes].astype(bf16)

    def rows_of(numbers, first_row):
        return [block(4 * plane + first_row // 2, first_row) for plane in numbers]

    for ref, members in ((up_send, UP_MSG), (down_send, DOWN_MSG)):
        for i, number in enumerate(members):
            ref[2 * i] = block(number, 0)
            ref[2 * i + 1] = block(number, 1)
        ref[16] = count_lo[:, :128]
        ref[17] = count_lo[:, 128:]
        ref[18] = count_hi[:, :128]
        ref[19] = count_hi[:, 128:]
    for side in range(2):
        lanes = slice(128 * side, 128 * side + 128)
        for i, plane in enumerate(range(4)):
            side_send[side, i] = block(4 * plane + 3 * side, side)
        side_send[side, 4] = count_lo[:, lanes]
        side_send[side, 5] = count_hi[:, lanes]
        for vertical, planes in ((0, (0, 3)), (1, (1, 2))):
            for i, plane in enumerate(planes):
                corner_send[2 * vertical + side, i] = block(4 * plane + 3 * side, side)
            corner_send[2 * vertical + side, 2] = count_lo[:, lanes]
            corner_send[2 * vertical + side, 3] = count_hi[:, lanes]

    copies = []

    def send(src, dst, place, da, db):
        if comm:
            copy = pltpu.make_async_remote_copy(
                src_ref=src, dst_ref=dst, send_sem=send_sem.at[place],
                recv_sem=recv_sem.at[place], device_id=near(da, db), device_id_type=MESH,
            )
            copy.start()
            copies.append(copy)

    if comm:
        pl.semaphore_wait(barrier, len(around) + 30)
    send(list_send.at[0], list_recv.at[1], 0, -1, 0)
    send(list_send.at[1], list_recv.at[0], 1, 1, 0)
    send(up_send, up_recv, 2, 1, 0)
    send(down_send, down_recv, 3, -1, 0)
    for side in range(2):
        db = 2 * side - 1
        send(side_send.at[side], side_recv.at[side], 4 + side, 0, db)
        for vertical in range(2):
            i = 2 * vertical + side
            send(corner_send.at[i], corner_recv.at[i], 6 + i, 2 * vertical - 1, db)

    load_cot.wait()
    acc_cot[...] = jnp.zeros_like(acc_cot)

    def splat_cot(k, carry):
        row = codes[k].astype(bf16)
        values = cot[:, pl.ds(pl.multiple_of(k * S, 128), S)]
        acc_cot[...] += lax.dot_general(
            jnp.concatenate(masked_rows(row, values, STAY), axis=0), onehots[k], NT,
            preferred_element_type=f32,
        )
        return carry

    lax.fori_loop(0, OWN, splat_cot, 0)

    if comm:
        copies[0].wait()
        copies[1].wait()
    for side in range(2):
        present = (a > 0) if side == 0 else (a < n_a - 1)
        place = jnp.where(present, list_recv[side], -1.0).astype(jnp.int32)
        live = place >= 0
        row = jnp.where(live, jnp.right_shift(place, 8) + 8 * side, 16).astype(f32)
        codes[OWN + side] = row
        hot = one_hot(jnp.bitwise_and(place, 255).astype(f32).astype(bf16), LO)
        onehots[OWN + side] = hot
        values = cot[:, (OWN + side) * S : (OWN + side + 1) * S]
        members = STAY[4 * side : 4 * side + 4]
        acc_cot[64 * side : 64 * side + 64, :] += lax.dot_general(
            jnp.concatenate(masked_rows(row.astype(bf16), values, members), axis=0), hot, NT,
            preferred_element_type=f32,
        )

    if comm:
        for copy in copies[2:]:
            copy.wait()
    has_below = a > 0
    has_above = a < n_a - 1
    has_left = b > 0
    has_right = b < n_b - 1

    def unpack(ref, at, flag):
        total = ref[at + 1].astype(f32) * 256.0 + ref[at].astype(f32)
        return jnp.where(flag, total, 0.0)

    for i, (ref, flag) in enumerate(((up_recv, has_below), (down_recv, has_above))):
        for half in range(2):
            total = ref[18 + half].astype(f32) * 256.0 + ref[16 + half].astype(f32)
            counts_in[2 * i + half] = jnp.where(flag, total, 0.0)
    side_flag = (has_right, has_left)
    for side in range(2):
        for i, (ref, at) in enumerate(
            ((side_recv.at[side], 4), (corner_recv.at[side], 2), (corner_recv.at[2 + side], 2))
        ):
            flag = side_flag[side]
            if i == 1:
                flag = jnp.logical_and(flag, has_above)
            if i == 2:
                flag = jnp.logical_and(flag, has_below)
            total = ref[at + 1].astype(f32) * 256.0 + ref[at].astype(f32)
            counts_in[(4 if i == 0 else 4 + 2 * i) + side] = jnp.where(flag, total, 0.0)

    def mean(sums, count):
        return sums / jnp.maximum(count, 1.0)

    sources = (
        (3, up_recv, 4, 2, 0, has_below),
        (0, up_recv, 0, 1, 0, has_below),
        (2, down_recv, 4, 3, 2, has_above),
        (1, down_recv, 0, 0, 2, has_above),
    )
    for plane, (mine, ref, at, theirs, where, flag) in enumerate(sources):
        for row in range(8):
            half = row % 2
            lanes = slice(128 * half, 128 * half + 128)
            number = 4 * mine + row // 2
            other = 4 * theirs + row // 2
            got = ref[2 * (at + row // 2) + half].astype(f32)
            sums = acc[16 * number : 16 * number + 16, lanes] + jnp.where(flag, got, 0.0)
            count = acc[256 + number : 257 + number, lanes]
            count = count + counts_in[where + half, other : other + 1, :]
            divisor = jnp.broadcast_to(jnp.maximum(count, 1.0), (CH, 128))
            grid[plane, 1 + row] = (sums / divisor).astype(bf16)
            if plane in (1, 2):
                divisors[8 * (plane - 1) + row] = divisor
    for side in range(2):
        flag = side_flag[side]
        y_hi = 3 * side
        halo = (
            (3, 1, 1, 2, has_below),
            (0, 1, 0, 1, has_below),
            (2, 0, 1, 3, has_above),
            (1, 0, 0, 0, has_above),
        )
        for plane, (direct, vertical, at, theirs, vertical_flag) in enumerate(halo):
            corner = 2 * vertical + side
            both = jnp.logical_and(flag, vertical_flag)
            sums = jnp.where(flag, side_recv[side, direct].astype(f32), 0.0)
            sums = sums + jnp.where(both, corner_recv[corner, at].astype(f32), 0.0)
            mine = 4 * direct + y_hi
            other = 4 * theirs + y_hi
            kind = 6 if vertical == 0 else 8
            count = counts_in[4 + side, mine : mine + 1, :]
            count = count + counts_in[kind + side, other : other + 1, :]
            grid[plane, 9 * (1 - side)] = mean(sums, count).astype(bf16)

    lane = lax.broadcasted_iota(jnp.int32, (CH, X), 1)
    first_x = lane == 0
    last_x = lane == X - 1
    for z in range(CZ):
        stacked = jnp.concatenate(
            [
                jnp.concatenate([grid[z + u, v + y] for y in range(CY)], axis=1)
                for u in range(3)
                for v in range(3)
            ],
            axis=0,
        )
        patches[z] = stacked
        pre[...] = jnp.dot(wmat[...], stacked, preferred_element_type=f32)
        for y in range(CY):
            lanes = slice(128 * y, 128 * y + 128)
            low_x = pltpu.roll(pre[0:16, lanes], 1, 1)
            high_x = pltpu.roll(pre[32:48, lanes], X - 1, 1)
            value = (
                pre[16:32, lanes]
                + jnp.where(first_x, 0.0, low_x)
                + jnp.where(last_x, 0.0, high_x)
            )
            sigma = sigmoid(value)
            group = 4 * z + y // 2
            half = slice(128 * (y % 2), 128 * (y % 2) + 128)
            table[16 * group : 16 * group + 16, half] = (value * sigma).astype(bf16)
            cot_sum = acc_cot[16 * group : 16 * group + 16, half]
            gpad[z + 1, y + 1] = (cot_sum * sigma * (1.0 + value * (1.0 - sigma))).astype(bf16)

    copies_2 = []

    def send_2nd(src, dst, place, da, db):
        if comm:
            copy = pltpu.make_async_remote_copy(
                src_ref=src, dst_ref=dst, send_sem=send_2.at[place],
                recv_sem=recv_2.at[place], device_id=near(da, db), device_id_type=MESH,
            )
            copy.start()
            copies_2.append(copy)

    send_2nd(gpad.at[1, pl.ds(1, 8)], gpad.at[3, pl.ds(1, 8)], 0, -1, 0)
    send_2nd(gpad.at[2, pl.ds(1, 8)], gpad.at[0, pl.ds(1, 8)], 1, 1, 0)
    send_2nd(gpad.at[pl.ds(1, 2), 1], gpad.at[pl.ds(1, 2), 9], 2, 0, -1)
    send_2nd(gpad.at[pl.ds(1, 2), 8], gpad.at[pl.ds(1, 2), 0], 3, 0, 1)
    send_2nd(gpad.at[1, 1], gpad.at[3, 9], 4, -1, -1)
    send_2nd(gpad.at[1, 8], gpad.at[3, 0], 5, -1, 1)
    send_2nd(gpad.at[2, 1], gpad.at[0, 9], 6, 1, -1)
    send_2nd(gpad.at[2, 8], gpad.at[0, 0], 7, 1, 1)

    def move(plane, row):
        value = gpad[plane, row]
        wide = value.astype(f32)
        gp3[plane, row, 0:16] = jnp.where(last_x, 0.0, pltpu.roll(wide, X - 1, 1)).astype(bf16)
        gp3[plane, row, 16:32] = value
        gp3[plane, row, 32:48] = jnp.where(first_x, 0.0, pltpu.roll(wide, 1, 1)).astype(bf16)

    wide_grad = jnp.zeros((48, 144), f32)
    for z in range(CZ):
        for y in range(CY):
            move(z + 1, y + 1)
        moved = jnp.concatenate([gp3[z + 1, y + 1] for y in range(CY)], axis=1)
        wide_grad += lax.dot_general(moved, patches[z], NT, preferred_element_type=f32)
    compact = jnp.zeros((CH, 128), f32)
    for col_k in range(3):
        kept = jnp.where(same_group, wide_grad[16 * col_k : 16 * col_k + 16], 0.0)
        compact += jnp.dot(
            kept, spread[col_k].astype(f32), preferred_element_type=f32,
            precision=lax.Precision.HIGHEST,
        )
    part[...] = compact

    def spread_1(d):
        return pltpu.make_async_remote_copy(
            src_ref=part, dst_ref=gather_1.at[d - 1], send_sem=red_send.at[0, d - 1],
            recv_sem=red_recv.at[0, d - 1], device_id=peer_1(d), device_id_type=MESH,
        )

    def spread_2(d):
        return pltpu.make_async_remote_copy(
            src_ref=total_1, dst_ref=gather_2.at[d - 1], send_sem=red_send.at[1, d - 1],
            recv_sem=red_recv.at[1, d - 1], device_id=peer_2(d), device_id_type=MESH,
        )

    def start_all(make):
        def body(d, carry):
            make(d).start()
            return carry

        lax.fori_loop(1, 16, body, 0)

    def wait_all(make):
        def body(d, carry):
            make(d).wait()
            return carry

        lax.fori_loop(1, 16, body, 0)

    if comm:
        start_all(spread_1)

    def read_back(into):
        def body(k, carry):
            found = jnp.dot(table[...], onehots[k], preferred_element_type=f32)
            row = codes[k]
            value = jnp.zeros((CH, S), f32)
            for i, number in enumerate(STAY):
                value = jnp.where(row == float(number), found[16 * i : 16 * i + 16], value)
            into[:, pl.ds(pl.multiple_of(k * S, 128), S)] = value.astype(bf16)
            return carry

        lax.fori_loop(0, ALL, body, 0)

    read_back(out_buf)
    store_out = pltpu.make_async_copy(out_buf, out_hbm, store_sem.at[0])
    store_out.start()

    if comm:
        wait_all(spread_1)
    total = part[...]
    for d in range(15):
        total = total + gather_1[d]
    total_1[...] = total
    if comm:
        start_all(spread_2)

    for copy in copies_2:
        copy.wait()
    blank = jnp.zeros((CH, X), bf16)

    def clear(flag, places):
        @pl.when(flag)
        def _():
            for plane, row in places:
                gpad[plane, row] = blank

    clear(a == 0, [(0, row) for row in range(10)])
    clear(a == n_a - 1, [(3, row) for row in range(10)])
    clear(b == 0, [(plane, 0) for plane in range(4)])
    clear(b == n_b - 1, [(plane, 9) for plane in range(4)])
    for plane in range(4):
        for row in range(10):
            if plane in (0, 3) or row in (0, 9):
                move(plane, row)
    result = [None] * 16
    for plane in range(4):
        moved = jnp.concatenate([gp3[plane, row] for row in range(10)], axis=1)
        taps = lax.dot_general(
            wmat[...], moved, (((0,), (0,)), ((), ())), preferred_element_type=f32
        )
        for u in range(3):
            z = plane - 2 + u
            if z not in (0, 1):
                continue
            for v in range(3):
                rows = slice(16 * (3 * u + v), 16 * (3 * u + v) + 16)
                for y in range(CY):
                    source = y + 2 - v
                    term = taps[rows, 128 * source : 128 * source + 128]
                    i = 8 * z + y
                    result[i] = term if result[i] is None else result[i] + term
    for i in range(16):
        group = i // 2
        half = slice(128 * (i % 2), 128 * (i % 2) + 128)
        table[16 * group : 16 * group + 16, half] = (result[i] / divisors[i]).astype(bf16)
    read_back(grad_buf)
    store_grad = pltpu.make_async_copy(grad_buf, grad_hbm, store_sem.at[1])
    store_grad.start()

    if comm:
        wait_all(spread_2)
    total = total_1[...]
    for d in range(15):
        total = total + gather_2[d]
    wgrad_ref[...] = total * (1.0 / math.sqrt(CZ * CY * X * n_a * n_b))
    store_out.wait()
    store_grad.wait()


def fused(feats, cot, cells, slots, count, weight, comm=True):
    hbm = pl.BlockSpec(memory_space=pl.ANY)
    vmem = pl.BlockSpec(memory_space=pltpu.VMEM)
    smem = pl.BlockSpec(memory_space=pltpu.SMEM)
    slots_all = ALL * S
    dma = pltpu.SemaphoreType.DMA
    return pl.pallas_call(
        functools.partial(kernel, comm=comm),
        out_shape=[
            jax.ShapeDtypeStruct((CH, slots_all), bf16),
            jax.ShapeDtypeStruct((CH, slots_all), bf16),
            jax.ShapeDtypeStruct((CH, 128), f32),
        ],
        in_specs=[hbm, hbm, vmem, vmem, smem, vmem],
        out_specs=[hbm, hbm, vmem],
        scratch_shapes=[
            pltpu.VMEM((CH, OWN * S), bf16),
            pltpu.VMEM((CH, slots_all), bf16),
            pltpu.VMEM((CH, slots_all), bf16),
            pltpu.VMEM((CH, slots_all), bf16),
            pltpu.VMEM((ALL, LO, S), bf16),
            pltpu.VMEM((ALL, 1, S), f32),
            pltpu.VMEM((OWN, 1, S), f32),
            pltpu.VMEM((272, LO), f32),
            pltpu.VMEM((128, LO), f32),
            pltpu.VMEM((2, 1, S), f32),
            pltpu.VMEM((2, 1, S), f32),
            pltpu.VMEM((20, CH, 128), bf16),
            pltpu.VMEM((20, CH, 128), bf16),
            pltpu.VMEM((20, CH, 128), bf16),
            pltpu.VMEM((20, CH, 128), bf16),
            pltpu.VMEM((2, 6, CH, 128), bf16),
            pltpu.VMEM((2, 6, CH, 128), bf16),
            pltpu.VMEM((4, 4, CH, 128), bf16),
            pltpu.VMEM((4, 4, CH, 128), bf16),
            pltpu.VMEM((4, 10, CH, 128), bf16),
            pltpu.VMEM((4, 10, CH, 128), bf16),
            pltpu.VMEM((CZ, 144, CY * X), bf16),
            pltpu.VMEM((4, 10, 48, 128), bf16),
            pltpu.VMEM((128, LO), bf16),
            pltpu.VMEM((16, CH, 128), f32),
            pltpu.VMEM((48, 144), bf16),
            pltpu.VMEM((10, CH, 128), f32),
            pltpu.VMEM((48, CY * X), f32),
            pltpu.VMEM((CH, 128), f32),
            pltpu.VMEM((15, CH, 128), f32),
            pltpu.VMEM((CH, 128), f32),
            pltpu.VMEM((15, CH, 128), f32),
            dma((2,)),
            dma((2,)),
            dma((10,)),
            dma((10,)),
            dma((8,)),
            dma((8,)),
            dma((2, 15)),
            dma((2, 15)),
        ],
        compiler_params=pltpu.CompilerParams(
            vmem_limit_bytes=48 << 20,
            **(dict(collective_id=0, has_side_effects=True) if comm else {}),
        ),
    )(feats, cot, cells, slots, count, weight)


def local(point_feats, cell_index, send_slots, send_count, conv_weight, point_cot):
    cells = cell_index.reshape(-1, 128)
    weight = jnp.pad(conv_weight.reshape(CH, GRP * 27), ((0, 0), (0, 128 - GRP * 27)))
    out, grad, wgrad = fused(point_feats, point_cot, cells, send_slots, send_count, weight)
    return out, grad, wgrad[:, : GRP * 27].reshape(conv_weight.shape)


def solution(mesh):
    placed = (
        P(None, ("gz", "gy")),
        P(("gz", "gy")),
        P(("gz", "gy"), None, None),
        P(("gz", "gy"), None),
        P(),
        P(None, ("gz", "gy")),
    )
    return jax.shard_map(
        local,
        mesh=mesh,
        in_specs=placed,
        out_specs=(P(None, ("gz", "gy")), P(None, ("gz", "gy")), P()),
        check_vma=False,
    )
```

```python
import functools
import math

import jax
import jax.numpy as jnp
from jax import lax
from jax.experimental import pallas as pl
from jax.experimental.pallas import tpu as pltpu
from jax.sharding import PartitionSpec as P

CH = 16
GRP = 4
X = 128
CY = 8
CZ = 2
S = 1792
OWN = 8
ALL = OWN + 2
LO = 256
MESH = pl.DeviceIdType.MESH
f32 = jnp.float32
bf16 = jnp.bfloat16
NT = (((1,), (1,)), ((), ()))

UP_MSG = tuple(range(4, 12))
DOWN_MSG = (0, 1, 2, 3, 12, 13, 14, 15)
STAY = (0, 1, 2, 3, 8, 9, 10, 11)


def one_hot(row, count):
    ids = lax.broadcasted_iota(jnp.int32, (count, row.shape[1]), 0).astype(f32).astype(bf16)
    return jnp.where(ids == row, jnp.ones((), bf16), jnp.zeros((), bf16))


def masked_rows(row, values, codes):
    zero = jnp.zeros((), bf16)
    return [jnp.where(row == jnp.full((), code, bf16), values, zero) for code in codes]


def sigmoid(v):
    return 1.0 / (1.0 + jnp.exp(-v))


def kernel(
    feats_hbm, cot_hbm, cells_ref, slots_ref, count_ref, weight_ref,
    out_hbm, grad_hbm, wgrad_ref,
    feats, cot, out_buf, grad_buf, onehots, codes, lows, acc, acc_cot,
    list_send, list_recv,
    up_send, down_send, up_recv, down_recv,
    side_send, side_recv, corner_send, corner_recv,
    grid, gpad, patches, gp3, table, divisors, wmat, counts_in, pre,
    part, gather_1, total_1, gather_2,
    load_sem, store_sem, send_sem, recv_sem, send_2, recv_2, red_send, red_recv,
    *, comm,
):
    a = lax.axis_index("gz")
    b = lax.axis_index("gy")
    n_a = lax.axis_size("gz")
    n_b = lax.axis_size("gy")
    z_p = a // 8
    y_p = lax.rem(a // 2, 4)
    x_p = lax.rem(a, 2)

    load_feats = pltpu.make_async_copy(feats_hbm, feats, load_sem.at[0])
    load_cot = pltpu.make_async_copy(cot_hbm, cot, load_sem.at[1])
    load_feats.start()
    load_cot.start()

    def near(da, db):
        return (lax.rem(a + da + n_a, n_a), lax.rem(b + db + n_b, n_b))

    def peer_1(d):
        return (z_p * 8 + lax.rem(y_p + d // 4, 4) * 2 + x_p, lax.rem(b + lax.rem(d, 4), 4))

    def peer_2(d):
        return (lax.rem(z_p + d // 2, 8) * 8 + y_p * 2 + lax.rem(x_p + lax.rem(d, 2), 2), b)

    around = [(da, db) for da in (-1, 0, 1) for db in (-1, 0, 1) if (da, db) != (0, 0)]
    if comm:
        barrier = pltpu.get_barrier_semaphore()
        for da, db in around:
            pl.semaphore_signal(barrier, inc=1, device_id=near(da, db), device_id_type=MESH)

        def greet(d, carry):
            pl.semaphore_signal(barrier, inc=1, device_id=peer_1(d), device_id_type=MESH)
            pl.semaphore_signal(barrier, inc=1, device_id=peer_2(d), device_id_type=MESH)
            return carry

        lax.fori_loop(1, 16, greet, 0)

    tap_row = lax.broadcasted_iota(jnp.int32, (144, 128), 0)
    tap_col = lax.broadcasted_iota(jnp.int32, (144, 128), 1)
    tap_base = jnp.bitwise_and(tap_row, 3) + jnp.right_shift(tap_row, 4) * (3 * GRP)
    spread = [tap_base + GRP * col_k == tap_col for col_k in range(3)]
    out_ch = lax.broadcasted_iota(jnp.int32, (CH, 144), 0)
    in_ch = jnp.bitwise_and(lax.broadcasted_iota(jnp.int32, (CH, 144), 1), 15)
    same_group = jnp.right_shift(out_ch, 2) == jnp.right_shift(in_ch, 2)
    weight = jnp.concatenate(
        [weight_ref[i].astype(f32) for i in range(27)] + [jnp.zeros((20, CH), f32)], axis=0
    ).T.astype(bf16)
    for col_k in range(3):
        picked = lax.dot_general(
            weight, spread[col_k].astype(bf16), NT, preferred_element_type=f32
        )
        wmat[16 * col_k : 16 * col_k + 16, :] = jnp.where(same_group, picked, 0.0).astype(bf16)

    cells = jnp.concatenate(
        [cells_ref[pl.ds(0, 56, stride=2), :], cells_ref[pl.ds(1, 56, stride=2), :]], axis=1
    )
    cell_y = jnp.right_shift(jnp.bitwise_and(cells, 1023), 7) * 128
    cell_x = jnp.bitwise_and(cells, 127)
    pad = jnp.zeros((8, LO), f32)
    cell_table = jnp.concatenate(
        [cell_y.astype(f32), pad, cell_x.astype(f32), pad], axis=0
    ).astype(bf16)
    lane = lax.broadcasted_iota(jnp.int32, (1, S), 1)
    leaving = jnp.zeros((64, LO), f32)
    for side in range(2):
        listed = lane < count_ref[0, side]
        slot = slots_ref[0, side : side + 1, :]
        slot_hi = jnp.where(listed, jnp.right_shift(slot, 8), -1)
        hot_lo = one_hot(jnp.bitwise_and(slot, 255).astype(f32).astype(bf16), LO)
        hot_hi = lax.broadcasted_iota(jnp.int32, (64, S), 0) == slot_hi
        leaving += lax.dot_general(
            hot_hi.astype(f32).astype(bf16), hot_lo, NT, preferred_element_type=f32
        )
        found = jnp.dot(cell_table, hot_lo, preferred_element_type=f32)
        place = jnp.sum(jnp.where(hot_hi, found[:64] + found[64:], 0.0), axis=0, keepdims=True)
        list_send[side] = jnp.where(listed, place, -1.0)
    code = (
        jnp.bitwise_and(jnp.right_shift(cells, 8), 3) + jnp.right_shift(cells, 10) * 8
    ).astype(f32) + 4.0 * leaving[:56]
    low = jnp.bitwise_and(cells, 255).astype(f32)
    for row in range(7 * OWN):
        k, j = divmod(row, 7)
        codes[k, :, LO * j : LO * (j + 1)] = code[row : row + 1]
        lows[k, :, LO * j : LO * (j + 1)] = low[row : row + 1]

    load_feats.wait()
    acc[...] = jnp.zeros_like(acc)

    def splat_own(k, carry):
        hot = one_hot(lows[k].astype(bf16), LO)
        onehots[k] = hot
        row = codes[k].astype(bf16)
        values = feats[:, pl.ds(pl.multiple_of(k * S, 128), S)]
        rows = masked_rows(row, values, range(16)) + [one_hot(row, 16)]
        acc[...] += lax.dot_general(
            jnp.concatenate(rows, axis=0), hot, NT, preferred_element_type=f32
        )
        return carry

    lax.fori_loop(0, OWN, splat_own, 0, unroll=4)

    counts = acc[256:272, :]
    count_hi = jnp.floor(counts * (1.0 / 256.0))
    count_lo = (counts - 256.0 * count_hi).astype(bf16)
    count_hi = count_hi.astype(bf16)

    def block(number, row):
        lanes = slice(128 * (row % 2), 128 * (row % 2) + 128)
        return acc[16 * number : 16 * number + 16, lanes].astype(bf16)

    def rows_of(numbers, first_row):
        return [block(4 * plane + first_row // 2, first_row) for plane in numbers]

    for ref, members in ((up_send, UP_MSG), (down_send, DOWN_MSG)):
        for i, number in enumerate(members):
            ref[2 * i] = block(number, 0)
            ref[2 * i + 1] = block(number, 1)
        ref[16] = count_lo[:, :128]
        ref[17] = count_lo[:, 128:]
        ref[18] = count_hi[:, :128]
        ref[19] = count_hi[:, 128:]
    for side in range(2):
        lanes = slice(128 * side, 128 * side + 128)
        for i, plane in enumerate(range(4)):
            side_send[side, i] = block(4 * plane + 3 * side, side)
        side_send[side, 4] = count_lo[:, lanes]
        side_send[side, 5] = count_hi[:, lanes]
        for vertical, planes in ((0, (0, 3)), (1, (1, 2))):
            for i, plane in enumerate(planes):
                corner_send[2 * vertical + side, i] = block(4 * plane + 3 * side, side)
            corner_send[2 * vertical + side, 2] = count_lo[:, lanes]
            corner_send[2 * vertical + side, 3] = count_hi[:, lanes]

    copies = []

    def send(src, dst, place, da, db):
        if comm:
            copy = pltpu.make_async_remote_copy(
                src_ref=src, dst_ref=dst, send_sem=send_sem.at[place],
                recv_sem=recv_sem.at[place], device_id=near(da, db), device_id_type=MESH,
            )
            copy.start()
            copies.append(copy)

    if comm:
        pl.semaphore_wait(barrier, len(around) + 30)
    send(list_send.at[0], list_recv.at[1], 0, -1, 0)
    send(list_send.at[1], list_recv.at[0], 1, 1, 0)
    send(up_send, up_recv, 2, 1, 0)
    send(down_send, down_recv, 3, -1, 0)
    for side in range(2):
        db = 2 * side - 1
        send(side_send.at[side], side_recv.at[side], 4 + side, 0, db)
        for vertical in range(2):
            i = 2 * vertical + side
            send(corner_send.at[i], corner_recv.at[i], 6 + i, 2 * vertical - 1, db)

    load_cot.wait()
    acc_cot[...] = jnp.zeros_like(acc_cot)

    def splat_cot(k, carry):
        row = codes[k].astype(bf16)
        values = cot[:, pl.ds(pl.multiple_of(k * S, 128), S)]
        acc_cot[...] += lax.dot_general(
            jnp.concatenate(masked_rows(row, values, STAY), axis=0), onehots[k], NT,
            preferred_element_type=f32,
        )
        return carry

    lax.fori_loop(0, OWN, splat_cot, 0, unroll=4)

    if comm:
        copies[0].wait()
        copies[1].wait()
    for side in range(2):
        present = (a > 0) if side == 0 else (a < n_a - 1)
        place = jnp.where(present, list_recv[side], -1.0).astype(jnp.int32)
        live = place >= 0
        row = jnp.where(live, jnp.right_shift(place, 8) + 8 * side, 16).astype(f32)
        codes[OWN + side] = row
        hot = one_hot(jnp.bitwise_and(place, 255).astype(f32).astype(bf16), LO)
        onehots[OWN + side] = hot
        values = cot[:, (OWN + side) * S : (OWN + side + 1) * S]
        members = STAY[4 * side : 4 * side + 4]
        acc_cot[64 * side : 64 * side + 64, :] += lax.dot_general(
            jnp.concatenate(masked_rows(row.astype(bf16), values, members), axis=0), hot, NT,
            preferred_element_type=f32,
        )

    if comm:
        for copy in copies[2:]:
            copy.wait()
    has_below = a > 0
    has_above = a < n_a - 1
    has_left = b > 0
    has_right = b < n_b - 1

    def unpack(ref, at, flag):
        total = ref[at + 1].astype(f32) * 256.0 + ref[at].astype(f32)
        return jnp.where(flag, total, 0.0)

    for i, (ref, flag) in enumerate(((up_recv, has_below), (down_recv, has_above))):
        for half in range(2):
            total = ref[18 + half].astype(f32) * 256.0 + ref[16 + half].astype(f32)
            counts_in[2 * i + half] = jnp.where(flag, total, 0.0)
    side_flag = (has_right, has_left)
    for side in range(2):
        for i, (ref, at) in enumerate(
            ((side_recv.at[side], 4), (corner_recv.at[side], 2), (corner_recv.at[2 + side], 2))
        ):
            flag = side_flag[side]
            if i == 1:
                flag = jnp.logical_and(flag, has_above)
            if i == 2:
                flag = jnp.logical_and(flag, has_below)
            total = ref[at + 1].astype(f32) * 256.0 + ref[at].astype(f32)
            counts_in[(4 if i == 0 else 4 + 2 * i) + side] = jnp.where(flag, total, 0.0)

    def mean(sums, count):
        return sums / jnp.maximum(count, 1.0)

    sources = (
        (3, up_recv, 4, 2, 0, has_below),
        (0, up_recv, 0, 1, 0, has_below),
        (2, down_recv, 4, 3, 2, has_above),
        (1, down_recv, 0, 0, 2, has_above),
    )
    for plane, (mine, ref, at, theirs, where, flag) in enumerate(sources):
        for row in range(8):
            half = row % 2
            lanes = slice(128 * half, 128 * half + 128)
            number = 4 * mine + row // 2
            other = 4 * theirs + row // 2
            got = ref[2 * (at + row // 2) + half].astype(f32)
            sums = acc[16 * number : 16 * number + 16, lanes] + jnp.where(flag, got, 0.0)
            count = acc[256 + number : 257 + number, lanes]
            count = count + counts_in[where + half, other : other + 1, :]
            divisor = jnp.broadcast_to(jnp.maximum(count, 1.0), (CH, 128))
            grid[plane, 1 + row] = (sums / divisor).astype(bf16)
            if plane in (1, 2):
                divisors[8 * (plane - 1) + row] = divisor
    for side in range(2):
        flag = side_flag[side]
        y_hi = 3 * side
        halo = (
            (3, 1, 1, 2, has_below),
            (0, 1, 0, 1, has_below),
            (2, 0, 1, 3, has_above),
            (1, 0, 0, 0, has_above),
        )
        for plane, (direct, vertical, at, theirs, vertical_flag) in enumerate(halo):
            corner = 2 * vertical + side
            both = jnp.logical_and(flag, vertical_flag)
            sums = jnp.where(flag, side_recv[side, direct].astype(f32), 0.0)
            sums = sums + jnp.where(both, corner_recv[corner, at].astype(f32), 0.0)
            mine = 4 * direct + y_hi
            other = 4 * theirs + y_hi
            kind = 6 if vertical == 0 else 8
            count = counts_in[4 + side, mine : mine + 1, :]
            count = count + counts_in[kind + side, other : other + 1, :]
            grid[plane, 9 * (1 - side)] = mean(sums, count).astype(bf16)

    lane = lax.broadcasted_iota(jnp.int32, (CH, X), 1)
    first_x = lane == 0
    last_x = lane == X - 1
    for z in range(CZ):
        stacked = jnp.concatenate(
            [
                jnp.concatenate([grid[z + u, v + y] for y in range(CY)], axis=1)
                for u in range(3)
                for v in range(3)
            ],
            axis=0,
        )
        patches[z] = stacked
        pre[...] = jnp.dot(wmat[...], stacked, preferred_element_type=f32)
        for y in range(CY):
            lanes = slice(128 * y, 128 * y + 128)
            low_x = pltpu.roll(pre[0:16, lanes], 1, 1)
            high_x = pltpu.roll(pre[32:48, lanes], X - 1, 1)
            value = (
                pre[16:32, lanes]
                + jnp.where(first_x, 0.0, low_x)
                + jnp.where(last_x, 0.0, high_x)
            )
            sigma = sigmoid(value)
            group = 4 * z + y // 2
            half = slice(128 * (y % 2), 128 * (y % 2) + 128)
            table[16 * group : 16 * group + 16, half] = (value * sigma).astype(bf16)
            cot_sum = acc_cot[16 * group : 16 * group + 16, half]
            gpad[z + 1, y + 1] = (cot_sum * sigma * (1.0 + value * (1.0 - sigma))).astype(bf16)

    copies_2 = []

    def send_2nd(src, dst, place, da, db):
        if comm:
            copy = pltpu.make_async_remote_copy(
                src_ref=src, dst_ref=dst, send_sem=send_2.at[place],
                recv_sem=recv_2.at[place], device_id=near(da, db), device_id_type=MESH,
            )
            copy.start()
            copies_2.append(copy)

    send_2nd(gpad.at[1, pl.ds(1, 8)], gpad.at[3, pl.ds(1, 8)], 0, -1, 0)
    send_2nd(gpad.at[2, pl.ds(1, 8)], gpad.at[0, pl.ds(1, 8)], 1, 1, 0)
    send_2nd(gpad.at[pl.ds(1, 2), 1], gpad.at[pl.ds(1, 2), 9], 2, 0, -1)
    send_2nd(gpad.at[pl.ds(1, 2), 8], gpad.at[pl.ds(1, 2), 0], 3, 0, 1)
    send_2nd(gpad.at[1, 1], gpad.at[3, 9], 4, -1, -1)
    send_2nd(gpad.at[1, 8], gpad.at[3, 0], 5, -1, 1)
    send_2nd(gpad.at[2, 1], gpad.at[0, 9], 6, 1, -1)
    send_2nd(gpad.at[2, 8], gpad.at[0, 0], 7, 1, 1)

    def move(plane, row):
        value = gpad[plane, row]
        wide = value.astype(f32)
        gp3[plane, row, 0:16] = jnp.where(last_x, 0.0, pltpu.roll(wide, X - 1, 1)).astype(bf16)
        gp3[plane, row, 16:32] = value
        gp3[plane, row, 32:48] = jnp.where(first_x, 0.0, pltpu.roll(wide, 1, 1)).astype(bf16)

    wide_grad = jnp.zeros((48, 144), f32)
    for z in range(CZ):
        for y in range(CY):
            move(z + 1, y + 1)
        moved = jnp.concatenate([gp3[z + 1, y + 1] for y in range(CY)], axis=1)
        wide_grad += lax.dot_general(moved, patches[z], NT, preferred_element_type=f32)
    compact = jnp.zeros((CH, 128), f32)
    for col_k in range(3):
        kept = jnp.where(same_group, wide_grad[16 * col_k : 16 * col_k + 16], 0.0)
        compact += jnp.dot(
            kept, spread[col_k].astype(f32), preferred_element_type=f32,
            precision=lax.Precision.HIGHEST,
        )
    part[...] = compact

    def spread_1(d):
        return pltpu.make_async_remote_copy(
            src_ref=part, dst_ref=gather_1.at[d - 1], send_sem=red_send.at[0, d - 1],
            recv_sem=red_recv.at[0, d - 1], device_id=peer_1(d), device_id_type=MESH,
        )

    def spread_2(d):
        return pltpu.make_async_remote_copy(
            src_ref=total_1, dst_ref=gather_2.at[d - 1], send_sem=red_send.at[1, d - 1],
            recv_sem=red_recv.at[1, d - 1], device_id=peer_2(d), device_id_type=MESH,
        )

    def start_all(make):
        def body(d, carry):
            make(d).start()
            return carry

        lax.fori_loop(1, 16, body, 0)

    def wait_all(make):
        def body(d, carry):
            make(d).wait()
            return carry

        lax.fori_loop(1, 16, body, 0)

    if comm:
        start_all(spread_1)

    def read_back(into):
        def body(k, carry):
            found = jnp.dot(table[...], onehots[k], preferred_element_type=f32)
            row = codes[k]
            value = jnp.zeros((CH, S), f32)
            for i, number in enumerate(STAY):
                value = jnp.where(row == float(number), found[16 * i : 16 * i + 16], value)
            into[:, pl.ds(pl.multiple_of(k * S, 128), S)] = value.astype(bf16)
            return carry

        lax.fori_loop(0, ALL, body, 0, unroll=5)

    read_back(out_buf)
    store_out = pltpu.make_async_copy(out_buf, out_hbm, store_sem.at[0])
    store_out.start()

    if comm:
        wait_all(spread_1)
    total = part[...]
    for d in range(15):
        total = total + gather_1[d]
    total_1[...] = total
    if comm:
        start_all(spread_2)

    for copy in copies_2:
        copy.wait()
    blank = jnp.zeros((CH, X), bf16)

    def clear(flag, places):
        @pl.when(flag)
        def _():
            for plane, row in places:
                gpad[plane, row] = blank

    clear(a == 0, [(0, row) for row in range(10)])
    clear(a == n_a - 1, [(3, row) for row in range(10)])
    clear(b == 0, [(plane, 0) for plane in range(4)])
    clear(b == n_b - 1, [(plane, 9) for plane in range(4)])
    for plane in range(4):
        for row in range(10):
            if plane in (0, 3) or row in (0, 9):
                move(plane, row)
    result = [None] * 16
    for plane in range(4):
        moved = jnp.concatenate([gp3[plane, row] for row in range(10)], axis=1)
        taps = lax.dot_general(
            wmat[...], moved, (((0,), (0,)), ((), ())), preferred_element_type=f32
        )
        for u in range(3):
            z = plane - 2 + u
            if z not in (0, 1):
                continue
            for v in range(3):
                rows = slice(16 * (3 * u + v), 16 * (3 * u + v) + 16)
                for y in range(CY):
                    source = y + 2 - v
                    term = taps[rows, 128 * source : 128 * source + 128]
                    i = 8 * z + y
                    result[i] = term if result[i] is None else result[i] + term
    for i in range(16):
        group = i // 2
        half = slice(128 * (i % 2), 128 * (i % 2) + 128)
        table[16 * group : 16 * group + 16, half] = (result[i] / divisors[i]).astype(bf16)
    read_back(grad_buf)
    store_grad = pltpu.make_async_copy(grad_buf, grad_hbm, store_sem.at[1])
    store_grad.start()

    if comm:
        wait_all(spread_2)
    total = total_1[...]
    for d in range(15):
        total = total + gather_2[d]
    total = (total * (1.0 / math.sqrt(CZ * CY * X * n_a * n_b))).T
    for i in range(27):
        wgrad_ref[i] = total[GRP * i : GRP * i + GRP]
    store_out.wait()
    store_grad.wait()


def fused(feats, cot, cells, slots, count, weight, comm=True):
    hbm = pl.BlockSpec(memory_space=pl.ANY)
    vmem = pl.BlockSpec(memory_space=pltpu.VMEM)
    smem = pl.BlockSpec(memory_space=pltpu.SMEM)
    slots_all = ALL * S
    dma = pltpu.SemaphoreType.DMA
    return pl.pallas_call(
        functools.partial(kernel, comm=comm),
        out_shape=[
            jax.ShapeDtypeStruct((CH, slots_all), bf16),
            jax.ShapeDtypeStruct((CH, slots_all), bf16),
            jax.ShapeDtypeStruct((27, GRP, CH), f32),
        ],
        in_specs=[hbm, hbm, vmem, vmem, smem, vmem],
        out_specs=[hbm, hbm, vmem],
        scratch_shapes=[
            pltpu.VMEM((CH, OWN * S), bf16),
            pltpu.VMEM((CH, slots_all), bf16),
            pltpu.VMEM((CH, slots_all), bf16),
            pltpu.VMEM((CH, slots_all), bf16),
            pltpu.VMEM((ALL, LO, S), bf16),
            pltpu.VMEM((ALL, 1, S), f32),
            pltpu.VMEM((OWN, 1, S), f32),
            pltpu.VMEM((272, LO), f32),
            pltpu.VMEM((128, LO), f32),
            pltpu.VMEM((2, 1, S), f32),
            pltpu.VMEM((2, 1, S), f32),
            pltpu.VMEM((20, CH, 128), bf16),
            pltpu.VMEM((20, CH, 128), bf16),
            pltpu.VMEM((20, CH, 128), bf16),
            pltpu.VMEM((20, CH, 128), bf16),
            pltpu.VMEM((2, 6, CH, 128), bf16),
            pltpu.VMEM((2, 6, CH, 128), bf16),
            pltpu.VMEM((4, 4, CH, 128), bf16),
            pltpu.VMEM((4, 4, CH, 128), bf16),
            pltpu.VMEM((4, 10, CH, 128), bf16),
            pltpu.VMEM((4, 10, CH, 128), bf16),
            pltpu.VMEM((CZ, 144, CY * X), bf16),
            pltpu.VMEM((4, 10, 48, 128), bf16),
            pltpu.VMEM((128, LO), bf16),
            pltpu.VMEM((16, CH, 128), f32),
            pltpu.VMEM((48, 144), bf16),
            pltpu.VMEM((10, CH, 128), f32),
            pltpu.VMEM((48, CY * X), f32),
            pltpu.VMEM((CH, 128), f32),
            pltpu.VMEM((15, CH, 128), f32),
            pltpu.VMEM((CH, 128), f32),
            pltpu.VMEM((15, CH, 128), f32),
            dma((2,)),
            dma((2,)),
            dma((10,)),
            dma((10,)),
            dma((8,)),
            dma((8,)),
            dma((2, 15)),
            dma((2, 15)),
        ],
        compiler_params=pltpu.CompilerParams(
            vmem_limit_bytes=60 << 20,
            **(dict(collective_id=0, has_side_effects=True) if comm else {}),
        ),
    )(feats, cot, cells, slots, count, weight)


def local(point_feats, cell_index, send_slots, send_count, conv_weight, point_cot):
    cells = cell_index.reshape(-1, 128)
    weight = conv_weight.transpose(2, 3, 4, 1, 0).reshape(27, GRP, CH)
    out, grad, wgrad = fused(point_feats, point_cot, cells, send_slots, send_count, weight)
    return out, grad, wgrad.reshape(3, 3, 3, GRP, CH).transpose(4, 3, 0, 1, 2)


def solution(mesh):
    placed = (
        P(None, ("gz", "gy")),
        P(("gz", "gy")),
        P(("gz", "gy"), None, None),
        P(("gz", "gy"), None),
        P(),
        P(None, ("gz", "gy")),
    )
    return jax.shard_map(
        local,
        mesh=mesh,
        in_specs=placed,
        out_specs=(P(None, ("gz", "gy")), P(None, ("gz", "gy")), P()),
        check_vma=False,
    )
```

```python
import functools
import math

import jax
import jax.numpy as jnp
from jax import lax
from jax.experimental import pallas as pl
from jax.experimental.pallas import tpu as pltpu
from jax.sharding import PartitionSpec as P

CH = 16
GRP = 4
X = 128
CY = 8
CZ = 2
S = 1792
OWN = 8
ALL = OWN + 2
LO = 256
MESH = pl.DeviceIdType.MESH
f32 = jnp.float32
bf16 = jnp.bfloat16
NT = (((1,), (1,)), ((), ()))

UP_MSG = tuple(range(4, 12))
DOWN_MSG = (0, 1, 2, 3, 12, 13, 14, 15)
STAY = (0, 1, 2, 3, 8, 9, 10, 11)


def one_hot(row, count):
    ids = lax.broadcasted_iota(jnp.int32, (count, row.shape[1]), 0).astype(f32).astype(bf16)
    return jnp.where(ids == row, jnp.ones((), bf16), jnp.zeros((), bf16))


def masked_rows(row, values, codes):
    zero = jnp.zeros((), bf16)
    return [jnp.where(row == jnp.full((), code, bf16), values, zero) for code in codes]


def sigmoid(v):
    return 1.0 / (1.0 + jnp.exp(-v))


def select(found, row):
    value = jnp.zeros((CH, S), f32)
    for i, number in enumerate(STAY):
        value = jnp.where(row == float(number), found[16 * i : 16 * i + 16], value)
    return value.astype(bf16)


def kernel(
    feats_hbm, cot_hbm, cells_hbm, slots_hbm, count_hbm, weight_hbm,
    onehots, codes, table, out_buf, wgrad_ref,
    feats, cot, cells_ref, slots_ref, count_ref, weight_ref, lows, acc, acc_cot,
    list_send, list_recv,
    up_send, down_send, up_recv, down_recv,
    side_send, side_recv, corner_send, corner_recv,
    grid, gpad, patches, gp3, act, divisors, wmat, counts_in, pre,
    part, gather_1, row_sum, gather_2, full,
    load_sem, send_sem, recv_sem, send_2, recv_2, red_send, red_recv,
    *, comm,
):
    a = lax.axis_index("gz")
    b = lax.axis_index("gy")
    n_a = lax.axis_size("gz")
    n_b = lax.axis_size("gy")
    z_p = a // 8
    y_p = lax.rem(a // 2, 4)
    x_p = lax.rem(a, 2)

    loads = [
        pltpu.make_async_copy(src, dst, load_sem.at[i])
        for i, (src, dst) in enumerate(
            (
                (cells_hbm, cells_ref), (slots_hbm, slots_ref), (count_hbm, count_ref),
                (feats_hbm, feats), (weight_hbm, weight_ref), (cot_hbm, cot),
            )
        )
    ]
    for load in loads:
        load.start()
    load_cells, load_slots, load_count, load_feats, load_weight, load_cot = loads

    a_near = {-1: lax.rem(a + n_a - 1, n_a), 0: a, 1: lax.rem(a + 1, n_a)}
    b_all = [b] + [lax.rem(b + k, n_b) for k in range(1, 4)]
    z_all = [z_p] + [lax.rem(z_p + k, 8) for k in range(1, 8)]
    y_all = [y_p] + [lax.rem(y_p + k, 4) for k in range(1, 4)]
    peers_1 = [(z_p * 8 + x_p + y_all[d // 4] * 2, b_all[d % 4]) for d in range(1, 16)]
    rows_1 = [y_all[d // 4] * 4 + b_all[d % 4] for d in range(1, 16)]
    peers_2 = [
        (z_all[d // 2] * 8 + y_p * 2 + (1 - x_p if d % 2 else x_p), b) for d in range(1, 16)
    ]
    my_row = y_p * 4 + b

    def near(da, db):
        return (a_near[da], b_all[db % 4])

    around = [(da, db) for da in (-1, 0, 1) for db in (-1, 0, 1) if (da, db) != (0, 0)]
    if comm:
        barrier = pltpu.get_barrier_semaphore()
        for place in [near(da, db) for da, db in around] + peers_1 + peers_2:
            pl.semaphore_signal(barrier, inc=1, device_id=place, device_id_type=MESH)

    tap_row = lax.broadcasted_iota(jnp.int32, (144, 128), 0)
    tap_col = lax.broadcasted_iota(jnp.int32, (144, 128), 1)
    tap_base = jnp.bitwise_and(tap_row, 3) + jnp.right_shift(tap_row, 4) * (3 * GRP)
    spread = [tap_base + GRP * col_k == tap_col for col_k in range(3)]
    out_ch = lax.broadcasted_iota(jnp.int32, (CH, 144), 0)
    in_ch = jnp.bitwise_and(lax.broadcasted_iota(jnp.int32, (CH, 144), 1), 15)
    same_group = jnp.right_shift(out_ch, 2) == jnp.right_shift(in_ch, 2)
    load_cells.wait()
    load_slots.wait()
    load_count.wait()
    cells = jnp.concatenate(
        [cells_ref[pl.ds(0, 56, stride=2), :], cells_ref[pl.ds(1, 56, stride=2), :]], axis=1
    )
    cell_y = jnp.right_shift(jnp.bitwise_and(cells, 1023), 7) * 128
    cell_x = jnp.bitwise_and(cells, 127)
    pad = jnp.zeros((8, LO), f32)
    cell_table = jnp.concatenate(
        [cell_y.astype(f32), pad, cell_x.astype(f32), pad], axis=0
    ).astype(bf16)
    lane = lax.broadcasted_iota(jnp.int32, (1, S), 1)
    leaving = jnp.zeros((64, LO), f32)
    for side in range(2):
        listed = lane < count_ref[:, side : side + 1]
        slot = slots_ref[0, side : side + 1, :]
        slot_hi = jnp.where(listed, jnp.right_shift(slot, 8), -1)
        hot_lo = one_hot(jnp.bitwise_and(slot, 255).astype(f32).astype(bf16), LO)
        hot_hi = lax.broadcasted_iota(jnp.int32, (64, S), 0) == slot_hi
        leaving += lax.dot_general(
            hot_hi.astype(f32).astype(bf16), hot_lo, NT, preferred_element_type=f32
        )
        found = jnp.dot(cell_table, hot_lo, preferred_element_type=f32)
        place = jnp.sum(jnp.where(hot_hi, found[:64] + found[64:], 0.0), axis=0, keepdims=True)
        list_send[side] = jnp.where(listed, place, -1.0)
    code = (
        jnp.bitwise_and(jnp.right_shift(cells, 8), 3) + jnp.right_shift(cells, 10) * 8
    ).astype(f32) + 4.0 * leaving[:56]
    low = jnp.bitwise_and(cells, 255).astype(f32)
    for row in range(7 * OWN):
        k, j = divmod(row, 7)
        codes[k, :, LO * j : LO * (j + 1)] = code[row : row + 1]
        lows[k, :, LO * j : LO * (j + 1)] = low[row : row + 1]

    load_feats.wait()
    acc[...] = jnp.zeros_like(acc)

    def splat_own(k, carry):
        hot = one_hot(lows[k].astype(bf16), LO)
        onehots[k] = hot
        row = codes[k].astype(bf16)
        values = feats[:, pl.ds(pl.multiple_of(k * S, 128), S)]
        rows = masked_rows(row, values, range(16)) + [one_hot(row, 16)]
        acc[...] += lax.dot_general(
            jnp.concatenate(rows, axis=0), hot, NT, preferred_element_type=f32
        )
        return carry

    lax.fori_loop(0, OWN, splat_own, 0, unroll=4)

    counts = acc[256:272, :]
    count_hi = jnp.floor(counts * (1.0 / 256.0))
    count_lo = (counts - 256.0 * count_hi).astype(bf16)
    count_hi = count_hi.astype(bf16)

    def block(number, row):
        lanes = slice(128 * (row % 2), 128 * (row % 2) + 128)
        return acc[16 * number : 16 * number + 16, lanes].astype(bf16)

    def rows_of(numbers, first_row):
        return [block(4 * plane + first_row // 2, first_row) for plane in numbers]

    for ref, members in ((up_send, UP_MSG), (down_send, DOWN_MSG)):
        for i, number in enumerate(members):
            ref[2 * i] = block(number, 0)
            ref[2 * i + 1] = block(number, 1)
        ref[16] = count_lo[:, :128]
        ref[17] = count_lo[:, 128:]
        ref[18] = count_hi[:, :128]
        ref[19] = count_hi[:, 128:]
    for side in range(2):
        lanes = slice(128 * side, 128 * side + 128)
        for i, plane in enumerate(range(4)):
            side_send[side, i] = block(4 * plane + 3 * side, side)
        side_send[side, 4] = count_lo[:, lanes]
        side_send[side, 5] = count_hi[:, lanes]
        for vertical, planes in ((0, (0, 3)), (1, (1, 2))):
            for i, plane in enumerate(planes):
                corner_send[2 * vertical + side, i] = block(4 * plane + 3 * side, side)
            corner_send[2 * vertical + side, 2] = count_lo[:, lanes]
            corner_send[2 * vertical + side, 3] = count_hi[:, lanes]

    copies = []

    def send(src, dst, place, da, db):
        if comm:
            copy = pltpu.make_async_remote_copy(
                src_ref=src, dst_ref=dst, send_sem=send_sem.at[place],
                recv_sem=recv_sem.at[place], device_id=near(da, db), device_id_type=MESH,
            )
            copy.start()
            copies.append(copy)

    if comm:
        pl.semaphore_wait(barrier, len(around) + 30)
    send(list_send.at[0], list_recv.at[1], 0, -1, 0)
    send(list_send.at[1], list_recv.at[0], 1, 1, 0)
    send(up_send, up_recv, 2, 1, 0)
    send(down_send, down_recv, 3, -1, 0)
    for side in range(2):
        db = 2 * side - 1
        send(side_send.at[side], side_recv.at[side], 4 + side, 0, db)
        for vertical in range(2):
            i = 2 * vertical + side
            send(corner_send.at[i], corner_recv.at[i], 6 + i, 2 * vertical - 1, db)

    load_weight.wait()
    weight = jnp.concatenate(
        [weight_ref[i].astype(f32) for i in range(27)] + [jnp.zeros((20, CH), f32)], axis=0
    ).T.astype(bf16)
    for col_k in range(3):
        picked = lax.dot_general(
            weight, spread[col_k].astype(bf16), NT, preferred_element_type=f32
        )
        wmat[16 * col_k : 16 * col_k + 16, :] = jnp.where(same_group, picked, 0.0).astype(bf16)

    load_cot.wait()
    acc_cot[...] = jnp.zeros_like(acc_cot)

    def splat_cot(k, carry):
        row = codes[k].astype(bf16)
        values = cot[:, pl.ds(pl.multiple_of(k * S, 128), S)]
        acc_cot[...] += lax.dot_general(
            jnp.concatenate(masked_rows(row, values, STAY), axis=0), onehots[k], NT,
            preferred_element_type=f32,
        )
        return carry

    lax.fori_loop(0, OWN, splat_cot, 0, unroll=4)

    if comm:
        copies[0].wait()
        copies[1].wait()
    for side in range(2):
        present = (a > 0) if side == 0 else (a < n_a - 1)
        place = jnp.where(present, list_recv[side], -1.0).astype(jnp.int32)
        live = place >= 0
        row = jnp.where(live, jnp.right_shift(place, 8) + 8 * side, 16).astype(f32)
        codes[OWN + side] = row
        hot = one_hot(jnp.bitwise_and(place, 255).astype(f32).astype(bf16), LO)
        onehots[OWN + side] = hot
        values = cot[:, (OWN + side) * S : (OWN + side + 1) * S]
        members = STAY[4 * side : 4 * side + 4]
        acc_cot[64 * side : 64 * side + 64, :] += lax.dot_general(
            jnp.concatenate(masked_rows(row.astype(bf16), values, members), axis=0), hot, NT,
            preferred_element_type=f32,
        )

    if comm:
        for copy in copies[2:]:
            copy.wait()
    has_below = a > 0
    has_above = a < n_a - 1
    has_left = b > 0
    has_right = b < n_b - 1

    def unpack(ref, at, flag):
        total = ref[at + 1].astype(f32) * 256.0 + ref[at].astype(f32)
        return jnp.where(flag, total, 0.0)

    for i, (ref, flag) in enumerate(((up_recv, has_below), (down_recv, has_above))):
        for half in range(2):
            total = ref[18 + half].astype(f32) * 256.0 + ref[16 + half].astype(f32)
            counts_in[2 * i + half] = jnp.where(flag, total, 0.0)
    side_flag = (has_right, has_left)
    for side in range(2):
        for i, (ref, at) in enumerate(
            ((side_recv.at[side], 4), (corner_recv.at[side], 2), (corner_recv.at[2 + side], 2))
        ):
            flag = side_flag[side]
            if i == 1:
                flag = jnp.logical_and(flag, has_above)
            if i == 2:
                flag = jnp.logical_and(flag, has_below)
            total = ref[at + 1].astype(f32) * 256.0 + ref[at].astype(f32)
            counts_in[(4 if i == 0 else 4 + 2 * i) + side] = jnp.where(flag, total, 0.0)

    def mean(sums, count):
        return sums / jnp.maximum(count, 1.0)

    sources = (
        (3, up_recv, 4, 2, 0, has_below),
        (0, up_recv, 0, 1, 0, has_below),
        (2, down_recv, 4, 3, 2, has_above),
        (1, down_recv, 0, 0, 2, has_above),
    )
    for plane, (mine, ref, at, theirs, where, flag) in enumerate(sources):
        for row in range(8):
            half = row % 2
            lanes = slice(128 * half, 128 * half + 128)
            number = 4 * mine + row // 2
            other = 4 * theirs + row // 2
            got = ref[2 * (at + row // 2) + half].astype(f32)
            sums = acc[16 * number : 16 * number + 16, lanes] + jnp.where(flag, got, 0.0)
            count = acc[256 + number : 257 + number, lanes]
            count = count + counts_in[where + half, other : other + 1, :]
            divisor = jnp.broadcast_to(jnp.maximum(count, 1.0), (CH, 128))
            grid[plane, 1 + row] = (sums / divisor).astype(bf16)
            if plane in (1, 2):
                divisors[8 * (plane - 1) + row] = divisor
    for side in range(2):
        flag = side_flag[side]
        y_hi = 3 * side
        halo = (
            (3, 1, 1, 2, has_below),
            (0, 1, 0, 1, has_below),
            (2, 0, 1, 3, has_above),
            (1, 0, 0, 0, has_above),
        )
        for plane, (direct, vertical, at, theirs, vertical_flag) in enumerate(halo):
            corner = 2 * vertical + side
            both = jnp.logical_and(flag, vertical_flag)
            sums = jnp.where(flag, side_recv[side, direct].astype(f32), 0.0)
            sums = sums + jnp.where(both, corner_recv[corner, at].astype(f32), 0.0)
            mine = 4 * direct + y_hi
            other = 4 * theirs + y_hi
            kind = 6 if vertical == 0 else 8
            count = counts_in[4 + side, mine : mine + 1, :]
            count = count + counts_in[kind + side, other : other + 1, :]
            grid[plane, 9 * (1 - side)] = mean(sums, count).astype(bf16)

    lane = lax.broadcasted_iota(jnp.int32, (CH, X), 1)
    first_x = lane == 0
    last_x = lane == X - 1
    for z in range(CZ):
        stacked = jnp.concatenate(
            [
                jnp.concatenate([grid[z + u, v + y] for y in range(CY)], axis=1)
                for u in range(3)
                for v in range(3)
            ],
            axis=0,
        )
        patches[z] = stacked
        pre[...] = jnp.dot(wmat[...], stacked, preferred_element_type=f32)
        for y in range(CY):
            lanes = slice(128 * y, 128 * y + 128)
            low_x = pltpu.roll(pre[0:16, lanes], 1, 1)
            high_x = pltpu.roll(pre[32:48, lanes], X - 1, 1)
            value = (
                pre[16:32, lanes]
                + jnp.where(first_x, 0.0, low_x)
                + jnp.where(last_x, 0.0, high_x)
            )
            sigma = sigmoid(value)
            group = 4 * z + y // 2
            half = slice(128 * (y % 2), 128 * (y % 2) + 128)
            act[16 * group : 16 * group + 16, half] = (value * sigma).astype(bf16)
            cot_sum = acc_cot[16 * group : 16 * group + 16, half]
            gpad[z + 1, y + 1] = (cot_sum * sigma * (1.0 + value * (1.0 - sigma))).astype(bf16)

    copies_2 = []

    def send_2nd(src, dst, place, da, db):
        if comm:
            copy = pltpu.make_async_remote_copy(
                src_ref=src, dst_ref=dst, send_sem=send_2.at[place],
                recv_sem=recv_2.at[place], device_id=near(da, db), device_id_type=MESH,
            )
            copy.start()
            copies_2.append(copy)

    send_2nd(gpad.at[1, pl.ds(1, 8)], gpad.at[3, pl.ds(1, 8)], 0, -1, 0)
    send_2nd(gpad.at[2, pl.ds(1, 8)], gpad.at[0, pl.ds(1, 8)], 1, 1, 0)
    send_2nd(gpad.at[pl.ds(1, 2), 1], gpad.at[pl.ds(1, 2), 9], 2, 0, -1)
    send_2nd(gpad.at[pl.ds(1, 2), 8], gpad.at[pl.ds(1, 2), 0], 3, 0, 1)
    send_2nd(gpad.at[1, 1], gpad.at[3, 9], 4, -1, -1)
    send_2nd(gpad.at[1, 8], gpad.at[3, 0], 5, -1, 1)
    send_2nd(gpad.at[2, 1], gpad.at[0, 9], 6, 1, -1)
    send_2nd(gpad.at[2, 8], gpad.at[0, 0], 7, 1, 1)

    def move(plane, row):
        value = gpad[plane, row]
        wide = value.astype(f32)
        gp3[plane, row, 0:16] = jnp.where(last_x, 0.0, pltpu.roll(wide, X - 1, 1)).astype(bf16)
        gp3[plane, row, 16:32] = value
        gp3[plane, row, 32:48] = jnp.where(first_x, 0.0, pltpu.roll(wide, 1, 1)).astype(bf16)

    wide_grad = jnp.zeros((48, 144), f32)
    for z in range(CZ):
        for y in range(CY):
            move(z + 1, y + 1)
        moved = jnp.concatenate([gp3[z + 1, y + 1] for y in range(CY)], axis=1)
        wide_grad += lax.dot_general(moved, patches[z], NT, preferred_element_type=f32)
    compact = jnp.zeros((CH, 128), f32)
    for col_k in range(3):
        kept = jnp.where(same_group, wide_grad[16 * col_k : 16 * col_k + 16], 0.0)
        first = kept.astype(bf16)
        rest = kept - first.astype(f32)
        second = rest.astype(bf16)
        third = (rest - second.astype(f32)).astype(bf16)
        picked = jnp.dot(
            jnp.concatenate([first, second, third], axis=0), spread[col_k].astype(bf16),
            preferred_element_type=f32,
        )
        compact += picked[0:16] + picked[16:32] + picked[32:48]
    for i in range(CH):
        part[i] = compact[i : i + 1]

    def reduce_send(step, peers, sources, targets):
        if comm:
            for place, src, dst in zip(peers, sources, targets):
                pltpu.make_async_remote_copy(
                    src_ref=src, dst_ref=dst, send_sem=red_send.at[step],
                    recv_sem=red_recv.at[step], device_id=place, device_id_type=MESH,
                ).start()

    def reduce_wait(step, buffer):
        if comm:
            pltpu.make_async_copy(buffer, buffer, red_send.at[step]).wait()
            pltpu.make_async_copy(buffer, buffer, red_recv.at[step]).wait()

    reduce_send(0, peers_1, [part.at[r] for r in rows_1], [gather_1.at[d] for d in range(15)])

    def read_back(group):
        def body(k, carry):
            found = jnp.dot(act[...], onehots[k], preferred_element_type=f32)
            out_buf[:, pl.ds(pl.multiple_of(k * S, 128), S)] = select(found, codes[k])
            return carry

        lax.fori_loop(5 * group, 5 * group + 5, body, 0, unroll=5)

    read_back(0)
    reduce_wait(0, gather_1)
    row = part[my_row]
    for d in range(15):
        row = row + gather_1[d]
    row_sum[...] = row
    reduce_send(1, peers_2, [row_sum] * 15, [gather_2.at[d] for d in range(15)])
    read_back(1)

    for copy in copies_2:
        copy.wait()
    reduce_wait(1, gather_2)
    row = row_sum[...]
    for d in range(15):
        row = row + gather_2[d]
    full[my_row] = row
    reduce_send(2, peers_1, [full.at[my_row]] * 15, [full.at[my_row]] * 15)
    blank = jnp.zeros((CH, X), bf16)

    def clear(flag, places):
        @pl.when(flag)
        def _():
            for plane, row in places:
                gpad[plane, row] = blank

    clear(a == 0, [(0, row) for row in range(10)])
    clear(a == n_a - 1, [(3, row) for row in range(10)])
    clear(b == 0, [(plane, 0) for plane in range(4)])
    clear(b == n_b - 1, [(plane, 9) for plane in range(4)])
    for plane in range(4):
        for row in range(10):
            if plane in (0, 3) or row in (0, 9):
                move(plane, row)
    result = [None] * 16
    for plane in range(4):
        moved = jnp.concatenate([gp3[plane, row] for row in range(10)], axis=1)
        taps = lax.dot_general(
            wmat[...], moved, (((0,), (0,)), ((), ())), preferred_element_type=f32
        )
        for u in range(3):
            z = plane - 2 + u
            if z not in (0, 1):
                continue
            for v in range(3):
                rows = slice(16 * (3 * u + v), 16 * (3 * u + v) + 16)
                for y in range(CY):
                    source = y + 2 - v
                    term = taps[rows, 128 * source : 128 * source + 128]
                    i = 8 * z + y
                    result[i] = term if result[i] is None else result[i] + term
    for i in range(16):
        group = i // 2
        half = slice(128 * (i % 2), 128 * (i % 2) + 128)
        table[16 * group : 16 * group + 16, half] = (result[i] / divisors[i]).astype(bf16)
    reduce_wait(2, gather_1)
    total = jnp.concatenate([full[i] for i in range(CH)], axis=0)
    total = (total * (1.0 / math.sqrt(CZ * CY * X * n_a * n_b))).T
    for i in range(27):
        wgrad_ref[i] = total[GRP * i : GRP * i + GRP]


def last_kernel(
    onehots, codes, table, out_buf, wgrad_ref, out_hbm, grad_hbm, wgrad_hbm, grad_buf, sem
):
    store_out = pltpu.make_async_copy(out_buf, out_hbm, sem.at[0])
    store_weight = pltpu.make_async_copy(wgrad_ref, wgrad_hbm, sem.at[1])
    store_out.start()
    store_weight.start()

    def store(group):
        lanes = pl.ds(pl.multiple_of(group * (5 * S), 128), 5 * S)
        return pltpu.make_async_copy(
            grad_buf.at[:, lanes], grad_hbm.at[:, lanes], sem.at[2 + group]
        )

    def body(group, carry):
        for j in range(5):
            k = 5 * group + j
            found = jnp.dot(table[...], onehots[k], preferred_element_type=f32)
            grad_buf[:, pl.ds(pl.multiple_of(k * S, 128), S)] = select(found, codes[k])
        store(group).start()
        return carry

    lax.fori_loop(0, 2, body, 0)
    store_out.wait()
    store_weight.wait()
    store(0).wait()
    store(1).wait()


def fused(feats, cot, cells, slots, count, weight, comm=True):
    hbm = pl.BlockSpec(memory_space=pltpu.HBM)
    vmem = pl.BlockSpec(memory_space=pltpu.VMEM)
    slots_all = ALL * S
    dma = pltpu.SemaphoreType.DMA
    shape = jax.ShapeDtypeStruct
    feats, cot, cells, slots, count, weight = (
        pltpu.with_memory_space_constraint(v, pltpu.HBM)
        for v in (feats, cot, cells, slots, count, weight)
    )
    parts = pl.pallas_call(
        functools.partial(kernel, comm=comm),
        out_shape=[
            shape((ALL, LO, S), bf16),
            shape((ALL, 1, S), f32),
            shape((128, LO), bf16),
            shape((CH, slots_all), bf16),
            shape((27, GRP, CH), f32),
        ],
        in_specs=[hbm] * 6,
        out_specs=[vmem] * 5,
        scratch_shapes=[
            pltpu.VMEM((CH, OWN * S), bf16),
            pltpu.VMEM((CH, slots_all), bf16),
            pltpu.VMEM((112, 128), jnp.int32),
            pltpu.VMEM((1, 2, S), jnp.int32),
            pltpu.VMEM((1, 2), jnp.int32),
            pltpu.VMEM((27, GRP, CH), bf16),
            pltpu.VMEM((OWN, 1, S), f32),
            pltpu.VMEM((272, LO), f32),
            pltpu.VMEM((128, LO), f32),
            pltpu.VMEM((2, 1, S), f32),
            pltpu.VMEM((2, 1, S), f32),
            pltpu.VMEM((20, CH, 128), bf16),
            pltpu.VMEM((20, CH, 128), bf16),
            pltpu.VMEM((20, CH, 128), bf16),
            pltpu.VMEM((20, CH, 128), bf16),
            pltpu.VMEM((2, 6, CH, 128), bf16),
            pltpu.VMEM((2, 6, CH, 128), bf16),
            pltpu.VMEM((4, 4, CH, 128), bf16),
            pltpu.VMEM((4, 4, CH, 128), bf16),
            pltpu.VMEM((4, 10, CH, 128), bf16),
            pltpu.VMEM((4, 10, CH, 128), bf16),
            pltpu.VMEM((CZ, 144, CY * X), bf16),
            pltpu.VMEM((4, 10, 48, 128), bf16),
            pltpu.VMEM((128, LO), bf16),
            pltpu.VMEM((16, CH, 128), f32),
            pltpu.VMEM((48, 144), bf16),
            pltpu.VMEM((10, CH, 128), f32),
            pltpu.VMEM((48, CY * X), f32),
            pltpu.VMEM((CH, 1, 128), f32),
            pltpu.VMEM((15, 1, 128), f32),
            pltpu.VMEM((1, 128), f32),
            pltpu.VMEM((15, 1, 128), f32),
            pltpu.VMEM((CH, 1, 128), f32),
            dma((6,)),
            dma((10,)),
            dma((10,)),
            dma((8,)),
            dma((8,)),
            dma((3,)),
            dma((3,)),
        ],
        compiler_params=pltpu.CompilerParams(
            vmem_limit_bytes=30 << 20,
            **(dict(collective_id=0, has_side_effects=True) if comm else {}),
        ),
    )(feats, cot, cells, slots, count, weight)
    return pl.pallas_call(
        last_kernel,
        out_shape=[
            shape((CH, slots_all), bf16),
            shape((CH, slots_all), bf16),
            shape((27, GRP, CH), f32),
        ],
        in_specs=[vmem] * 5,
        out_specs=[hbm] * 3,
        scratch_shapes=[pltpu.VMEM((CH, slots_all), bf16), dma((4,))],
        compiler_params=pltpu.CompilerParams(vmem_limit_bytes=24 << 20),
    )(*parts)


def local(point_feats, cell_index, send_slots, send_count, conv_weight, point_cot):
    cells = cell_index.reshape(-1, 128)
    weight = conv_weight.transpose(2, 3, 4, 1, 0).reshape(27, GRP, CH)
    out, grad, wgrad = fused(point_feats, point_cot, cells, send_slots, send_count, weight)
    return out, grad, wgrad.reshape(3, 3, 3, GRP, CH).transpose(4, 3, 0, 1, 2)


def solution(mesh):
    placed = (
        P(None, ("gz", "gy")),
        P(("gz", "gy")),
        P(("gz", "gy"), None, None),
        P(("gz", "gy"), None),
        P(),
        P(None, ("gz", "gy")),
    )
    return jax.shard_map(
        local,
        mesh=mesh,
        in_specs=placed,
        out_specs=(P(None, ("gz", "gy")), P(None, ("gz", "gy")), P()),
        check_vma=False,
    )
```

```python
import functools
import math

import jax
import jax.numpy as jnp
from jax import lax
from jax.experimental import pallas as pl
from jax.experimental.pallas import tpu as pltpu
from jax.sharding import PartitionSpec as P

CH = 16
GRP = 4
X = 128
CY = 8
CZ = 2
S = 1792
OWN = 8
ALL = OWN + 2
LO = 256
MESH = pl.DeviceIdType.MESH
f32 = jnp.float32
bf16 = jnp.bfloat16
NT = (((1,), (1,)), ((), ()))

UP_MSG = tuple(range(4, 12))
DOWN_MSG = (0, 1, 2, 3, 12, 13, 14, 15)
STAY = (0, 1, 2, 3, 8, 9, 10, 11)


def one_hot(row, count):
    ids = lax.broadcasted_iota(jnp.int32, (count, row.shape[1]), 0).astype(f32).astype(bf16)
    return jnp.where(ids == row, jnp.ones((), bf16), jnp.zeros((), bf16))


def masked_rows(row, values, codes):
    zero = jnp.zeros((), bf16)
    return [jnp.where(row == jnp.full((), code, bf16), values, zero) for code in codes]


def sigmoid(v):
    return 1.0 / (1.0 + jnp.exp(-v))


def select(found, row):
    value = jnp.zeros((CH, S), f32)
    for i, number in enumerate(STAY):
        value = jnp.where(row == float(number), found[16 * i : 16 * i + 16], value)
    return value.astype(bf16)


def kernel(
    feats_hbm, cot_hbm, cells_hbm, slots_hbm, count_hbm, weight_hbm,
    out_buf, grad_buf, wgrad_ref,
    onehots, codes, table, feats, cot, cells_ref, slots_ref, count_ref, weight_ref, lows, acc, acc_cot,
    list_send, list_recv,
    up_send, down_send, up_recv, down_recv,
    side_send, side_recv, corner_send, corner_recv,
    grid, gpad, patches, gp3, act, divisors, wmat, counts_in, pre,
    part, gather_1, plane_sum, gather_2,
    load_sem, send_sem, recv_sem, send_2, recv_2, red_send, red_recv,
    *, comm,
):
    a = lax.axis_index("gz")
    b = lax.axis_index("gy")
    n_a = lax.axis_size("gz")
    n_b = lax.axis_size("gy")
    z_p = a // 8
    y_p = lax.rem(a // 2, 4)
    x_p = lax.rem(a, 2)

    loads = [
        pltpu.make_async_copy(src, dst, load_sem.at[i])
        for i, (src, dst) in enumerate(
            (
                (cells_hbm, cells_ref), (slots_hbm, slots_ref), (count_hbm, count_ref),
                (feats_hbm, feats), (weight_hbm, weight_ref), (cot_hbm, cot),
            )
        )
    ]
    for load in loads:
        load.start()
    load_cells, load_slots, load_count, load_feats, load_weight, load_cot = loads

    a_near = {-1: lax.rem(a + n_a - 1, n_a), 0: a, 1: lax.rem(a + 1, n_a)}
    b_all = [b] + [lax.rem(b + k, n_b) for k in range(1, 4)]
    plane_all = [
        lax.rem(y_p + k // 2, 4) * 2 + (1 - x_p if k % 2 else x_p) for k in range(8)
    ]
    peers_1 = [(z_p * 8 + plane_all[d // 4], b_all[d % 4]) for d in range(1, 32)]
    peers_2 = [(lax.rem(z_p + k, 8) * 8 + plane_all[0], b) for k in range(1, 8)]

    def near(da, db):
        return (a_near[da], b_all[db % 4])

    around = [(da, db) for da in (-1, 0, 1) for db in (-1, 0, 1) if (da, db) != (0, 0)]
    if comm:
        barrier = pltpu.get_barrier_semaphore()
        for place in [near(da, db) for da, db in around] + peers_1 + peers_2:
            pl.semaphore_signal(barrier, inc=1, device_id=place, device_id_type=MESH)

    tap_row = lax.broadcasted_iota(jnp.int32, (144, 128), 0)
    tap_col = lax.broadcasted_iota(jnp.int32, (144, 128), 1)
    tap_base = jnp.bitwise_and(tap_row, 3) + jnp.right_shift(tap_row, 4) * (3 * GRP)
    spread = [tap_base + GRP * col_k == tap_col for col_k in range(3)]
    out_ch = lax.broadcasted_iota(jnp.int32, (CH, 144), 0)
    in_ch = jnp.bitwise_and(lax.broadcasted_iota(jnp.int32, (CH, 144), 1), 15)
    same_group = jnp.right_shift(out_ch, 2) == jnp.right_shift(in_ch, 2)
    load_cells.wait()
    load_slots.wait()
    load_count.wait()
    cells = jnp.concatenate(
        [cells_ref[pl.ds(0, 56, stride=2), :], cells_ref[pl.ds(1, 56, stride=2), :]], axis=1
    )
    cell_y = jnp.right_shift(jnp.bitwise_and(cells, 1023), 7) * 128
    cell_x = jnp.bitwise_and(cells, 127)
    pad = jnp.zeros((8, LO), f32)
    cell_table = jnp.concatenate(
        [cell_y.astype(f32), pad, cell_x.astype(f32), pad], axis=0
    ).astype(bf16)
    lane = lax.broadcasted_iota(jnp.int32, (1, S), 1)
    leaving = jnp.zeros((64, LO), f32)
    for side in range(2):
        listed = lane < count_ref[:, side : side + 1]
        slot = slots_ref[0, side : side + 1, :]
        slot_hi = jnp.where(listed, jnp.right_shift(slot, 8), -1)
        hot_lo = one_hot(jnp.bitwise_and(slot, 255).astype(f32).astype(bf16), LO)
        hot_hi = lax.broadcasted_iota(jnp.int32, (64, S), 0) == slot_hi
        leaving += lax.dot_general(
            hot_hi.astype(f32).astype(bf16), hot_lo, NT, preferred_element_type=f32
        )
        found = jnp.dot(cell_table, hot_lo, preferred_element_type=f32)
        place = jnp.sum(jnp.where(hot_hi, found[:64] + found[64:], 0.0), axis=0, keepdims=True)
        list_send[side] = jnp.where(listed, place, -1.0)
    code = (
        jnp.bitwise_and(jnp.right_shift(cells, 8), 3) + jnp.right_shift(cells, 10) * 8
    ).astype(f32) + 4.0 * leaving[:56]
    low = jnp.bitwise_and(cells, 255).astype(f32)
    for row in range(7 * OWN):
        k, j = divmod(row, 7)
        codes[k, :, LO * j : LO * (j + 1)] = code[row : row + 1]
        lows[k, :, LO * j : LO * (j + 1)] = low[row : row + 1]

    load_feats.wait()
    acc[...] = jnp.zeros_like(acc)

    def splat_own(k, carry):
        hot = one_hot(lows[k].astype(bf16), LO)
        onehots[k] = hot
        row = codes[k].astype(bf16)
        values = feats[:, pl.ds(pl.multiple_of(k * S, 128), S)]
        rows = masked_rows(row, values, range(16)) + [one_hot(row, 16)]
        acc[...] += lax.dot_general(
            jnp.concatenate(rows, axis=0), hot, NT, preferred_element_type=f32
        )
        return carry

    lax.fori_loop(0, OWN, splat_own, 0, unroll=4)

    counts = acc[256:272, :]
    count_hi = jnp.floor(counts * (1.0 / 256.0))
    count_lo = counts - 256.0 * count_hi

    def block(number, row):
        lanes = slice(128 * (row % 2), 128 * (row % 2) + 128)
        return acc[16 * number : 16 * number + 16, lanes].astype(bf16)

    def rows_of(numbers, first_row):
        return [block(4 * plane + first_row // 2, first_row) for plane in numbers]

    for ref, members in ((up_send, UP_MSG), (down_send, DOWN_MSG)):
        for i, number in enumerate(members):
            ref[2 * i] = block(number, 0)
            ref[2 * i + 1] = block(number, 1)
        both = jnp.concatenate(
            [part_of[c : c + 4] for part_of in (count_lo, count_hi) for c in members[::4]], axis=0
        ).astype(bf16)
        ref[16] = both[:, :128]
        ref[17] = both[:, 128:]
    for side in range(2):
        lanes = slice(128 * side, 128 * side + 128)
        for i, plane in enumerate(range(4)):
            side_send[side, i] = block(4 * plane + 3 * side, side)
        side_send[side, 4] = count_lo[:, lanes].astype(bf16)
        side_send[side, 5] = count_hi[:, lanes].astype(bf16)
        for vertical, planes in ((0, (0, 3)), (1, (1, 2))):
            for i, plane in enumerate(planes):
                corner_send[2 * vertical + side, i] = block(4 * plane + 3 * side, side)
            corner_send[2 * vertical + side, 2] = count_lo[:, lanes].astype(bf16)
            corner_send[2 * vertical + side, 3] = count_hi[:, lanes].astype(bf16)

    copies = []

    def send(src, dst, place, da, db):
        if comm:
            copy = pltpu.make_async_remote_copy(
                src_ref=src, dst_ref=dst, send_sem=send_sem.at[place],
                recv_sem=recv_sem.at[place], device_id=near(da, db), device_id_type=MESH,
            )
            copy.start()
            copies.append(copy)

    if comm:
        pl.semaphore_wait(barrier, len(around) + len(peers_1) + len(peers_2))
    send(list_send.at[0], list_recv.at[1], 0, -1, 0)
    send(list_send.at[1], list_recv.at[0], 1, 1, 0)
    send(up_send, up_recv, 2, 1, 0)
    send(down_send, down_recv, 3, -1, 0)
    for side in range(2):
        db = 2 * side - 1
        send(side_send.at[side], side_recv.at[side], 4 + side, 0, db)
        for vertical in range(2):
            i = 2 * vertical + side
            send(corner_send.at[i], corner_recv.at[i], 6 + i, 2 * vertical - 1, db)

    load_weight.wait()
    weight = jnp.concatenate(
        [weight_ref[i].astype(f32) for i in range(27)] + [jnp.zeros((20, CH), f32)], axis=0
    ).T.astype(bf16)
    for col_k in range(3):
        picked = lax.dot_general(
            weight, spread[col_k].astype(bf16), NT, preferred_element_type=f32
        )
        wmat[16 * col_k : 16 * col_k + 16, :] = jnp.where(same_group, picked, 0.0).astype(bf16)

    load_cot.wait()
    acc_cot[...] = jnp.zeros_like(acc_cot)

    def splat_cot(k, carry):
        row = codes[k].astype(bf16)
        values = cot[:, pl.ds(pl.multiple_of(k * S, 128), S)]
        acc_cot[...] += lax.dot_general(
            jnp.concatenate(masked_rows(row, values, STAY), axis=0), onehots[k], NT,
            preferred_element_type=f32,
        )
        return carry

    lax.fori_loop(0, OWN, splat_cot, 0, unroll=4)

    if comm:
        copies[0].wait()
        copies[1].wait()
    for side in range(2):
        present = (a > 0) if side == 0 else (a < n_a - 1)
        place = jnp.where(present, list_recv[side], -1.0).astype(jnp.int32)
        live = place >= 0
        row = jnp.where(live, jnp.right_shift(place, 8) + 8 * side, 16).astype(f32)
        codes[OWN + side] = row
        hot = one_hot(jnp.bitwise_and(place, 255).astype(f32).astype(bf16), LO)
        onehots[OWN + side] = hot
        values = cot[:, (OWN + side) * S : (OWN + side + 1) * S]
        members = STAY[4 * side : 4 * side + 4]
        acc_cot[64 * side : 64 * side + 64, :] += lax.dot_general(
            jnp.concatenate(masked_rows(row.astype(bf16), values, members), axis=0), hot, NT,
            preferred_element_type=f32,
        )

    if comm:
        for copy in copies[2:]:
            copy.wait()
    has_below = a > 0
    has_above = a < n_a - 1
    has_left = b > 0
    has_right = b < n_b - 1

    for i, (ref, flag) in enumerate(((up_recv, has_below), (down_recv, has_above))):
        for half in range(2):
            both = ref[16 + half].astype(f32)
            counts_in[2 * i + half, 0:8] = jnp.where(flag, both[0:8] + 256.0 * both[8:16], 0.0)
    side_flag = (has_right, has_left)
    for side in range(2):
        for i, (ref, at) in enumerate(
            ((side_recv.at[side], 4), (corner_recv.at[side], 2), (corner_recv.at[2 + side], 2))
        ):
            flag = side_flag[side]
            if i == 1:
                flag = jnp.logical_and(flag, has_above)
            if i == 2:
                flag = jnp.logical_and(flag, has_below)
            total = ref[at + 1].astype(f32) * 256.0 + ref[at].astype(f32)
            counts_in[(4 if i == 0 else 4 + 2 * i) + side] = jnp.where(flag, total, 0.0)

    def mean(sums, count):
        return sums / jnp.maximum(count, 1.0)

    sources = (
        (3, up_recv, 4, 0, has_below),
        (0, up_recv, 0, 0, has_below),
        (2, down_recv, 4, 2, has_above),
        (1, down_recv, 0, 2, has_above),
    )
    for plane, (mine, ref, at, where, flag) in enumerate(sources):
        for row in range(8):
            half = row % 2
            lanes = slice(128 * half, 128 * half + 128)
            number = 4 * mine + row // 2
            other = at + row // 2
            got = ref[2 * (at + row // 2) + half].astype(f32)
            sums = acc[16 * number : 16 * number + 16, lanes] + jnp.where(flag, got, 0.0)
            count = acc[256 + number : 257 + number, lanes]
            count = count + counts_in[where + half, other : other + 1, :]
            divisor = jnp.broadcast_to(jnp.maximum(count, 1.0), (CH, 128))
            grid[plane, 1 + row] = (sums / divisor).astype(bf16)
            if plane in (1, 2):
                divisors[8 * (plane - 1) + row] = divisor
    for side in range(2):
        flag = side_flag[side]
        y_hi = 3 * side
        halo = (
            (3, 1, 1, 2, has_below),
            (0, 1, 0, 1, has_below),
            (2, 0, 1, 3, has_above),
            (1, 0, 0, 0, has_above),
        )
        for plane, (direct, vertical, at, theirs, vertical_flag) in enumerate(halo):
            corner = 2 * vertical + side
            both = jnp.logical_and(flag, vertical_flag)
            sums = jnp.where(flag, side_recv[side, direct].astype(f32), 0.0)
            sums = sums + jnp.where(both, corner_recv[corner, at].astype(f32), 0.0)
            mine = 4 * direct + y_hi
            other = 4 * theirs + y_hi
            kind = 6 if vertical == 0 else 8
            count = counts_in[4 + side, mine : mine + 1, :]
            count = count + counts_in[kind + side, other : other + 1, :]
            grid[plane, 9 * (1 - side)] = mean(sums, count).astype(bf16)

    lane = lax.broadcasted_iota(jnp.int32, (CH, X), 1)
    first_x = lane == 0
    last_x = lane == X - 1
    for z in range(CZ):
        stacked = jnp.concatenate(
            [
                jnp.concatenate([grid[z + u, v + y] for y in range(CY)], axis=1)
                for u in range(3)
                for v in range(3)
            ],
            axis=0,
        )
        patches[z] = stacked
        pre[...] = jnp.dot(wmat[...], stacked, preferred_element_type=f32)
        for y in range(CY):
            lanes = slice(128 * y, 128 * y + 128)
            low_x = pltpu.roll(pre[0:16, lanes], 1, 1)
            high_x = pltpu.roll(pre[32:48, lanes], X - 1, 1)
            value = (
                pre[16:32, lanes]
                + jnp.where(first_x, 0.0, low_x)
                + jnp.where(last_x, 0.0, high_x)
            )
            sigma = sigmoid(value)
            group = 4 * z + y // 2
            half = slice(128 * (y % 2), 128 * (y % 2) + 128)
            act[16 * group : 16 * group + 16, half] = (value * sigma).astype(bf16)
            cot_sum = acc_cot[16 * group : 16 * group + 16, half]
            gpad[z + 1, y + 1] = (cot_sum * sigma * (1.0 + value * (1.0 - sigma))).astype(bf16)

    def move(plane, row):
        value = gpad[plane, row]
        wide = value.astype(f32)
        gp3[plane, row, 0:16] = jnp.where(last_x, 0.0, pltpu.roll(wide, X - 1, 1)).astype(bf16)
        gp3[plane, row, 16:32] = value
        gp3[plane, row, 32:48] = jnp.where(first_x, 0.0, pltpu.roll(wide, 1, 1)).astype(bf16)

    wide_grad = jnp.zeros((48, 144), f32)
    for z in range(CZ):
        for y in range(CY):
            move(z + 1, y + 1)
        moved = jnp.concatenate([gp3[z + 1, y + 1] for y in range(CY)], axis=1)
        wide_grad += lax.dot_general(moved, patches[z], NT, preferred_element_type=f32)
    compact = jnp.zeros((CH, 128), f32)
    for col_k in range(3):
        kept = jnp.where(same_group, wide_grad[16 * col_k : 16 * col_k + 16], 0.0)
        first = kept.astype(bf16)
        rest = kept - first.astype(f32)
        second = rest.astype(bf16)
        third = (rest - second.astype(f32)).astype(bf16)
        picked = jnp.dot(
            jnp.concatenate([first, second, third], axis=0), spread[col_k].astype(bf16),
            preferred_element_type=f32,
        )
        compact += picked[0:16] + picked[16:32] + picked[32:48]
    part[...] = compact.astype(bf16)

    def reduce_send(step, peers, source, target):
        if comm:
            for d, place in enumerate(peers):
                pltpu.make_async_remote_copy(
                    src_ref=source, dst_ref=target.at[d], send_sem=red_send.at[step],
                    recv_sem=red_recv.at[step], device_id=place, device_id_type=MESH,
                ).start()

    def reduce_wait(step, buffer):
        if comm:
            pltpu.make_async_copy(buffer, buffer, red_send.at[step]).wait()
            pltpu.make_async_copy(buffer, buffer, red_recv.at[step]).wait()

    reduce_send(0, peers_1, part, gather_1)
    copies_2 = []

    def send_2nd(src, dst, place, da, db):
        if comm:
            copy = pltpu.make_async_remote_copy(
                src_ref=src, dst_ref=dst, send_sem=send_2.at[place],
                recv_sem=recv_2.at[place], device_id=near(da, db), device_id_type=MESH,
            )
            copy.start()
            copies_2.append(copy)

    send_2nd(gpad.at[1, pl.ds(1, 8)], gpad.at[3, pl.ds(1, 8)], 0, -1, 0)
    send_2nd(gpad.at[2, pl.ds(1, 8)], gpad.at[0, pl.ds(1, 8)], 1, 1, 0)
    send_2nd(gpad.at[pl.ds(1, 2), 1], gpad.at[pl.ds(1, 2), 9], 2, 0, -1)
    send_2nd(gpad.at[pl.ds(1, 2), 8], gpad.at[pl.ds(1, 2), 0], 3, 0, 1)
    send_2nd(gpad.at[1, 1], gpad.at[3, 9], 4, -1, -1)
    send_2nd(gpad.at[1, 8], gpad.at[3, 0], 5, -1, 1)
    send_2nd(gpad.at[2, 1], gpad.at[0, 9], 6, 1, -1)
    send_2nd(gpad.at[2, 8], gpad.at[0, 0], 7, 1, 1)


    def read_back(values, into):
        def body(k, carry):
            found = jnp.dot(values[...], onehots[k], preferred_element_type=f32)
            into[:, pl.ds(pl.multiple_of(k * S, 128), S)] = select(found, codes[k])
            return carry

        lax.fori_loop(0, ALL, body, 0, unroll=5)

    read_back(act, out_buf)

    for copy in copies_2:
        copy.wait()
    blank = jnp.zeros((CH, X), bf16)

    def clear(flag, places):
        @pl.when(flag)
        def _():
            for plane, row in places:
                gpad[plane, row] = blank

    clear(a == 0, [(0, row) for row in range(10)])
    clear(a == n_a - 1, [(3, row) for row in range(10)])
    clear(b == 0, [(plane, 0) for plane in range(4)])
    clear(b == n_b - 1, [(plane, 9) for plane in range(4)])
    for plane in range(4):
        for row in range(10):
            if plane in (0, 3) or row in (0, 9):
                move(plane, row)
    result = [None] * 16
    for plane in range(4):
        moved = jnp.concatenate([gp3[plane, row] for row in range(10)], axis=1)
        taps = lax.dot_general(
            wmat[...], moved, (((0,), (0,)), ((), ())), preferred_element_type=f32
        )
        for u in range(3):
            z = plane - 2 + u
            if z not in (0, 1):
                continue
            for v in range(3):
                rows = slice(16 * (3 * u + v), 16 * (3 * u + v) + 16)
                for y in range(CY):
                    source = y + 2 - v
                    term = taps[rows, 128 * source : 128 * source + 128]
                    i = 8 * z + y
                    result[i] = term if result[i] is None else result[i] + term
    for i in range(16):
        group = i // 2
        half = slice(128 * (i % 2), 128 * (i % 2) + 128)
        table[16 * group : 16 * group + 16, half] = (result[i] / divisors[i]).astype(bf16)
    reduce_wait(0, gather_1)
    total = compact
    for d in range(31):
        total = total + gather_1[d].astype(f32)
    plane_sum[...] = total.astype(bf16)
    reduce_send(1, peers_2, plane_sum, gather_2)

    read_back(table, grad_buf)

    reduce_wait(1, gather_2)
    for d in range(7):
        total = total + gather_2[d].astype(f32)
    total = (total * (1.0 / math.sqrt(CZ * CY * X * n_a * n_b))).T
    for i in range(27):
        wgrad_ref[i] = total[GRP * i : GRP * i + GRP]


def copy_kernel(*refs):
    sources, targets, sem = refs[:3], refs[3:6], refs[6]
    copies = [
        pltpu.make_async_copy(src, dst, sem.at[i])
        for i, (src, dst) in enumerate(zip(sources, targets))
    ]
    for copy in copies:
        copy.start()
    for copy in copies:
        copy.wait()


def fused(feats, cot, cells, slots, count, weight, comm=True):
    hbm = pl.BlockSpec(memory_space=pltpu.HBM)
    vmem = pl.BlockSpec(memory_space=pltpu.VMEM)
    slots_all = ALL * S
    dma = pltpu.SemaphoreType.DMA
    shape = jax.ShapeDtypeStruct
    feats, cot, cells, slots, count, weight = (
        pltpu.with_memory_space_constraint(v, pltpu.HBM)
        for v in (feats, cot, cells, slots, count, weight)
    )
    parts = pl.pallas_call(
        functools.partial(kernel, comm=comm),
        out_shape=[
            shape((CH, slots_all), bf16),
            shape((CH, slots_all), bf16),
            shape((27, GRP, CH), f32),
        ],
        in_specs=[hbm] * 6,
        out_specs=[vmem] * 3,
        scratch_shapes=[
            pltpu.VMEM((ALL, LO, S), bf16),
            pltpu.VMEM((ALL, 1, S), f32),
            pltpu.VMEM((128, LO), bf16),
            pltpu.VMEM((CH, OWN * S), bf16),
            pltpu.VMEM((CH, slots_all), bf16),
            pltpu.VMEM((112, 128), jnp.int32),
            pltpu.VMEM((1, 2, S), jnp.int32),
            pltpu.VMEM((1, 2), jnp.int32),
            pltpu.VMEM((27, GRP, CH), bf16),
            pltpu.VMEM((OWN, 1, S), f32),
            pltpu.VMEM((272, LO), f32),
            pltpu.VMEM((128, LO), f32),
            pltpu.VMEM((2, 1, S), f32),
            pltpu.VMEM((2, 1, S), f32),
            pltpu.VMEM((18, CH, 128), bf16),
            pltpu.VMEM((18, CH, 128), bf16),
            pltpu.VMEM((18, CH, 128), bf16),
            pltpu.VMEM((18, CH, 128), bf16),
            pltpu.VMEM((2, 6, CH, 128), bf16),
            pltpu.VMEM((2, 6, CH, 128), bf16),
            pltpu.VMEM((4, 4, CH, 128), bf16),
            pltpu.VMEM((4, 4, CH, 128), bf16),
            pltpu.VMEM((4, 10, CH, 128), bf16),
            pltpu.VMEM((4, 10, CH, 128), bf16),
            pltpu.VMEM((CZ, 144, CY * X), bf16),
            pltpu.VMEM((4, 10, 48, 128), bf16),
            pltpu.VMEM((128, LO), bf16),
            pltpu.VMEM((16, CH, 128), f32),
            pltpu.VMEM((48, 144), bf16),
            pltpu.VMEM((10, CH, 128), f32),
            pltpu.VMEM((48, CY * X), f32),
            pltpu.VMEM((CH, 128), bf16),
            pltpu.VMEM((31, CH, 128), bf16),
            pltpu.VMEM((CH, 128), bf16),
            pltpu.VMEM((7, CH, 128), bf16),
            dma((6,)),
            dma((10,)),
            dma((10,)),
            dma((8,)),
            dma((8,)),
            dma((2,)),
            dma((2,)),
        ],
        compiler_params=pltpu.CompilerParams(
            vmem_limit_bytes=30 << 20,
            **(dict(collective_id=0, has_side_effects=True) if comm else {}),
        ),
    )(feats, cot, cells, slots, count, weight)
    return pl.pallas_call(
        copy_kernel,
        out_shape=[
            shape((CH, slots_all), bf16),
            shape((CH, slots_all), bf16),
            shape((27, GRP, CH), f32),
        ],
        in_specs=[vmem] * 3,
        out_specs=[hbm] * 3,
        scratch_shapes=[dma((3,))],
    )(*(pltpu.with_memory_space_constraint(v, pltpu.VMEM) for v in parts))


def local(point_feats, cell_index, send_slots, send_count, conv_weight, point_cot):
    cells = cell_index.reshape(-1, 128)
    weight = conv_weight.transpose(2, 3, 4, 1, 0).reshape(27, GRP, CH)
    out, grad, wgrad = fused(point_feats, point_cot, cells, send_slots, send_count, weight)
    return out, grad, wgrad.reshape(3, 3, 3, GRP, CH).transpose(4, 3, 0, 1, 2)


def solution(mesh):
    placed = (
        P(None, ("gz", "gy")),
        P(("gz", "gy")),
        P(("gz", "gy"), None, None),
        P(("gz", "gy"), None),
        P(),
        P(None, ("gz", "gy")),
    )
    return jax.shard_map(
        local,
        mesh=mesh,
        in_specs=placed,
        out_specs=(P(None, ("gz", "gy")), P(None, ("gz", "gy")), P()),
        check_vma=False,
    )
```

```python
import functools
import math

import jax
import jax.numpy as jnp
from jax import lax
from jax.experimental import pallas as pl
from jax.experimental.pallas import tpu as pltpu
from jax.sharding import PartitionSpec as P

CH = 16
GRP = 4
X = 128
CY = 8
CZ = 2
S = 1792
OWN = 8
ALL = OWN + 2
LO = 256
MESH = pl.DeviceIdType.MESH
f32 = jnp.float32
bf16 = jnp.bfloat16
NT = (((1,), (1,)), ((), ()))

UP_MSG = tuple(range(4, 12))
DOWN_MSG = (0, 1, 2, 3, 12, 13, 14, 15)
STAY = (0, 1, 2, 3, 8, 9, 10, 11)


def one_hot(row, count):
    ids = lax.broadcasted_iota(jnp.int32, (count, row.shape[1]), 0).astype(f32).astype(bf16)
    return jnp.where(ids == row, jnp.ones((), bf16), jnp.zeros((), bf16))


def masked_rows(row, values, codes):
    zero = jnp.zeros((), bf16)
    return [jnp.where(row == jnp.full((), code, bf16), values, zero) for code in codes]


def sigmoid(v):
    return 1.0 / (1.0 + jnp.exp(-v))


def select(found, row):
    value = jnp.zeros((CH, S), f32)
    for i, number in enumerate(STAY):
        value = jnp.where(row == float(number), found[16 * i : 16 * i + 16], value)
    return value.astype(bf16)


def kernel(
    feats_hbm, cot_hbm, cells_hbm, slots_hbm, count_hbm, weight_hbm,
    out_buf, grad_buf, wgrad_ref,
    onehots, codes, table, feats, cot, cells_ref, slots_ref, count_ref, weight_ref, lows, acc, acc_cot,
    list_send, list_recv,
    up_send, down_send, up_recv, down_recv,
    side_send, side_recv, corner_send, corner_recv,
    grid, gpad, patches, gp3, act, divisors, wmat, counts_in, pre,
    part, gather_1, plane_sum, gather_2,
    load_sem, send_sem, recv_sem, send_2, recv_2, red_send, red_recv,
    *, comm,
):
    a = lax.axis_index("gz")
    b = lax.axis_index("gy")
    n_a = lax.axis_size("gz")
    n_b = lax.axis_size("gy")
    z_p = a // 8
    y_p = lax.rem(a // 2, 4)
    x_p = lax.rem(a, 2)

    loads = [
        pltpu.make_async_copy(src, dst, load_sem.at[i])
        for i, (src, dst) in enumerate(
            (
                (cells_hbm, cells_ref), (slots_hbm, slots_ref), (count_hbm, count_ref),
                (feats_hbm, feats), (weight_hbm, weight_ref), (cot_hbm, cot),
            )
        )
    ]
    for load in loads:
        load.start()
    load_cells, load_slots, load_count, load_feats, load_weight, load_cot = loads

    a_near = {-1: lax.rem(a + n_a - 1, n_a), 0: a, 1: lax.rem(a + 1, n_a)}
    b_all = [b] + [lax.rem(b + k, n_b) for k in range(1, 4)]
    plane_all = [
        lax.rem(y_p + k // 2, 4) * 2 + (1 - x_p if k % 2 else x_p) for k in range(8)
    ]
    peers_1 = [(z_p * 8 + plane_all[d // 4], b_all[d % 4]) for d in range(1, 32)]
    peers_2 = [(lax.rem(z_p + k, 8) * 8 + plane_all[0], b) for k in range(1, 8)]

    def near(da, db):
        return (a_near[da], b_all[db % 4])

    around = [(da, db) for da in (-1, 0, 1) for db in (-1, 0, 1) if (da, db) != (0, 0)]
    if comm:
        barrier = pltpu.get_barrier_semaphore()
        for place in [near(da, db) for da, db in around] + peers_1 + peers_2:
            pl.semaphore_signal(barrier, inc=1, device_id=place, device_id_type=MESH)

    tap_row = lax.broadcasted_iota(jnp.int32, (144, 128), 0)
    tap_col = lax.broadcasted_iota(jnp.int32, (144, 128), 1)
    tap_base = jnp.bitwise_and(tap_row, 3) + jnp.right_shift(tap_row, 4) * (3 * GRP)
    spread = [tap_base + GRP * col_k == tap_col for col_k in range(3)]
    out_ch = lax.broadcasted_iota(jnp.int32, (CH, 144), 0)
    in_ch = jnp.bitwise_and(lax.broadcasted_iota(jnp.int32, (CH, 144), 1), 15)
    same_group = jnp.right_shift(out_ch, 2) == jnp.right_shift(in_ch, 2)
    load_cells.wait()
    load_slots.wait()
    load_count.wait()
    cells = jnp.concatenate(
        [cells_ref[pl.ds(0, 56, stride=2), :], cells_ref[pl.ds(1, 56, stride=2), :]], axis=1
    )
    cell_y = jnp.right_shift(jnp.bitwise_and(cells, 1023), 7) * 128
    cell_x = jnp.bitwise_and(cells, 127)
    pad = jnp.zeros((8, LO), f32)
    cell_table = jnp.concatenate(
        [cell_y.astype(f32), pad, cell_x.astype(f32), pad], axis=0
    ).astype(bf16)
    lane = lax.broadcasted_iota(jnp.int32, (1, S), 1)
    leaving = jnp.zeros((64, LO), f32)
    for side in range(2):
        listed = lane < count_ref[:, side : side + 1]
        slot = slots_ref[0, side : side + 1, :]
        slot_hi = jnp.where(listed, jnp.right_shift(slot, 8), -1)
        hot_lo = one_hot(jnp.bitwise_and(slot, 255).astype(f32).astype(bf16), LO)
        hot_hi = lax.broadcasted_iota(jnp.int32, (64, S), 0) == slot_hi
        leaving += lax.dot_general(
            hot_hi.astype(f32).astype(bf16), hot_lo, NT, preferred_element_type=f32
        )
        found = jnp.dot(cell_table, hot_lo, preferred_element_type=f32)
        place = jnp.sum(jnp.where(hot_hi, found[:64] + found[64:], 0.0), axis=0, keepdims=True)
        list_send[side] = jnp.where(listed, place, -1.0)
    code = (
        jnp.bitwise_and(jnp.right_shift(cells, 8), 3) + jnp.right_shift(cells, 10) * 8
    ).astype(f32) + 4.0 * leaving[:56]
    low = jnp.bitwise_and(cells, 255).astype(f32)
    for row in range(7 * OWN):
        k, j = divmod(row, 7)
        codes[k, :, LO * j : LO * (j + 1)] = code[row : row + 1]
        lows[k, :, LO * j : LO * (j + 1)] = low[row : row + 1]

    load_feats.wait()
    acc[...] = jnp.zeros_like(acc)

    def splat_own(k, carry):
        hot = one_hot(lows[k].astype(bf16), LO)
        onehots[k] = hot
        row = codes[k].astype(bf16)
        values = feats[:, pl.ds(pl.multiple_of(k * S, 128), S)]
        rows = masked_rows(row, values, range(16)) + [one_hot(row, 16)]
        acc[...] += lax.dot_general(
            jnp.concatenate(rows, axis=0), hot, NT, preferred_element_type=f32
        )
        return carry

    lax.fori_loop(0, OWN, splat_own, 0, unroll=4)

    counts = acc[256:272, :]
    count_hi = jnp.floor(counts * (1.0 / 256.0))
    count_lo = counts - 256.0 * count_hi

    def block(number, row):
        lanes = slice(128 * (row % 2), 128 * (row % 2) + 128)
        return acc[16 * number : 16 * number + 16, lanes].astype(bf16)

    def rows_of(numbers, first_row):
        return [block(4 * plane + first_row // 2, first_row) for plane in numbers]

    for ref, members in ((up_send, UP_MSG), (down_send, DOWN_MSG)):
        for i, number in enumerate(members):
            ref[2 * i] = block(number, 0)
            ref[2 * i + 1] = block(number, 1)
        both = jnp.concatenate(
            [part_of[c : c + 4] for part_of in (count_lo, count_hi) for c in members[::4]], axis=0
        ).astype(bf16)
        ref[16] = both[:, :128]
        ref[17] = both[:, 128:]
    nothing = jnp.zeros((8, 128), f32)
    for side in range(2):
        lanes = slice(128 * side, 128 * side + 128)
        rows = [
            part_of[4 * plane + 3 * side : 4 * plane + 3 * side + 1, lanes]
            for part_of in (count_lo, count_hi)
            for plane in range(4)
        ]
        tile = jnp.concatenate(rows + [nothing], axis=0).astype(bf16)
        for plane in range(4):
            side_send[side, plane] = block(4 * plane + 3 * side, side)
        side_send[side, 4] = tile
        for vertical, planes in ((0, (0, 3)), (1, (1, 2))):
            for i, plane in enumerate(planes):
                corner_send[2 * vertical + side, i] = block(4 * plane + 3 * side, side)
            corner_send[2 * vertical + side, 2] = tile

    def inside(da, db):
        tests = []
        if da:
            tests.append(a < n_a - 1 if da > 0 else a > 0)
        if db:
            tests.append(b < n_b - 1 if db > 0 else b > 0)
        return tests[0] if len(tests) == 1 else jnp.logical_and(*tests)

    def send(src, dst, sems, place, da, db):
        if not comm:
            return lambda: None
        copy = pltpu.make_async_remote_copy(
            src_ref=src, dst_ref=dst, send_sem=sems[0].at[place],
            recv_sem=sems[1].at[place], device_id=near(da, db), device_id_type=MESH,
        )

        @pl.when(inside(da, db))
        def _():
            copy.start()

        def finish():
            @pl.when(inside(da, db))
            def _():
                copy.wait_send()

            @pl.when(inside(-da, -db))
            def _():
                copy.wait_recv()

        return finish

    if comm:
        pl.semaphore_wait(barrier, len(around) + len(peers_1) + len(peers_2))
    first = (send_sem, recv_sem)
    finish_lists = [
        send(list_send.at[0], list_recv.at[1], first, 0, -1, 0),
        send(list_send.at[1], list_recv.at[0], first, 1, 1, 0),
    ]
    finish_grid = [
        send(up_send, up_recv, first, 2, 1, 0),
        send(down_send, down_recv, first, 3, -1, 0),
    ]
    for side in range(2):
        db = 2 * side - 1
        finish_grid.append(send(side_send.at[side], side_recv.at[side], first, 4 + side, 0, db))
        for vertical in range(2):
            i = 2 * vertical + side
            finish_grid.append(
                send(corner_send.at[i], corner_recv.at[i], first, 6 + i, 2 * vertical - 1, db)
            )

    load_weight.wait()
    weight = jnp.concatenate(
        [weight_ref[i].astype(f32) for i in range(27)] + [jnp.zeros((20, CH), f32)], axis=0
    ).T.astype(bf16)
    for col_k in range(3):
        picked = lax.dot_general(
            weight, spread[col_k].astype(bf16), NT, preferred_element_type=f32
        )
        wmat[16 * col_k : 16 * col_k + 16, :] = jnp.where(same_group, picked, 0.0).astype(bf16)

    load_cot.wait()
    acc_cot[...] = jnp.zeros_like(acc_cot)

    def splat_cot(k, carry):
        row = codes[k].astype(bf16)
        values = cot[:, pl.ds(pl.multiple_of(k * S, 128), S)]
        acc_cot[...] += lax.dot_general(
            jnp.concatenate(masked_rows(row, values, STAY), axis=0), onehots[k], NT,
            preferred_element_type=f32,
        )
        return carry

    lax.fori_loop(0, OWN, splat_cot, 0, unroll=4)

    for finish in finish_lists:
        finish()
    for side in range(2):
        present = (a > 0) if side == 0 else (a < n_a - 1)
        place = jnp.where(present, list_recv[side], -1.0).astype(jnp.int32)
        live = place >= 0
        row = jnp.where(live, jnp.right_shift(place, 8) + 8 * side, 16).astype(f32)
        codes[OWN + side] = row
        hot = one_hot(jnp.bitwise_and(place, 255).astype(f32).astype(bf16), LO)
        onehots[OWN + side] = hot
        values = cot[:, (OWN + side) * S : (OWN + side + 1) * S]
        members = STAY[4 * side : 4 * side + 4]
        acc_cot[64 * side : 64 * side + 64, :] += lax.dot_general(
            jnp.concatenate(masked_rows(row.astype(bf16), values, members), axis=0), hot, NT,
            preferred_element_type=f32,
        )

    for finish in finish_grid:
        finish()
    has_below = a > 0
    has_above = a < n_a - 1
    has_left = b > 0
    has_right = b < n_b - 1

    for i, (ref, flag) in enumerate(((up_recv, has_below), (down_recv, has_above))):
        for half in range(2):
            both = ref[16 + half].astype(f32)
            counts_in[2 * i + half, 0:8] = jnp.where(flag, both[0:8] + 256.0 * both[8:16], 0.0)
    side_flag = (has_right, has_left)
    for side in range(2):
        for i, (ref, at) in enumerate(
            ((side_recv.at[side], 4), (corner_recv.at[side], 2), (corner_recv.at[2 + side], 2))
        ):
            flag = side_flag[side]
            if i == 1:
                flag = jnp.logical_and(flag, has_above)
            if i == 2:
                flag = jnp.logical_and(flag, has_below)
            both = ref[at].astype(f32)
            counts_in[4 + 2 * i + side, 0:4] = jnp.where(flag, both[0:4] + 256.0 * both[4:8], 0.0)

    def mean(sums, count):
        return sums / jnp.maximum(count, 1.0)

    sources = (
        (3, up_recv, 4, 0, has_below),
        (0, up_recv, 0, 0, has_below),
        (2, down_recv, 4, 2, has_above),
        (1, down_recv, 0, 2, has_above),
    )
    for plane, (mine, ref, at, where, flag) in enumerate(sources):
        for row in range(8):
            half = row % 2
            lanes = slice(128 * half, 128 * half + 128)
            number = 4 * mine + row // 2
            other = at + row // 2
            got = ref[2 * (at + row // 2) + half].astype(f32)
            sums = acc[16 * number : 16 * number + 16, lanes] + jnp.where(flag, got, 0.0)
            count = acc[256 + number : 257 + number, lanes]
            count = count + counts_in[where + half, other : other + 1, :]
            divisor = jnp.broadcast_to(jnp.maximum(count, 1.0), (CH, 128))
            grid[plane, 1 + row] = (sums / divisor).astype(bf16)
            if plane in (1, 2):
                divisors[8 * (plane - 1) + row] = divisor
    for side in range(2):
        flag = side_flag[side]
        halo = (
            (3, 1, 1, 2, has_below),
            (0, 1, 0, 1, has_below),
            (2, 0, 1, 3, has_above),
            (1, 0, 0, 0, has_above),
        )
        for plane, (direct, vertical, at, theirs, vertical_flag) in enumerate(halo):
            corner = 2 * vertical + side
            both = jnp.logical_and(flag, vertical_flag)
            sums = jnp.where(flag, side_recv[side, direct].astype(f32), 0.0)
            sums = sums + jnp.where(both, corner_recv[corner, at].astype(f32), 0.0)
            kind = 6 if vertical == 0 else 8
            count = counts_in[4 + side, direct : direct + 1, :]
            count = count + counts_in[kind + side, theirs : theirs + 1, :]
            grid[plane, 9 * (1 - side)] = mean(sums, count).astype(bf16)

    lane = lax.broadcasted_iota(jnp.int32, (CH, X), 1)
    first_x = lane == 0
    last_x = lane == X - 1
    for z in range(CZ):
        stacked = jnp.concatenate(
            [
                jnp.concatenate([grid[z + u, v + y] for y in range(CY)], axis=1)
                for u in range(3)
                for v in range(3)
            ],
            axis=0,
        )
        patches[z] = stacked
        pre[...] = jnp.dot(wmat[...], stacked, preferred_element_type=f32)
        for y in range(CY):
            lanes = slice(128 * y, 128 * y + 128)
            low_x = pltpu.roll(pre[0:16, lanes], 1, 1)
            high_x = pltpu.roll(pre[32:48, lanes], X - 1, 1)
            value = (
                pre[16:32, lanes]
                + jnp.where(first_x, 0.0, low_x)
                + jnp.where(last_x, 0.0, high_x)
            )
            sigma = sigmoid(value)
            group = 4 * z + y // 2
            half = slice(128 * (y % 2), 128 * (y % 2) + 128)
            act[16 * group : 16 * group + 16, half] = (value * sigma).astype(bf16)
            cot_sum = acc_cot[16 * group : 16 * group + 16, half]
            gpad[z + 1, y + 1] = (cot_sum * sigma * (1.0 + value * (1.0 - sigma))).astype(bf16)

    def move(plane, row):
        value = gpad[plane, row]
        wide = value.astype(f32)
        gp3[plane, row, 0:16] = jnp.where(last_x, 0.0, pltpu.roll(wide, X - 1, 1)).astype(bf16)
        gp3[plane, row, 16:32] = value
        gp3[plane, row, 32:48] = jnp.where(first_x, 0.0, pltpu.roll(wide, 1, 1)).astype(bf16)

    wide_grad = jnp.zeros((48, 144), f32)
    for z in range(CZ):
        for y in range(CY):
            move(z + 1, y + 1)
        moved = jnp.concatenate([gp3[z + 1, y + 1] for y in range(CY)], axis=1)
        wide_grad += lax.dot_general(moved, patches[z], NT, preferred_element_type=f32)
    compact = jnp.zeros((CH, 128), f32)
    for col_k in range(3):
        kept = jnp.where(same_group, wide_grad[16 * col_k : 16 * col_k + 16], 0.0)
        compact += jnp.dot(
            kept.astype(bf16), spread[col_k].astype(bf16), preferred_element_type=f32
        )
    part[...] = compact.astype(bf16)

    def reduce_send(step, peers, source, target):
        if comm:
            for d, place in enumerate(peers):
                pltpu.make_async_remote_copy(
                    src_ref=source, dst_ref=target.at[d], send_sem=red_send.at[step],
                    recv_sem=red_recv.at[step], device_id=place, device_id_type=MESH,
                ).start()

    def reduce_wait(step, buffer):
        if comm:
            pltpu.make_async_copy(buffer, buffer, red_send.at[step]).wait()
            pltpu.make_async_copy(buffer, buffer, red_recv.at[step]).wait()

    reduce_send(0, peers_1, part, gather_1)
    second = (send_2, recv_2)
    finish_halo = []

    def send_2nd(src, dst, place, da, db):
        finish_halo.append(send(src, dst, second, place, da, db))

    send_2nd(gpad.at[1, pl.ds(1, 8)], gpad.at[3, pl.ds(1, 8)], 0, -1, 0)
    send_2nd(gpad.at[2, pl.ds(1, 8)], gpad.at[0, pl.ds(1, 8)], 1, 1, 0)
    send_2nd(gpad.at[pl.ds(1, 2), 1], gpad.at[pl.ds(1, 2), 9], 2, 0, -1)
    send_2nd(gpad.at[pl.ds(1, 2), 8], gpad.at[pl.ds(1, 2), 0], 3, 0, 1)
    send_2nd(gpad.at[1, 1], gpad.at[3, 9], 4, -1, -1)
    send_2nd(gpad.at[1, 8], gpad.at[3, 0], 5, -1, 1)
    send_2nd(gpad.at[2, 1], gpad.at[0, 9], 6, 1, -1)
    send_2nd(gpad.at[2, 8], gpad.at[0, 0], 7, 1, 1)


    def read_back(values, into):
        def body(k, carry):
            found = jnp.dot(values[...], onehots[k], preferred_element_type=f32)
            into[:, pl.ds(pl.multiple_of(k * S, 128), S)] = select(found, codes[k])
            return carry

        lax.fori_loop(0, ALL, body, 0, unroll=5)

    read_back(act, out_buf)

    for finish in finish_halo:
        finish()
    blank = jnp.zeros((CH, X), bf16)

    def clear(flag, places):
        @pl.when(flag)
        def _():
            for plane, row in places:
                gpad[plane, row] = blank

    clear(a == 0, [(0, row) for row in range(10)])
    clear(a == n_a - 1, [(3, row) for row in range(10)])
    clear(b == 0, [(plane, 0) for plane in range(4)])
    clear(b == n_b - 1, [(plane, 9) for plane in range(4)])
    for plane in range(4):
        for row in range(10):
            if plane in (0, 3) or row in (0, 9):
                move(plane, row)
    result = [None] * 16
    for plane in range(4):
        moved = jnp.concatenate([gp3[plane, row] for row in range(10)], axis=1)
        taps = lax.dot_general(
            wmat[...], moved, (((0,), (0,)), ((), ())), preferred_element_type=f32
        )
        for u in range(3):
            z = plane - 2 + u
            if z not in (0, 1):
                continue
            for v in range(3):
                rows = slice(16 * (3 * u + v), 16 * (3 * u + v) + 16)
                for y in range(CY):
                    source = y + 2 - v
                    term = taps[rows, 128 * source : 128 * source + 128]
                    i = 8 * z + y
                    result[i] = term if result[i] is None else result[i] + term
    for i in range(16):
        group = i // 2
        half = slice(128 * (i % 2), 128 * (i % 2) + 128)
        table[16 * group : 16 * group + 16, half] = (result[i] / divisors[i]).astype(bf16)
    reduce_wait(0, gather_1)
    total = compact
    for d in range(31):
        total = total + gather_1[d].astype(f32)
    plane_sum[...] = total.astype(bf16)
    reduce_send(1, peers_2, plane_sum, gather_2)

    read_back(table, grad_buf)

    reduce_wait(1, gather_2)
    for d in range(7):
        total = total + gather_2[d].astype(f32)
    total = (total * (1.0 / math.sqrt(CZ * CY * X * n_a * n_b))).T
    for i in range(27):
        wgrad_ref[i] = total[GRP * i : GRP * i + GRP]


def copy_kernel(*refs):
    sources, targets, sem = refs[:3], refs[3:6], refs[6]
    copies = [
        pltpu.make_async_copy(src, dst, sem.at[i])
        for i, (src, dst) in enumerate(zip(sources, targets))
    ]
    for copy in copies:
        copy.start()
    for copy in copies:
        copy.wait()


def fused(feats, cot, cells, slots, count, weight, comm=True):
    hbm = pl.BlockSpec(memory_space=pltpu.HBM)
    vmem = pl.BlockSpec(memory_space=pltpu.VMEM)
    slots_all = ALL * S
    dma = pltpu.SemaphoreType.DMA
    shape = jax.ShapeDtypeStruct
    feats, cot, cells, slots, count, weight = (
        pltpu.with_memory_space_constraint(v, pltpu.HBM)
        for v in (feats, cot, cells, slots, count, weight)
    )
    parts = pl.pallas_call(
        functools.partial(kernel, comm=comm),
        out_shape=[
            shape((CH, slots_all), bf16),
            shape((CH, slots_all), bf16),
            shape((27, GRP, CH), f32),
        ],
        in_specs=[hbm] * 6,
        out_specs=[vmem] * 3,
        scratch_shapes=[
            pltpu.VMEM((ALL, LO, S), bf16),
            pltpu.VMEM((ALL, 1, S), f32),
            pltpu.VMEM((128, LO), bf16),
            pltpu.VMEM((CH, OWN * S), bf16),
            pltpu.VMEM((CH, slots_all), bf16),
            pltpu.VMEM((112, 128), jnp.int32),
            pltpu.VMEM((1, 2, S), jnp.int32),
            pltpu.VMEM((1, 2), jnp.int32),
            pltpu.VMEM((27, GRP, CH), bf16),
            pltpu.VMEM((OWN, 1, S), f32),
            pltpu.VMEM((272, LO), f32),
            pltpu.VMEM((128, LO), f32),
            pltpu.VMEM((2, 1, S), f32),
            pltpu.VMEM((2, 1, S), f32),
            pltpu.VMEM((18, CH, 128), bf16),
            pltpu.VMEM((18, CH, 128), bf16),
            pltpu.VMEM((18, CH, 128), bf16),
            pltpu.VMEM((18, CH, 128), bf16),
            pltpu.VMEM((2, 5, CH, 128), bf16),
            pltpu.VMEM((2, 5, CH, 128), bf16),
            pltpu.VMEM((4, 3, CH, 128), bf16),
            pltpu.VMEM((4, 3, CH, 128), bf16),
            pltpu.VMEM((4, 10, CH, 128), bf16),
            pltpu.VMEM((4, 10, CH, 128), bf16),
            pltpu.VMEM((CZ, 144, CY * X), bf16),
            pltpu.VMEM((4, 10, 48, 128), bf16),
            pltpu.VMEM((128, LO), bf16),
            pltpu.VMEM((16, CH, 128), f32),
            pltpu.VMEM((48, 144), bf16),
            pltpu.VMEM((10, CH, 128), f32),
            pltpu.VMEM((48, CY * X), f32),
            pltpu.VMEM((CH, 128), bf16),
            pltpu.VMEM((31, CH, 128), bf16),
            pltpu.VMEM((CH, 128), bf16),
            pltpu.VMEM((7, CH, 128), bf16),
            dma((6,)),
            dma((10,)),
            dma((10,)),
            dma((8,)),
            dma((8,)),
            dma((2,)),
            dma((2,)),
        ],
        compiler_params=pltpu.CompilerParams(
            vmem_limit_bytes=30 << 20,
            **(dict(collective_id=0, has_side_effects=True) if comm else {}),
        ),
    )(feats, cot, cells, slots, count, weight)
    return pl.pallas_call(
        copy_kernel,
        out_shape=[
            shape((CH, slots_all), bf16),
            shape((CH, slots_all), bf16),
            shape((27, GRP, CH), f32),
        ],
        in_specs=[vmem] * 3,
        out_specs=[hbm] * 3,
        scratch_shapes=[dma((3,))],
    )(*(pltpu.with_memory_space_constraint(v, pltpu.VMEM) for v in parts))


def local(point_feats, cell_index, send_slots, send_count, conv_weight, point_cot):
    cells = cell_index.reshape(-1, 128)
    weight = conv_weight.transpose(2, 3, 4, 1, 0).reshape(27, GRP, CH)
    out, grad, wgrad = fused(point_feats, point_cot, cells, send_slots, send_count, weight)
    return out, grad, wgrad.reshape(3, 3, 3, GRP, CH).transpose(4, 3, 0, 1, 2)


def solution(mesh):
    placed = (
        P(None, ("gz", "gy")),
        P(("gz", "gy")),
        P(("gz", "gy"), None, None),
        P(("gz", "gy"), None),
        P(),
        P(None, ("gz", "gy")),
    )
    return jax.shard_map(
        local,
        mesh=mesh,
        in_specs=placed,
        out_specs=(P(None, ("gz", "gy")), P(None, ("gz", "gy")), P()),
        check_vma=False,
    )
```

```python
import functools
import math

import jax
import jax.numpy as jnp
from jax import lax
from jax.experimental import pallas as pl
from jax.experimental.pallas import tpu as pltpu
from jax.sharding import PartitionSpec as P

CH = 16
GRP = 4
X = 128
CY = 8
CZ = 2
S = 1792
OWN = 8
ALL = OWN + 2
LO = 256
MESH = pl.DeviceIdType.MESH
f32 = jnp.float32
bf16 = jnp.bfloat16
NT = (((1,), (1,)), ((), ()))

UP_MSG = tuple(range(4, 12))
DOWN_MSG = (0, 1, 2, 3, 12, 13, 14, 15)
STAY = (0, 1, 2, 3, 8, 9, 10, 11)


def one_hot(row, count):
    ids = lax.broadcasted_iota(jnp.int32, (count, row.shape[1]), 0).astype(f32).astype(bf16)
    return jnp.where(ids == row, jnp.ones((), bf16), jnp.zeros((), bf16))


def masked_rows(row, values, codes):
    zero = jnp.zeros((), bf16)
    return [jnp.where(row == jnp.full((), code, bf16), values, zero) for code in codes]


def sigmoid(v):
    return 1.0 / (1.0 + jnp.exp(-v))


def select(found, row):
    value = jnp.zeros((CH, S), f32)
    for i, number in enumerate(STAY):
        value = jnp.where(row == float(number), found[16 * i : 16 * i + 16], value)
    return value.astype(bf16)


def kernel(
    feats_hbm, cot_hbm, cells_hbm, slots_hbm, count_hbm, weight_hbm,
    out_buf, grad_buf, wgrad_ref,
    onehots, codes, table, feats, cot, cells_ref, slots_ref, count_ref, weight_ref, lows, acc, acc_cot,
    list_send, list_recv,
    up_send, down_send, up_recv, down_recv,
    side_send, side_recv, corner_send, corner_recv,
    grid, gpad, patches, gp3, act, divisors, wmat, counts_in, pre,
    part, gather_1, plane_sum, gather_2,
    load_sem, send_sem, recv_sem, send_2, recv_2, red_send, red_recv,
    *, comm,
):
    a = lax.axis_index("gz")
    b = lax.axis_index("gy")
    n_a = lax.axis_size("gz")
    n_b = lax.axis_size("gy")
    z_p = a // 8
    y_p = lax.rem(a // 2, 4)
    x_p = lax.rem(a, 2)

    loads = [
        pltpu.make_async_copy(src, dst, load_sem.at[i])
        for i, (src, dst) in enumerate(
            (
                (cells_hbm, cells_ref), (slots_hbm, slots_ref), (count_hbm, count_ref),
                (feats_hbm, feats), (weight_hbm, weight_ref), (cot_hbm, cot),
            )
        )
    ]
    for load in loads:
        load.start()
    load_cells, load_slots, load_count, load_feats, load_weight, load_cot = loads

    a_near = {-1: lax.rem(a + n_a - 1, n_a), 0: a, 1: lax.rem(a + 1, n_a)}
    b_all = [b] + [lax.rem(b + k, n_b) for k in range(1, 4)]
    plane_all = [
        lax.rem(y_p + k // 2, 4) * 2 + (1 - x_p if k % 2 else x_p) for k in range(8)
    ]
    peers_1 = [(z_p * 8 + plane_all[d // 4], b_all[d % 4]) for d in range(1, 32)]
    peers_2 = [(lax.rem(z_p + k, 8) * 8 + plane_all[0], b) for k in range(1, 8)]

    def near(da, db):
        return (a_near[da], b_all[db % 4])

    around = [(da, db) for da in (-1, 0, 1) for db in (-1, 0, 1) if (da, db) != (0, 0)]
    if comm:
        barrier = pltpu.get_barrier_semaphore()
        for place in [near(da, db) for da, db in around] + peers_1 + peers_2:
            pl.semaphore_signal(barrier, inc=1, device_id=place, device_id_type=MESH)

    tap_row = lax.broadcasted_iota(jnp.int32, (144, 128), 0)
    tap_col = lax.broadcasted_iota(jnp.int32, (144, 128), 1)
    tap_base = jnp.bitwise_and(tap_row, 3) + jnp.right_shift(tap_row, 4) * (3 * GRP)
    spread = [tap_base + GRP * col_k == tap_col for col_k in range(3)]
    out_ch = lax.broadcasted_iota(jnp.int32, (CH, 144), 0)
    in_ch = jnp.bitwise_and(lax.broadcasted_iota(jnp.int32, (CH, 144), 1), 15)
    same_group = jnp.right_shift(out_ch, 2) == jnp.right_shift(in_ch, 2)
    load_cells.wait()
    load_slots.wait()
    load_count.wait()
    cells = jnp.concatenate(
        [cells_ref[pl.ds(0, 56, stride=2), :], cells_ref[pl.ds(1, 56, stride=2), :]], axis=1
    )
    cell_y = jnp.right_shift(jnp.bitwise_and(cells, 1023), 7) * 128
    cell_x = jnp.bitwise_and(cells, 127)
    pad = jnp.zeros((8, LO), f32)
    cell_table = jnp.concatenate(
        [cell_y.astype(f32), pad, cell_x.astype(f32), pad], axis=0
    ).astype(bf16)
    lane = lax.broadcasted_iota(jnp.int32, (1, S), 1)
    leaving = jnp.zeros((64, LO), f32)
    for side in range(2):
        listed = lane < count_ref[:, side : side + 1]
        slot = slots_ref[0, side : side + 1, :]
        slot_hi = jnp.where(listed, jnp.right_shift(slot, 8), -1)
        hot_lo = one_hot(jnp.bitwise_and(slot, 255).astype(f32).astype(bf16), LO)
        hot_hi = lax.broadcasted_iota(jnp.int32, (64, S), 0) == slot_hi
        leaving += lax.dot_general(
            hot_hi.astype(f32).astype(bf16), hot_lo, NT, preferred_element_type=f32
        )
        found = jnp.dot(cell_table, hot_lo, preferred_element_type=f32)
        place = jnp.sum(jnp.where(hot_hi, found[:64] + found[64:], 0.0), axis=0, keepdims=True)
        list_send[side] = jnp.where(listed, place, -1.0)
    code = (
        jnp.bitwise_and(jnp.right_shift(cells, 8), 3) + jnp.right_shift(cells, 10) * 8
    ).astype(f32) + 4.0 * leaving[:56]
    low = jnp.bitwise_and(cells, 255).astype(f32)
    for row in range(7 * OWN):
        k, j = divmod(row, 7)
        codes[k, :, LO * j : LO * (j + 1)] = code[row : row + 1]
        lows[k, :, LO * j : LO * (j + 1)] = low[row : row + 1]

    load_feats.wait()
    acc[...] = jnp.zeros_like(acc)

    def splat_own(k, carry):
        hot = one_hot(lows[k].astype(bf16), LO)
        onehots[k] = hot
        row = codes[k].astype(bf16)
        values = feats[:, pl.ds(pl.multiple_of(k * S, 128), S)]
        rows = masked_rows(row, values, range(16)) + [one_hot(row, 16)]
        acc[...] += lax.dot_general(
            jnp.concatenate(rows, axis=0), hot, NT, preferred_element_type=f32
        )
        return carry

    lax.fori_loop(0, OWN, splat_own, 0, unroll=4)

    counts = acc[256:272, :]
    count_hi = jnp.floor(counts * (1.0 / 256.0))
    count_lo = counts - 256.0 * count_hi

    def block(number, row):
        lanes = slice(128 * (row % 2), 128 * (row % 2) + 128)
        return acc[16 * number : 16 * number + 16, lanes].astype(bf16)

    def rows_of(numbers, first_row):
        return [block(4 * plane + first_row // 2, first_row) for plane in numbers]

    for ref, members in ((up_send, UP_MSG), (down_send, DOWN_MSG)):
        for i, number in enumerate(members):
            ref[2 * i] = block(number, 0)
            ref[2 * i + 1] = block(number, 1)
        both = jnp.concatenate(
            [part_of[c : c + 4] for part_of in (count_lo, count_hi) for c in members[::4]], axis=0
        ).astype(bf16)
        ref[16] = both[:, :128]
        ref[17] = both[:, 128:]
    nothing = jnp.zeros((8, 128), f32)
    for side in range(2):
        lanes = slice(128 * side, 128 * side + 128)
        rows = [
            part_of[4 * plane + 3 * side : 4 * plane + 3 * side + 1, lanes]
            for part_of in (count_lo, count_hi)
            for plane in range(4)
        ]
        tile = jnp.concatenate(rows + [nothing], axis=0).astype(bf16)
        for plane in range(4):
            side_send[side, plane] = block(4 * plane + 3 * side, side)
        side_send[side, 4] = tile
        for vertical, planes in ((0, (0, 3)), (1, (1, 2))):
            for i, plane in enumerate(planes):
                corner_send[2 * vertical + side, i] = block(4 * plane + 3 * side, side)
            corner_send[2 * vertical + side, 2] = tile

    def inside(da, db):
        tests = []
        if da:
            tests.append(a < n_a - 1 if da > 0 else a > 0)
        if db:
            tests.append(b < n_b - 1 if db > 0 else b > 0)
        return tests[0] if len(tests) == 1 else jnp.logical_and(*tests)

    def send(src, dst, sems, place, da, db):
        if not comm:
            return lambda: None
        copy = pltpu.make_async_remote_copy(
            src_ref=src, dst_ref=dst, send_sem=sems[0].at[place],
            recv_sem=sems[1].at[place], device_id=near(da, db), device_id_type=MESH,
        )

        @pl.when(inside(da, db))
        def _():
            copy.start()

        def finish():
            @pl.when(inside(da, db))
            def _():
                copy.wait_send()

            @pl.when(inside(-da, -db))
            def _():
                copy.wait_recv()

        return finish

    if comm:
        pl.semaphore_wait(barrier, len(around) + len(peers_1) + len(peers_2))
    first = (send_sem, recv_sem)
    finish_lists = [
        send(list_send.at[0], list_recv.at[1], first, 0, -1, 0),
        send(list_send.at[1], list_recv.at[0], first, 1, 1, 0),
    ]
    finish_grid = [
        send(up_send, up_recv, first, 2, 1, 0),
        send(down_send, down_recv, first, 3, -1, 0),
    ]
    for side in range(2):
        db = 2 * side - 1
        finish_grid.append(send(side_send.at[side], side_recv.at[side], first, 4 + side, 0, db))
        for vertical in range(2):
            i = 2 * vertical + side
            finish_grid.append(
                send(corner_send.at[i], corner_recv.at[i], first, 6 + i, 2 * vertical - 1, db)
            )

    load_weight.wait()
    weight = jnp.concatenate(
        [weight_ref[i].astype(f32) for i in range(27)] + [jnp.zeros((20, CH), f32)], axis=0
    ).T.astype(bf16)
    for col_k in range(3):
        picked = lax.dot_general(
            weight, spread[col_k].astype(bf16), NT, preferred_element_type=f32
        )
        wmat[16 * col_k : 16 * col_k + 16, :] = jnp.where(same_group, picked, 0.0).astype(bf16)

    load_cot.wait()
    acc_cot[...] = jnp.zeros_like(acc_cot)

    def splat_cot(k, carry):
        row = codes[k].astype(bf16)
        values = cot[:, pl.ds(pl.multiple_of(k * S, 128), S)]
        acc_cot[...] += lax.dot_general(
            jnp.concatenate(masked_rows(row, values, STAY), axis=0), onehots[k], NT,
            preferred_element_type=f32,
        )
        return carry

    lax.fori_loop(0, OWN, splat_cot, 0, unroll=4)

    for finish in finish_lists:
        finish()
    for side in range(2):
        present = (a > 0) if side == 0 else (a < n_a - 1)
        place = jnp.where(present, list_recv[side], -1.0).astype(jnp.int32)
        live = place >= 0
        row = jnp.where(live, jnp.right_shift(place, 8) + 8 * side, 16).astype(f32)
        codes[OWN + side] = row
        hot = one_hot(jnp.bitwise_and(place, 255).astype(f32).astype(bf16), LO)
        onehots[OWN + side] = hot
        values = cot[:, (OWN + side) * S : (OWN + side + 1) * S]
        members = STAY[4 * side : 4 * side + 4]
        acc_cot[64 * side : 64 * side + 64, :] += lax.dot_general(
            jnp.concatenate(masked_rows(row.astype(bf16), values, members), axis=0), hot, NT,
            preferred_element_type=f32,
        )

    for finish in finish_grid:
        finish()
    has_below = a > 0
    has_above = a < n_a - 1
    has_left = b > 0
    has_right = b < n_b - 1

    for i, (ref, flag) in enumerate(((up_recv, has_below), (down_recv, has_above))):
        for half in range(2):
            both = ref[16 + half].astype(f32)
            counts_in[2 * i + half, 0:8] = jnp.where(flag, both[0:8] + 256.0 * both[8:16], 0.0)
    side_flag = (has_right, has_left)
    for side in range(2):
        for i, (ref, at) in enumerate(
            ((side_recv.at[side], 4), (corner_recv.at[side], 2), (corner_recv.at[2 + side], 2))
        ):
            flag = side_flag[side]
            if i == 1:
                flag = jnp.logical_and(flag, has_above)
            if i == 2:
                flag = jnp.logical_and(flag, has_below)
            both = ref[at].astype(f32)
            counts_in[4 + 2 * i + side, 0:4] = jnp.where(flag, both[0:4] + 256.0 * both[4:8], 0.0)

    def mean(sums, count):
        return sums / jnp.maximum(count, 1.0)

    sources = (
        (3, up_recv, 4, 0, has_below),
        (0, up_recv, 0, 0, has_below),
        (2, down_recv, 4, 2, has_above),
        (1, down_recv, 0, 2, has_above),
    )
    for plane, (mine, ref, at, where, flag) in enumerate(sources):
        for row in range(8):
            half = row % 2
            lanes = slice(128 * half, 128 * half + 128)
            number = 4 * mine + row // 2
            other = at + row // 2
            got = ref[2 * (at + row // 2) + half].astype(f32)
            sums = acc[16 * number : 16 * number + 16, lanes] + jnp.where(flag, got, 0.0)
            count = acc[256 + number : 257 + number, lanes]
            count = count + counts_in[where + half, other : other + 1, :]
            divisor = jnp.broadcast_to(jnp.maximum(count, 1.0), (CH, 128))
            grid[plane, 1 + row] = (sums / divisor).astype(bf16)
            if plane in (1, 2):
                divisors[8 * (plane - 1) + row] = divisor
    for side in range(2):
        flag = side_flag[side]
        halo = (
            (3, 1, 1, 2, has_below),
            (0, 1, 0, 1, has_below),
            (2, 0, 1, 3, has_above),
            (1, 0, 0, 0, has_above),
        )
        for plane, (direct, vertical, at, theirs, vertical_flag) in enumerate(halo):
            corner = 2 * vertical + side
            both = jnp.logical_and(flag, vertical_flag)
            sums = jnp.where(flag, side_recv[side, direct].astype(f32), 0.0)
            sums = sums + jnp.where(both, corner_recv[corner, at].astype(f32), 0.0)
            kind = 6 if vertical == 0 else 8
            count = counts_in[4 + side, direct : direct + 1, :]
            count = count + counts_in[kind + side, theirs : theirs + 1, :]
            grid[plane, 9 * (1 - side)] = mean(sums, count).astype(bf16)

    lane = lax.broadcasted_iota(jnp.int32, (CH, X), 1)
    first_x = lane == 0
    last_x = lane == X - 1
    for z in range(CZ):
        stacked = jnp.concatenate(
            [
                jnp.concatenate([grid[z + u, v + y] for y in range(CY)], axis=1)
                for u in range(3)
                for v in range(3)
            ],
            axis=0,
        )
        patches[z] = stacked
        pre[...] = jnp.dot(wmat[...], stacked, preferred_element_type=f32)
        for y in range(CY):
            lanes = slice(128 * y, 128 * y + 128)
            low_x = pltpu.roll(pre[0:16, lanes], 1, 1)
            high_x = pltpu.roll(pre[32:48, lanes], X - 1, 1)
            value = (
                pre[16:32, lanes]
                + jnp.where(first_x, 0.0, low_x)
                + jnp.where(last_x, 0.0, high_x)
            )
            sigma = sigmoid(value)
            group = 4 * z + y // 2
            half = slice(128 * (y % 2), 128 * (y % 2) + 128)
            act[16 * group : 16 * group + 16, half] = (value * sigma).astype(bf16)
            cot_sum = acc_cot[16 * group : 16 * group + 16, half]
            gpad[z + 1, y + 1] = (cot_sum * sigma * (1.0 + value * (1.0 - sigma))).astype(bf16)

    def move(plane, row):
        value = gpad[plane, row]
        wide = value.astype(f32)
        gp3[plane, row, 0:16] = jnp.where(last_x, 0.0, pltpu.roll(wide, X - 1, 1)).astype(bf16)
        gp3[plane, row, 16:32] = value
        gp3[plane, row, 32:48] = jnp.where(first_x, 0.0, pltpu.roll(wide, 1, 1)).astype(bf16)

    wide_grad = jnp.zeros((48, 144), f32)
    for z in range(CZ):
        for y in range(CY):
            move(z + 1, y + 1)
        moved = jnp.concatenate([gp3[z + 1, y + 1] for y in range(CY)], axis=1)
        wide_grad += lax.dot_general(moved, patches[z], NT, preferred_element_type=f32)
    compact = jnp.zeros((CH, 128), f32)
    for col_k in range(3):
        kept = jnp.where(same_group, wide_grad[16 * col_k : 16 * col_k + 16], 0.0)
        compact += jnp.dot(
            kept.astype(bf16), spread[col_k].astype(bf16), preferred_element_type=f32
        )
    part[...] = compact.astype(bf16)

    def reduce_send(step, peers, source, target):
        if comm:
            for d, place in enumerate(peers):
                pltpu.make_async_remote_copy(
                    src_ref=source, dst_ref=target.at[d], send_sem=red_send.at[step],
                    recv_sem=red_recv.at[step], device_id=place, device_id_type=MESH,
                ).start()

    def reduce_wait(step, buffer):
        if comm:
            pltpu.make_async_copy(buffer, buffer, red_send.at[step]).wait()
            pltpu.make_async_copy(buffer, buffer, red_recv.at[step]).wait()

    reduce_send(0, peers_1, part, gather_1)
    second = (send_2, recv_2)
    finish_halo = []

    def send_2nd(src, dst, place, da, db):
        finish_halo.append(send(src, dst, second, place, da, db))

    send_2nd(gpad.at[1, pl.ds(1, 8)], gpad.at[3, pl.ds(1, 8)], 0, -1, 0)
    send_2nd(gpad.at[2, pl.ds(1, 8)], gpad.at[0, pl.ds(1, 8)], 1, 1, 0)
    send_2nd(gpad.at[pl.ds(1, 2), 1], gpad.at[pl.ds(1, 2), 9], 2, 0, -1)
    send_2nd(gpad.at[pl.ds(1, 2), 8], gpad.at[pl.ds(1, 2), 0], 3, 0, 1)
    send_2nd(gpad.at[1, 1], gpad.at[3, 9], 4, -1, -1)
    send_2nd(gpad.at[1, 8], gpad.at[3, 0], 5, -1, 1)
    send_2nd(gpad.at[2, 1], gpad.at[0, 9], 6, 1, -1)
    send_2nd(gpad.at[2, 8], gpad.at[0, 0], 7, 1, 1)


    def read_back(values, into):
        def body(k, carry):
            found = jnp.dot(values[...], onehots[k], preferred_element_type=f32)
            into[:, pl.ds(pl.multiple_of(k * S, 128), S)] = select(found, codes[k])
            return carry

        lax.fori_loop(0, ALL, body, 0, unroll=5)

    read_back(act, out_buf)

    reduce_wait(0, gather_1)
    total = compact
    for d in range(31):
        total = total + gather_1[d].astype(f32)
    plane_sum[...] = total.astype(bf16)
    reduce_send(1, peers_2, plane_sum, gather_2)

    for finish in finish_halo:
        finish()
    blank = jnp.zeros((CH, X), bf16)

    def clear(flag, places):
        @pl.when(flag)
        def _():
            for plane, row in places:
                gpad[plane, row] = blank

    clear(a == 0, [(0, row) for row in range(10)])
    clear(a == n_a - 1, [(3, row) for row in range(10)])
    clear(b == 0, [(plane, 0) for plane in range(4)])
    clear(b == n_b - 1, [(plane, 9) for plane in range(4)])
    for plane in range(4):
        for row in range(10):
            if plane in (0, 3) or row in (0, 9):
                move(plane, row)
    result = [None] * 16
    for plane in range(4):
        moved = jnp.concatenate([gp3[plane, row] for row in range(10)], axis=1)
        taps = lax.dot_general(
            wmat[...], moved, (((0,), (0,)), ((), ())), preferred_element_type=f32
        )
        for u in range(3):
            z = plane - 2 + u
            if z not in (0, 1):
                continue
            for v in range(3):
                rows = slice(16 * (3 * u + v), 16 * (3 * u + v) + 16)
                for y in range(CY):
                    source = y + 2 - v
                    term = taps[rows, 128 * source : 128 * source + 128]
                    i = 8 * z + y
                    result[i] = term if result[i] is None else result[i] + term
    for i in range(16):
        group = i // 2
        half = slice(128 * (i % 2), 128 * (i % 2) + 128)
        table[16 * group : 16 * group + 16, half] = (result[i] / divisors[i]).astype(bf16)
    read_back(table, grad_buf)

    reduce_wait(1, gather_2)
    for d in range(7):
        total = total + gather_2[d].astype(f32)
    wgrad_ref[...] = total * (1.0 / math.sqrt(CZ * CY * X * n_a * n_b))


def copy_kernel(out, grad, total, out_hbm, grad_hbm, wgrad_hbm, wgrad, sem):
    copies = [
        pltpu.make_async_copy(src, dst, sem.at[i])
        for i, (src, dst) in enumerate(((out, out_hbm), (grad, grad_hbm), (wgrad, wgrad_hbm)))
    ]
    copies[0].start()
    copies[1].start()
    turned = total[...].T
    for i in range(27):
        wgrad[i] = turned[GRP * i : GRP * i + GRP]
    copies[2].start()
    for copy in copies:
        copy.wait()


def fused(feats, cot, cells, slots, count, weight, comm=True):
    hbm = pl.BlockSpec(memory_space=pltpu.HBM)
    vmem = pl.BlockSpec(memory_space=pltpu.VMEM)
    slots_all = ALL * S
    dma = pltpu.SemaphoreType.DMA
    shape = jax.ShapeDtypeStruct
    feats, cot, cells, slots, count, weight = (
        pltpu.with_memory_space_constraint(v, pltpu.HBM)
        for v in (feats, cot, cells, slots, count, weight)
    )
    parts = pl.pallas_call(
        functools.partial(kernel, comm=comm),
        out_shape=[
            shape((CH, slots_all), bf16),
            shape((CH, slots_all), bf16),
            shape((CH, 128), f32),
        ],
        in_specs=[hbm] * 6,
        out_specs=[vmem] * 3,
        scratch_shapes=[
            pltpu.VMEM((ALL, LO, S), bf16),
            pltpu.VMEM((ALL, 1, S), f32),
            pltpu.VMEM((128, LO), bf16),
            pltpu.VMEM((CH, OWN * S), bf16),
            pltpu.VMEM((CH, slots_all), bf16),
            pltpu.VMEM((112, 128), jnp.int32),
            pltpu.VMEM((1, 2, S), jnp.int32),
            pltpu.VMEM((1, 2), jnp.int32),
            pltpu.VMEM((27, GRP, CH), bf16),
            pltpu.VMEM((OWN, 1, S), f32),
            pltpu.VMEM((272, LO), f32),
            pltpu.VMEM((128, LO), f32),
            pltpu.VMEM((2, 1, S), f32),
            pltpu.VMEM((2, 1, S), f32),
            pltpu.VMEM((18, CH, 128), bf16),
            pltpu.VMEM((18, CH, 128), bf16),
            pltpu.VMEM((18, CH, 128), bf16),
            pltpu.VMEM((18, CH, 128), bf16),
            pltpu.VMEM((2, 5, CH, 128), bf16),
            pltpu.VMEM((2, 5, CH, 128), bf16),
            pltpu.VMEM((4, 3, CH, 128), bf16),
            pltpu.VMEM((4, 3, CH, 128), bf16),
            pltpu.VMEM((4, 10, CH, 128), bf16),
            pltpu.VMEM((4, 10, CH, 128), bf16),
            pltpu.VMEM((CZ, 144, CY * X), bf16),
            pltpu.VMEM((4, 10, 48, 128), bf16),
            pltpu.VMEM((128, LO), bf16),
            pltpu.VMEM((16, CH, 128), f32),
            pltpu.VMEM((48, 144), bf16),
            pltpu.VMEM((10, CH, 128), f32),
            pltpu.VMEM((48, CY * X), f32),
            pltpu.VMEM((CH, 128), bf16),
            pltpu.VMEM((31, CH, 128), bf16),
            pltpu.VMEM((CH, 128), bf16),
            pltpu.VMEM((7, CH, 128), bf16),
            dma((6,)),
            dma((10,)),
            dma((10,)),
            dma((8,)),
            dma((8,)),
            dma((2,)),
            dma((2,)),
        ],
        compiler_params=pltpu.CompilerParams(
            vmem_limit_bytes=30 << 20,
            **(dict(collective_id=0, has_side_effects=True) if comm else {}),
        ),
    )(feats, cot, cells, slots, count, weight)
    return pl.pallas_call(
        copy_kernel,
        out_shape=[
            shape((CH, slots_all), bf16),
            shape((CH, slots_all), bf16),
            shape((27, GRP, CH), f32),
        ],
        in_specs=[vmem] * 3,
        out_specs=[hbm] * 3,
        scratch_shapes=[pltpu.VMEM((27, GRP, CH), f32), dma((3,))],
    )(*(pltpu.with_memory_space_constraint(v, pltpu.VMEM) for v in parts))


def local(point_feats, cell_index, send_slots, send_count, conv_weight, point_cot):
    cells = cell_index.reshape(-1, 128)
    weight = conv_weight.transpose(2, 3, 4, 1, 0).reshape(27, GRP, CH)
    out, grad, wgrad = fused(point_feats, point_cot, cells, send_slots, send_count, weight)
    return out, grad, wgrad.reshape(3, 3, 3, GRP, CH).transpose(4, 3, 0, 1, 2)


def solution(mesh):
    placed = (
        P(None, ("gz", "gy")),
        P(("gz", "gy")),
        P(("gz", "gy"), None, None),
        P(("gz", "gy"), None),
        P(),
        P(None, ("gz", "gy")),
    )
    return jax.shard_map(
        local,
        mesh=mesh,
        in_specs=placed,
        out_specs=(P(None, ("gz", "gy")), P(None, ("gz", "gy")), P()),
        check_vma=False,
    )
```

```python
import functools
import math

import jax
import jax.numpy as jnp
from jax import lax
from jax.experimental import pallas as pl
from jax.experimental.pallas import tpu as pltpu
from jax.sharding import PartitionSpec as P

CH = 16
GRP = 4
X = 128
CY = 8
CZ = 2
S = 1792
OWN = 8
ALL = OWN + 2
LO = 256
MESH = pl.DeviceIdType.MESH
f32 = jnp.float32
bf16 = jnp.bfloat16
NT = (((1,), (1,)), ((), ()))

UP_MSG = tuple(range(4, 12))
DOWN_MSG = (0, 1, 2, 3, 12, 13, 14, 15)
STAY = (0, 1, 2, 3, 8, 9, 10, 11)


def links(d):
    step_y, step_x, step_b = (0, 1, 2, 1)[d // 8], d // 4 % 2, d % 4
    return step_y + (2 - step_x if step_b == 2 else max(step_x, step_b % 2))


FAR_FIRST = sorted(range(1, 32), key=links, reverse=True)


def one_hot(row, count):
    ids = lax.broadcasted_iota(jnp.int32, (count, row.shape[1]), 0).astype(f32).astype(bf16)
    return jnp.where(ids == row, jnp.ones((), bf16), jnp.zeros((), bf16))


def masked_rows(row, values, codes):
    zero = jnp.zeros((), bf16)
    return [jnp.where(row == jnp.full((), code, bf16), values, zero) for code in codes]


def sigmoid(v):
    return 1.0 / (1.0 + jnp.exp(-v))


def select(found, row):
    value = jnp.zeros((CH, S), f32)
    for i, number in enumerate(STAY):
        value = jnp.where(row == float(number), found[16 * i : 16 * i + 16], value)
    return value.astype(bf16)


def kernel(
    feats_hbm, cot_hbm, cells_hbm, slots_hbm, count_hbm, weight_hbm,
    out_buf, grad_buf, wgrad_ref,
    onehots, codes, table, feats, cot, cells_ref, slots_ref, count_ref, weight_ref, lows, acc, acc_cot,
    list_send, list_recv,
    up_send, down_send, up_recv, down_recv,
    side_send, side_recv, corner_send, corner_recv,
    grid, gpad, patches, gp3, act, divisors, wmat, counts_in, pre,
    part, gather_1, plane_sum, gather_2,
    load_sem, send_sem, recv_sem, send_2, recv_2, red_send, red_recv,
    *, comm,
):
    a = lax.axis_index("gz")
    b = lax.axis_index("gy")
    n_a = lax.axis_size("gz")
    n_b = lax.axis_size("gy")
    z_p = a // 8
    y_p = lax.rem(a // 2, 4)
    x_p = lax.rem(a, 2)

    loads = [
        pltpu.make_async_copy(src, dst, load_sem.at[i])
        for i, (src, dst) in enumerate(
            (
                (cells_hbm, cells_ref), (slots_hbm, slots_ref), (count_hbm, count_ref),
                (feats_hbm, feats), (weight_hbm, weight_ref), (cot_hbm, cot),
            )
        )
    ]
    for load in loads:
        load.start()
    load_cells, load_slots, load_count, load_feats, load_weight, load_cot = loads

    a_near = {-1: lax.rem(a + n_a - 1, n_a), 0: a, 1: lax.rem(a + 1, n_a)}
    b_all = [b] + [lax.rem(b + k, n_b) for k in range(1, 4)]
    plane_all = [
        lax.rem(y_p + k // 2, 4) * 2 + (1 - x_p if k % 2 else x_p) for k in range(8)
    ]
    peers_1 = [(z_p * 8 + plane_all[d // 4], b_all[d % 4]) for d in FAR_FIRST]
    peers_2 = [(lax.rem(z_p + k, 8) * 8 + plane_all[0], b) for k in (4, 3, 5, 2, 6, 1, 7)]

    def near(da, db):
        return (a_near[da], b_all[db % 4])

    around = [(da, db) for da in (-1, 0, 1) for db in (-1, 0, 1) if (da, db) != (0, 0)]
    if comm:
        barrier = pltpu.get_barrier_semaphore()
        for place in [near(da, db) for da, db in around] + peers_1 + peers_2:
            pl.semaphore_signal(barrier, inc=1, device_id=place, device_id_type=MESH)

    tap_row = lax.broadcasted_iota(jnp.int32, (144, 128), 0)
    tap_col = lax.broadcasted_iota(jnp.int32, (144, 128), 1)
    tap_base = jnp.bitwise_and(tap_row, 3) + jnp.right_shift(tap_row, 4) * (3 * GRP)
    spread = [tap_base + GRP * col_k == tap_col for col_k in range(3)]
    out_ch = lax.broadcasted_iota(jnp.int32, (CH, 144), 0)
    in_ch = jnp.bitwise_and(lax.broadcasted_iota(jnp.int32, (CH, 144), 1), 15)
    same_group = jnp.right_shift(out_ch, 2) == jnp.right_shift(in_ch, 2)
    load_cells.wait()
    load_slots.wait()
    load_count.wait()
    cells = jnp.concatenate(
        [cells_ref[pl.ds(0, 56, stride=2), :], cells_ref[pl.ds(1, 56, stride=2), :]], axis=1
    )
    cell_y = jnp.right_shift(jnp.bitwise_and(cells, 1023), 7) * 128
    cell_x = jnp.bitwise_and(cells, 127)
    pad = jnp.zeros((8, LO), f32)
    cell_table = jnp.concatenate(
        [cell_y.astype(f32), pad, cell_x.astype(f32), pad], axis=0
    ).astype(bf16)
    lane = lax.broadcasted_iota(jnp.int32, (1, S), 1)
    leaving = jnp.zeros((64, LO), f32)
    for side in range(2):
        listed = lane < count_ref[:, side : side + 1]
        slot = slots_ref[0, side : side + 1, :]
        slot_hi = jnp.where(listed, jnp.right_shift(slot, 8), -1)
        hot_lo = one_hot(jnp.bitwise_and(slot, 255).astype(f32).astype(bf16), LO)
        hot_hi = lax.broadcasted_iota(jnp.int32, (64, S), 0) == slot_hi
        leaving += lax.dot_general(
            hot_hi.astype(f32).astype(bf16), hot_lo, NT, preferred_element_type=f32
        )
        found = jnp.dot(cell_table, hot_lo, preferred_element_type=f32)
        place = jnp.sum(jnp.where(hot_hi, found[:64] + found[64:], 0.0), axis=0, keepdims=True)
        list_send[side] = jnp.where(listed, place, -1.0)
    code = (
        jnp.bitwise_and(jnp.right_shift(cells, 8), 3) + jnp.right_shift(cells, 10) * 8
    ).astype(f32) + 4.0 * leaving[:56]
    low = jnp.bitwise_and(cells, 255).astype(f32)
    for row in range(7 * OWN):
        k, j = divmod(row, 7)
        codes[k, :, LO * j : LO * (j + 1)] = code[row : row + 1]
        lows[k, :, LO * j : LO * (j + 1)] = low[row : row + 1]

    load_feats.wait()
    acc[...] = jnp.zeros_like(acc)

    def splat_own(k, carry):
        hot = one_hot(lows[k].astype(bf16), LO)
        onehots[k] = hot
        row = codes[k].astype(bf16)
        values = feats[:, pl.ds(pl.multiple_of(k * S, 128), S)]
        rows = masked_rows(row, values, range(16)) + [one_hot(row, 16)]
        acc[...] += lax.dot_general(
            jnp.concatenate(rows, axis=0), hot, NT, preferred_element_type=f32
        )
        return carry

    lax.fori_loop(0, OWN, splat_own, 0, unroll=4)

    counts = acc[256:272, :]
    count_hi = jnp.floor(counts * (1.0 / 256.0))
    count_lo = counts - 256.0 * count_hi

    def block(number, row):
        lanes = slice(128 * (row % 2), 128 * (row % 2) + 128)
        return acc[16 * number : 16 * number + 16, lanes].astype(bf16)

    def rows_of(numbers, first_row):
        return [block(4 * plane + first_row // 2, first_row) for plane in numbers]

    for ref, members in ((up_send, UP_MSG), (down_send, DOWN_MSG)):
        for i, number in enumerate(members):
            ref[2 * i] = block(number, 0)
            ref[2 * i + 1] = block(number, 1)
        both = jnp.concatenate(
            [part_of[c : c + 4] for part_of in (count_lo, count_hi) for c in members[::4]], axis=0
        ).astype(bf16)
        ref[16] = both[:, :128]
        ref[17] = both[:, 128:]
    nothing = jnp.zeros((8, 128), f32)
    for side in range(2):
        lanes = slice(128 * side, 128 * side + 128)
        rows = [
            part_of[4 * plane + 3 * side : 4 * plane + 3 * side + 1, lanes]
            for part_of in (count_lo, count_hi)
            for plane in range(4)
        ]
        tile = jnp.concatenate(rows + [nothing], axis=0).astype(bf16)
        for plane in range(4):
            side_send[side, plane] = block(4 * plane + 3 * side, side)
        side_send[side, 4] = tile
        for vertical, planes in ((0, (0, 3)), (1, (1, 2))):
            for i, plane in enumerate(planes):
                corner_send[2 * vertical + side, i] = block(4 * plane + 3 * side, side)
            corner_send[2 * vertical + side, 2] = tile

    def inside(da, db):
        tests = []
        if da:
            tests.append(a < n_a - 1 if da > 0 else a > 0)
        if db:
            tests.append(b < n_b - 1 if db > 0 else b > 0)
        return tests[0] if len(tests) == 1 else jnp.logical_and(*tests)

    wait_sent = []

    def send(src, dst, sems, place, da, db):
        if not comm:
            return lambda: None
        copy = pltpu.make_async_remote_copy(
            src_ref=src, dst_ref=dst, send_sem=sems[0].at[place],
            recv_sem=sems[1].at[place], device_id=near(da, db), device_id_type=MESH,
        )

        @pl.when(inside(da, db))
        def _():
            copy.start()

        def sent():
            @pl.when(inside(da, db))
            def _():
                copy.wait_send()

        def finish():
            @pl.when(inside(-da, -db))
            def _():
                copy.wait_recv()

        wait_sent.append(sent)

        return finish

    if comm:
        pl.semaphore_wait(barrier, len(around) + len(peers_1) + len(peers_2))
    first = (send_sem, recv_sem)
    finish_lists = [
        send(list_send.at[0], list_recv.at[1], first, 0, -1, 0),
        send(list_send.at[1], list_recv.at[0], first, 1, 1, 0),
    ]
    finish_grid = [
        send(up_send, up_recv, first, 2, 1, 0),
        send(down_send, down_recv, first, 3, -1, 0),
    ]
    for side in range(2):
        db = 2 * side - 1
        finish_grid.append(send(side_send.at[side], side_recv.at[side], first, 4 + side, 0, db))
        for vertical in range(2):
            i = 2 * vertical + side
            finish_grid.append(
                send(corner_send.at[i], corner_recv.at[i], first, 6 + i, 2 * vertical - 1, db)
            )

    load_weight.wait()
    weight = jnp.concatenate(
        [weight_ref[i].astype(f32) for i in range(27)] + [jnp.zeros((20, CH), f32)], axis=0
    ).T.astype(bf16)
    for col_k in range(3):
        picked = lax.dot_general(
            weight, spread[col_k].astype(bf16), NT, preferred_element_type=f32
        )
        wmat[16 * col_k : 16 * col_k + 16, :] = jnp.where(same_group, picked, 0.0).astype(bf16)

    load_cot.wait()
    acc_cot[...] = jnp.zeros_like(acc_cot)

    def splat_cot(k, carry):
        row = codes[k].astype(bf16)
        values = cot[:, pl.ds(pl.multiple_of(k * S, 128), S)]
        acc_cot[...] += lax.dot_general(
            jnp.concatenate(masked_rows(row, values, STAY), axis=0), onehots[k], NT,
            preferred_element_type=f32,
        )
        return carry

    lax.fori_loop(0, OWN, splat_cot, 0, unroll=4)

    for finish in finish_lists:
        finish()
    for side in range(2):
        present = (a > 0) if side == 0 else (a < n_a - 1)
        place = jnp.where(present, list_recv[side], -1.0).astype(jnp.int32)
        live = place >= 0
        row = jnp.where(live, jnp.right_shift(place, 8) + 8 * side, 16).astype(f32)
        codes[OWN + side] = row
        hot = one_hot(jnp.bitwise_and(place, 255).astype(f32).astype(bf16), LO)
        onehots[OWN + side] = hot
        values = cot[:, (OWN + side) * S : (OWN + side + 1) * S]
        members = STAY[4 * side : 4 * side + 4]
        acc_cot[64 * side : 64 * side + 64, :] += lax.dot_general(
            jnp.concatenate(masked_rows(row.astype(bf16), values, members), axis=0), hot, NT,
            preferred_element_type=f32,
        )

    for finish in finish_grid:
        finish()
    has_below = a > 0
    has_above = a < n_a - 1
    has_left = b > 0
    has_right = b < n_b - 1

    for i, (ref, flag) in enumerate(((up_recv, has_below), (down_recv, has_above))):
        for half in range(2):
            both = ref[16 + half].astype(f32)
            counts_in[2 * i + half, 0:8] = jnp.where(flag, both[0:8] + 256.0 * both[8:16], 0.0)
    side_flag = (has_right, has_left)
    for side in range(2):
        for i, (ref, at) in enumerate(
            ((side_recv.at[side], 4), (corner_recv.at[side], 2), (corner_recv.at[2 + side], 2))
        ):
            flag = side_flag[side]
            if i == 1:
                flag = jnp.logical_and(flag, has_above)
            if i == 2:
                flag = jnp.logical_and(flag, has_below)
            both = ref[at].astype(f32)
            counts_in[4 + 2 * i + side, 0:4] = jnp.where(flag, both[0:4] + 256.0 * both[4:8], 0.0)

    def mean(sums, count):
        return sums / jnp.maximum(count, 1.0)

    sources = (
        (3, up_recv, 4, 0, has_below),
        (0, up_recv, 0, 0, has_below),
        (2, down_recv, 4, 2, has_above),
        (1, down_recv, 0, 2, has_above),
    )
    for plane, (mine, ref, at, where, flag) in enumerate(sources):
        for row in range(8):
            half = row % 2
            lanes = slice(128 * half, 128 * half + 128)
            number = 4 * mine + row // 2
            other = at + row // 2
            got = ref[2 * (at + row // 2) + half].astype(f32)
            sums = acc[16 * number : 16 * number + 16, lanes] + jnp.where(flag, got, 0.0)
            count = acc[256 + number : 257 + number, lanes]
            count = count + counts_in[where + half, other : other + 1, :]
            divisor = jnp.broadcast_to(jnp.maximum(count, 1.0), (CH, 128))
            grid[plane, 1 + row] = (sums / divisor).astype(bf16)
            if plane in (1, 2):
                divisors[8 * (plane - 1) + row] = divisor
    for side in range(2):
        flag = side_flag[side]
        halo = (
            (3, 1, 1, 2, has_below),
            (0, 1, 0, 1, has_below),
            (2, 0, 1, 3, has_above),
            (1, 0, 0, 0, has_above),
        )
        for plane, (direct, vertical, at, theirs, vertical_flag) in enumerate(halo):
            corner = 2 * vertical + side
            both = jnp.logical_and(flag, vertical_flag)
            sums = jnp.where(flag, side_recv[side, direct].astype(f32), 0.0)
            sums = sums + jnp.where(both, corner_recv[corner, at].astype(f32), 0.0)
            kind = 6 if vertical == 0 else 8
            count = counts_in[4 + side, direct : direct + 1, :]
            count = count + counts_in[kind + side, theirs : theirs + 1, :]
            grid[plane, 9 * (1 - side)] = mean(sums, count).astype(bf16)

    lane = lax.broadcasted_iota(jnp.int32, (CH, X), 1)
    first_x = lane == 0
    last_x = lane == X - 1
    for z in range(CZ):
        stacked = jnp.concatenate(
            [
                jnp.concatenate([grid[z + u, v + y] for y in range(CY)], axis=1)
                for u in range(3)
                for v in range(3)
            ],
            axis=0,
        )
        patches[z] = stacked
        pre[...] = jnp.dot(wmat[...], stacked, preferred_element_type=f32)
        for y in range(CY):
            lanes = slice(128 * y, 128 * y + 128)
            low_x = pltpu.roll(pre[0:16, lanes], 1, 1)
            high_x = pltpu.roll(pre[32:48, lanes], X - 1, 1)
            value = (
                pre[16:32, lanes]
                + jnp.where(first_x, 0.0, low_x)
                + jnp.where(last_x, 0.0, high_x)
            )
            sigma = sigmoid(value)
            group = 4 * z + y // 2
            half = slice(128 * (y % 2), 128 * (y % 2) + 128)
            act[16 * group : 16 * group + 16, half] = (value * sigma).astype(bf16)
            cot_sum = acc_cot[16 * group : 16 * group + 16, half]
            gpad[z + 1, y + 1] = (cot_sum * sigma * (1.0 + value * (1.0 - sigma))).astype(bf16)

    def move(plane, row):
        value = gpad[plane, row]
        wide = value.astype(f32)
        gp3[plane, row, 0:16] = jnp.where(last_x, 0.0, pltpu.roll(wide, X - 1, 1)).astype(bf16)
        gp3[plane, row, 16:32] = value
        gp3[plane, row, 32:48] = jnp.where(first_x, 0.0, pltpu.roll(wide, 1, 1)).astype(bf16)

    wide_grad = jnp.zeros((48, 144), f32)
    for z in range(CZ):
        for y in range(CY):
            move(z + 1, y + 1)
        moved = jnp.concatenate([gp3[z + 1, y + 1] for y in range(CY)], axis=1)
        wide_grad += lax.dot_general(moved, patches[z], NT, preferred_element_type=f32)
    compact = jnp.zeros((CH, 128), f32)
    for col_k in range(3):
        kept = jnp.where(same_group, wide_grad[16 * col_k : 16 * col_k + 16], 0.0)
        compact += jnp.dot(
            kept.astype(bf16), spread[col_k].astype(bf16), preferred_element_type=f32
        )
    part[...] = compact.astype(bf16)

    def reduce_send(step, peers, source, target):
        if comm:
            for d, place in enumerate(peers):
                pltpu.make_async_remote_copy(
                    src_ref=source, dst_ref=target.at[d], send_sem=red_send.at[step],
                    recv_sem=red_recv.at[step], device_id=place, device_id_type=MESH,
                ).start()

    def reduce_wait(step, buffer):
        if comm:
            pltpu.make_async_copy(buffer, buffer, red_recv.at[step]).wait()
            wait_sent.append(pltpu.make_async_copy(buffer, buffer, red_send.at[step]).wait)

    reduce_send(0, peers_1, part, gather_1)
    second = (send_2, recv_2)
    finish_halo = []

    def send_2nd(src, dst, place, da, db):
        finish_halo.append(send(src, dst, second, place, da, db))

    send_2nd(gpad.at[1, pl.ds(1, 8)], gpad.at[3, pl.ds(1, 8)], 0, -1, 0)
    send_2nd(gpad.at[2, pl.ds(1, 8)], gpad.at[0, pl.ds(1, 8)], 1, 1, 0)
    send_2nd(gpad.at[pl.ds(1, 2), 1], gpad.at[pl.ds(1, 2), 9], 2, 0, -1)
    send_2nd(gpad.at[pl.ds(1, 2), 8], gpad.at[pl.ds(1, 2), 0], 3, 0, 1)
    send_2nd(gpad.at[1, 1], gpad.at[3, 9], 4, -1, -1)
    send_2nd(gpad.at[1, 8], gpad.at[3, 0], 5, -1, 1)
    send_2nd(gpad.at[2, 1], gpad.at[0, 9], 6, 1, -1)
    send_2nd(gpad.at[2, 8], gpad.at[0, 0], 7, 1, 1)


    def read_back(values, into):
        def body(k, carry):
            found = jnp.dot(values[...], onehots[k], preferred_element_type=f32)
            into[:, pl.ds(pl.multiple_of(k * S, 128), S)] = select(found, codes[k])
            return carry

        lax.fori_loop(0, ALL, body, 0, unroll=5)

    read_back(act, out_buf)

    reduce_wait(0, gather_1)
    total = compact
    for d in range(31):
        total = total + gather_1[d].astype(f32)
    plane_sum[...] = total.astype(bf16)
    reduce_send(1, peers_2, plane_sum, gather_2)

    for finish in finish_halo:
        finish()
    blank = jnp.zeros((CH, X), bf16)

    def clear(flag, places):
        @pl.when(flag)
        def _():
            for plane, row in places:
                gpad[plane, row] = blank

    clear(a == 0, [(0, row) for row in range(10)])
    clear(a == n_a - 1, [(3, row) for row in range(10)])
    clear(b == 0, [(plane, 0) for plane in range(4)])
    clear(b == n_b - 1, [(plane, 9) for plane in range(4)])
    for plane in range(4):
        for row in range(10):
            if plane in (0, 3) or row in (0, 9):
                move(plane, row)
    result = [None] * 16
    for plane in range(4):
        moved = jnp.concatenate([gp3[plane, row] for row in range(10)], axis=1)
        taps = lax.dot_general(
            wmat[...], moved, (((0,), (0,)), ((), ())), preferred_element_type=f32
        )
        for u in range(3):
            z = plane - 2 + u
            if z not in (0, 1):
                continue
            for v in range(3):
                rows = slice(16 * (3 * u + v), 16 * (3 * u + v) + 16)
                for y in range(CY):
                    source = y + 2 - v
                    term = taps[rows, 128 * source : 128 * source + 128]
                    i = 8 * z + y
                    result[i] = term if result[i] is None else result[i] + term
    for i in range(16):
        group = i // 2
        half = slice(128 * (i % 2), 128 * (i % 2) + 128)
        table[16 * group : 16 * group + 16, half] = (result[i] / divisors[i]).astype(bf16)
    read_back(table, grad_buf)

    reduce_wait(1, gather_2)
    for d in range(7):
        total = total + gather_2[d].astype(f32)
    for wait in wait_sent:
        wait()
    wgrad_ref[...] = total * (1.0 / math.sqrt(CZ * CY * X * n_a * n_b))


def copy_kernel(out, grad, total, out_hbm, grad_hbm, wgrad_hbm, wgrad, sem):
    copies = [
        pltpu.make_async_copy(src, dst, sem.at[i])
        for i, (src, dst) in enumerate(((out, out_hbm), (grad, grad_hbm), (wgrad, wgrad_hbm)))
    ]
    copies[0].start()
    copies[1].start()
    turned = total[...].T
    for i in range(27):
        wgrad[i] = turned[GRP * i : GRP * i + GRP]
    copies[2].start()
    for copy in copies:
        copy.wait()


def fused(feats, cot, cells, slots, count, weight, comm=True):
    hbm = pl.BlockSpec(memory_space=pltpu.HBM)
    vmem = pl.BlockSpec(memory_space=pltpu.VMEM)
    slots_all = ALL * S
    dma = pltpu.SemaphoreType.DMA
    shape = jax.ShapeDtypeStruct
    feats, cot, cells, slots, count, weight = (
        pltpu.with_memory_space_constraint(v, pltpu.HBM)
        for v in (feats, cot, cells, slots, count, weight)
    )
    parts = pl.pallas_call(
        functools.partial(kernel, comm=comm),
        out_shape=[
            shape((CH, slots_all), bf16),
            shape((CH, slots_all), bf16),
            shape((CH, 128), f32),
        ],
        in_specs=[hbm] * 6,
        out_specs=[vmem] * 3,
        scratch_shapes=[
            pltpu.VMEM((ALL, LO, S), bf16),
            pltpu.VMEM((ALL, 1, S), f32),
            pltpu.VMEM((128, LO), bf16),
            pltpu.VMEM((CH, OWN * S), bf16),
            pltpu.VMEM((CH, slots_all), bf16),
            pltpu.VMEM((112, 128), jnp.int32),
            pltpu.VMEM((1, 2, S), jnp.int32),
            pltpu.VMEM((1, 2), jnp.int32),
            pltpu.VMEM((27, GRP, CH), bf16),
            pltpu.VMEM((OWN, 1, S), f32),
            pltpu.VMEM((272, LO), f32),
            pltpu.VMEM((128, LO), f32),
            pltpu.VMEM((2, 1, S), f32),
            pltpu.VMEM((2, 1, S), f32),
            pltpu.VMEM((18, CH, 128), bf16),
            pltpu.VMEM((18, CH, 128), bf16),
            pltpu.VMEM((18, CH, 128), bf16),
            pltpu.VMEM((18, CH, 128), bf16),
            pltpu.VMEM((2, 5, CH, 128), bf16),
            pltpu.VMEM((2, 5, CH, 128), bf16),
            pltpu.VMEM((4, 3, CH, 128), bf16),
            pltpu.VMEM((4, 3, CH, 128), bf16),
            pltpu.VMEM((4, 10, CH, 128), bf16),
            pltpu.VMEM((4, 10, CH, 128), bf16),
            pltpu.VMEM((CZ, 144, CY * X), bf16),
            pltpu.VMEM((4, 10, 48, 128), bf16),
            pltpu.VMEM((128, LO), bf16),
            pltpu.VMEM((16, CH, 128), f32),
            pltpu.VMEM((48, 144), bf16),
            pltpu.VMEM((10, CH, 128), f32),
            pltpu.VMEM((48, CY * X), f32),
            pltpu.VMEM((CH, 128), bf16),
            pltpu.VMEM((31, CH, 128), bf16),
            pltpu.VMEM((CH, 128), bf16),
            pltpu.VMEM((7, CH, 128), bf16),
            dma((6,)),
            dma((10,)),
            dma((10,)),
            dma((8,)),
            dma((8,)),
            dma((2,)),
            dma((2,)),
        ],
        compiler_params=pltpu.CompilerParams(
            vmem_limit_bytes=30 << 20,
            **(dict(collective_id=0, has_side_effects=True) if comm else {}),
        ),
    )(feats, cot, cells, slots, count, weight)
    return pl.pallas_call(
        copy_kernel,
        out_shape=[
            shape((CH, slots_all), bf16),
            shape((CH, slots_all), bf16),
            shape((27, GRP, CH), f32),
        ],
        in_specs=[vmem] * 3,
        out_specs=[hbm] * 3,
        scratch_shapes=[pltpu.VMEM((27, GRP, CH), f32), dma((3,))],
    )(*(pltpu.with_memory_space_constraint(v, pltpu.VMEM) for v in parts))


def local(point_feats, cell_index, send_slots, send_count, conv_weight, point_cot):
    cells = cell_index.reshape(-1, 128)
    weight = conv_weight.transpose(2, 3, 4, 1, 0).reshape(27, GRP, CH)
    out, grad, wgrad = fused(point_feats, point_cot, cells, send_slots, send_count, weight)
    return out, grad, wgrad.reshape(3, 3, 3, GRP, CH).transpose(4, 3, 0, 1, 2)


def solution(mesh):
    placed = (
        P(None, ("gz", "gy")),
        P(("gz", "gy")),
        P(("gz", "gy"), None, None),
        P(("gz", "gy"), None),
        P(),
        P(None, ("gz", "gy")),
    )
    return jax.shard_map(
        local,
        mesh=mesh,
        in_specs=placed,
        out_specs=(P(None, ("gz", "gy")), P(None, ("gz", "gy")), P()),
        check_vma=False,
    )
```

```python
import functools
import math

import jax
import jax.numpy as jnp
from jax import lax
from jax.experimental import pallas as pl
from jax.experimental.pallas import tpu as pltpu
from jax.sharding import PartitionSpec as P

CH = 16
GRP = 4
X = 128
CY = 8
CZ = 2
S = 1792
OWN = 8
ALL = OWN + 2
LO = 256
MESH = pl.DeviceIdType.MESH
f32 = jnp.float32
bf16 = jnp.bfloat16
NT = (((1,), (1,)), ((), ()))

UP_MSG = tuple(range(4, 12))
DOWN_MSG = (0, 1, 2, 3, 12, 13, 14, 15)
STAY = (0, 1, 2, 3, 8, 9, 10, 11)


def links(d):
    step_y, step_x, step_b = (0, 1, 2, 1)[d // 8], d // 4 % 2, d % 4
    return step_y + (2 - step_x if step_b == 2 else max(step_x, step_b % 2))


FAR_FIRST = sorted(range(1, 32), key=links, reverse=True)


def one_hot(row, count):
    ids = lax.broadcasted_iota(jnp.int32, (count, row.shape[1]), 0).astype(f32).astype(bf16)
    return jnp.where(ids == row, jnp.ones((), bf16), jnp.zeros((), bf16))


def masked_rows(row, values, codes):
    zero = jnp.zeros((), bf16)
    return [jnp.where(row == jnp.full((), code, bf16), values, zero) for code in codes]


def sigmoid(v):
    return 1.0 / (1.0 + jnp.exp(-v))


def select(found, row):
    value = jnp.zeros((CH, S), f32)
    for i, number in enumerate(STAY):
        value = jnp.where(row == float(number), found[16 * i : 16 * i + 16], value)
    return value.astype(bf16)


def kernel(
    feats_hbm, cot_hbm, cells_hbm, slots_hbm, count_hbm, weight_hbm,
    out_buf, grad_buf, wgrad_ref,
    onehots, codes, table, feats, cot, cells_ref, slots_ref, count_ref, weight_ref, lows, acc, acc_cot,
    list_send, list_recv,
    up_send, down_send, up_recv, down_recv,
    side_send, side_recv, corner_send, corner_recv,
    grid, gpad, patches, gp3, act, divisors, wmat, counts_in, pre,
    part, gather_1, plane_sum, gather_2,
    load_sem, send_sem, recv_sem, send_2, recv_2, red_send, red_recv,
    *, comm,
):
    a = lax.axis_index("gz")
    b = lax.axis_index("gy")
    n_a = lax.axis_size("gz")
    n_b = lax.axis_size("gy")
    z_p = a // 8
    y_p = lax.rem(a // 2, 4)
    x_p = lax.rem(a, 2)

    loads = [
        pltpu.make_async_copy(src, dst, load_sem.at[i])
        for i, (src, dst) in enumerate(
            (
                (cells_hbm, cells_ref), (slots_hbm, slots_ref), (count_hbm, count_ref),
                (feats_hbm, feats), (weight_hbm, weight_ref), (cot_hbm, cot),
            )
        )
    ]
    for load in loads:
        load.start()
    load_cells, load_slots, load_count, load_feats, load_weight, load_cot = loads

    a_near = {-1: lax.rem(a + n_a - 1, n_a), 0: a, 1: lax.rem(a + 1, n_a)}
    b_all = [b] + [lax.rem(b + k, n_b) for k in range(1, 4)]
    plane_all = [
        lax.rem(y_p + k // 2, 4) * 2 + (1 - x_p if k % 2 else x_p) for k in range(8)
    ]
    peers_1 = [(z_p * 8 + plane_all[d // 4], b_all[d % 4]) for d in FAR_FIRST]
    peers_2 = [(lax.rem(z_p + k, 8) * 8 + plane_all[0], b) for k in (4, 3, 5, 2, 6, 1, 7)]

    def near(da, db):
        return (a_near[da], b_all[db % 4])

    around = [(da, db) for da in (-1, 0, 1) for db in (-1, 0, 1) if (da, db) != (0, 0)]
    if comm:
        barrier = pltpu.get_barrier_semaphore()
        for place in peers_2 + peers_1 + [near(da, db) for da, db in around]:
            pl.semaphore_signal(barrier, inc=1, device_id=place, device_id_type=MESH)

    tap_row = lax.broadcasted_iota(jnp.int32, (144, 128), 0)
    tap_col = lax.broadcasted_iota(jnp.int32, (144, 128), 1)
    tap_base = jnp.bitwise_and(tap_row, 3) + jnp.right_shift(tap_row, 4) * (3 * GRP)
    spread = [tap_base + GRP * col_k == tap_col for col_k in range(3)]
    out_ch = lax.broadcasted_iota(jnp.int32, (CH, 144), 0)
    in_ch = jnp.bitwise_and(lax.broadcasted_iota(jnp.int32, (CH, 144), 1), 15)
    same_group = jnp.right_shift(out_ch, 2) == jnp.right_shift(in_ch, 2)
    load_cells.wait()
    load_slots.wait()
    load_count.wait()
    cells = jnp.concatenate(
        [cells_ref[pl.ds(0, 56, stride=2), :], cells_ref[pl.ds(1, 56, stride=2), :]], axis=1
    )
    cell_y = jnp.right_shift(jnp.bitwise_and(cells, 1023), 7) * 128
    cell_x = jnp.bitwise_and(cells, 127)
    pad = jnp.zeros((8, LO), f32)
    cell_table = jnp.concatenate(
        [cell_y.astype(f32), pad, cell_x.astype(f32), pad], axis=0
    ).astype(bf16)
    lane = lax.broadcasted_iota(jnp.int32, (1, S), 1)
    leaving = jnp.zeros((64, LO), f32)
    for side in range(2):
        listed = lane < count_ref[:, side : side + 1]
        slot = slots_ref[0, side : side + 1, :]
        slot_hi = jnp.where(listed, jnp.right_shift(slot, 8), -1)
        hot_lo = one_hot(jnp.bitwise_and(slot, 255).astype(f32).astype(bf16), LO)
        hot_hi = lax.broadcasted_iota(jnp.int32, (64, S), 0) == slot_hi
        leaving += lax.dot_general(
            hot_hi.astype(f32).astype(bf16), hot_lo, NT, preferred_element_type=f32
        )
        found = jnp.dot(cell_table, hot_lo, preferred_element_type=f32)
        place = jnp.sum(jnp.where(hot_hi, found[:64] + found[64:], 0.0), axis=0, keepdims=True)
        list_send[side] = jnp.where(listed, place, -1.0)
    code = (
        jnp.bitwise_and(jnp.right_shift(cells, 8), 3) + jnp.right_shift(cells, 10) * 8
    ).astype(f32) + 4.0 * leaving[:56]
    low = jnp.bitwise_and(cells, 255).astype(f32)
    for row in range(7 * OWN):
        k, j = divmod(row, 7)
        codes[k, :, LO * j : LO * (j + 1)] = code[row : row + 1]
        lows[k, :, LO * j : LO * (j + 1)] = low[row : row + 1]

    load_feats.wait()
    acc[...] = jnp.zeros_like(acc)

    def splat_own(k, carry):
        hot = one_hot(lows[k].astype(bf16), LO)
        onehots[k] = hot
        row = codes[k].astype(bf16)
        values = feats[:, pl.ds(pl.multiple_of(k * S, 128), S)]
        rows = masked_rows(row, values, range(16)) + [one_hot(row, 16)]
        acc[...] += lax.dot_general(
            jnp.concatenate(rows, axis=0), hot, NT, preferred_element_type=f32
        )
        return carry

    lax.fori_loop(0, OWN, splat_own, 0, unroll=4)

    counts = acc[256:272, :]
    count_hi = jnp.floor(counts * (1.0 / 256.0))
    count_lo = counts - 256.0 * count_hi

    def block(number, row):
        lanes = slice(128 * (row % 2), 128 * (row % 2) + 128)
        return acc[16 * number : 16 * number + 16, lanes].astype(bf16)

    def rows_of(numbers, first_row):
        return [block(4 * plane + first_row // 2, first_row) for plane in numbers]

    for ref, members in ((up_send, UP_MSG), (down_send, DOWN_MSG)):
        for i, number in enumerate(members):
            ref[2 * i] = block(number, 0)
            ref[2 * i + 1] = block(number, 1)
        both = jnp.concatenate(
            [part_of[c : c + 4] for part_of in (count_lo, count_hi) for c in members[::4]], axis=0
        ).astype(bf16)
        ref[16] = both[:, :128]
        ref[17] = both[:, 128:]
    nothing = jnp.zeros((8, 128), f32)
    for side in range(2):
        lanes = slice(128 * side, 128 * side + 128)
        rows = [
            part_of[4 * plane + 3 * side : 4 * plane + 3 * side + 1, lanes]
            for part_of in (count_lo, count_hi)
            for plane in range(4)
        ]
        tile = jnp.concatenate(rows + [nothing], axis=0).astype(bf16)
        for plane in range(4):
            side_send[side, plane] = block(4 * plane + 3 * side, side)
        side_send[side, 4] = tile
        for vertical, planes in ((0, (0, 3)), (1, (1, 2))):
            for i, plane in enumerate(planes):
                corner_send[2 * vertical + side, i] = block(4 * plane + 3 * side, side)
            corner_send[2 * vertical + side, 2] = tile

    def inside(da, db):
        tests = []
        if da:
            tests.append(a < n_a - 1 if da > 0 else a > 0)
        if db:
            tests.append(b < n_b - 1 if db > 0 else b > 0)
        return tests[0] if len(tests) == 1 else jnp.logical_and(*tests)

    wait_sent = []

    def send(src, dst, sems, place, da, db):
        if not comm:
            return lambda: None
        copy = pltpu.make_async_remote_copy(
            src_ref=src, dst_ref=dst, send_sem=sems[0].at[place],
            recv_sem=sems[1].at[place], device_id=near(da, db), device_id_type=MESH,
        )

        @pl.when(inside(da, db))
        def _():
            copy.start()

        def sent():
            @pl.when(inside(da, db))
            def _():
                copy.wait_send()

        def finish():
            @pl.when(inside(-da, -db))
            def _():
                copy.wait_recv()

        wait_sent.append(sent)

        return finish

    if comm:
        pl.semaphore_wait(barrier, len(around) + len(peers_1) + len(peers_2))
    first = (send_sem, recv_sem)
    finish_lists = [
        send(list_send.at[0], list_recv.at[1], first, 0, -1, 0),
        send(list_send.at[1], list_recv.at[0], first, 1, 1, 0),
    ]
    finish_grid = [
        send(up_send, up_recv, first, 2, 1, 0),
        send(down_send, down_recv, first, 3, -1, 0),
    ]
    for side in range(2):
        db = 2 * side - 1
        finish_grid.append(send(side_send.at[side], side_recv.at[side], first, 4 + side, 0, db))
        for vertical in range(2):
            i = 2 * vertical + side
            finish_grid.append(
                send(corner_send.at[i], corner_recv.at[i], first, 6 + i, 2 * vertical - 1, db)
            )

    load_weight.wait()
    weight = jnp.concatenate(
        [weight_ref[i].astype(f32) for i in range(27)] + [jnp.zeros((20, CH), f32)], axis=0
    ).T.astype(bf16)
    for col_k in range(3):
        picked = lax.dot_general(
            weight, spread[col_k].astype(bf16), NT, preferred_element_type=f32
        )
        wmat[16 * col_k : 16 * col_k + 16, :] = jnp.where(same_group, picked, 0.0).astype(bf16)

    load_cot.wait()
    acc_cot[...] = jnp.zeros_like(acc_cot)

    def splat_cot(k, carry):
        row = codes[k].astype(bf16)
        values = cot[:, pl.ds(pl.multiple_of(k * S, 128), S)]
        acc_cot[...] += lax.dot_general(
            jnp.concatenate(masked_rows(row, values, STAY), axis=0), onehots[k], NT,
            preferred_element_type=f32,
        )
        return carry

    lax.fori_loop(0, OWN, splat_cot, 0, unroll=4)

    for finish in finish_lists:
        finish()
    for side in range(2):
        present = (a > 0) if side == 0 else (a < n_a - 1)
        place = jnp.where(present, list_recv[side], -1.0).astype(jnp.int32)
        live = place >= 0
        row = jnp.where(live, jnp.right_shift(place, 8) + 8 * side, 16).astype(f32)
        codes[OWN + side] = row
        hot = one_hot(jnp.bitwise_and(place, 255).astype(f32).astype(bf16), LO)
        onehots[OWN + side] = hot
        values = cot[:, (OWN + side) * S : (OWN + side + 1) * S]
        members = STAY[4 * side : 4 * side + 4]
        acc_cot[64 * side : 64 * side + 64, :] += lax.dot_general(
            jnp.concatenate(masked_rows(row.astype(bf16), values, members), axis=0), hot, NT,
            preferred_element_type=f32,
        )

    for finish in finish_grid:
        finish()
    has_below = a > 0
    has_above = a < n_a - 1
    has_left = b > 0
    has_right = b < n_b - 1

    for i, (ref, flag) in enumerate(((up_recv, has_below), (down_recv, has_above))):
        for half in range(2):
            both = ref[16 + half].astype(f32)
            counts_in[2 * i + half, 0:8] = jnp.where(flag, both[0:8] + 256.0 * both[8:16], 0.0)
    side_flag = (has_right, has_left)
    for side in range(2):
        for i, (ref, at) in enumerate(
            ((side_recv.at[side], 4), (corner_recv.at[side], 2), (corner_recv.at[2 + side], 2))
        ):
            flag = side_flag[side]
            if i == 1:
                flag = jnp.logical_and(flag, has_above)
            if i == 2:
                flag = jnp.logical_and(flag, has_below)
            both = ref[at].astype(f32)
            counts_in[4 + 2 * i + side, 0:4] = jnp.where(flag, both[0:4] + 256.0 * both[4:8], 0.0)

    def mean(sums, count):
        return sums / jnp.maximum(count, 1.0)

    sources = (
        (3, up_recv, 4, 0, has_below),
        (0, up_recv, 0, 0, has_below),
        (2, down_recv, 4, 2, has_above),
        (1, down_recv, 0, 2, has_above),
    )
    for plane, (mine, ref, at, where, flag) in enumerate(sources):
        for row in range(8):
            half = row % 2
            lanes = slice(128 * half, 128 * half + 128)
            number = 4 * mine + row // 2
            other = at + row // 2
            got = ref[2 * (at + row // 2) + half].astype(f32)
            sums = acc[16 * number : 16 * number + 16, lanes] + jnp.where(flag, got, 0.0)
            count = acc[256 + number : 257 + number, lanes]
            count = count + counts_in[where + half, other : other + 1, :]
            divisor = jnp.broadcast_to(jnp.maximum(count, 1.0), (CH, 128))
            grid[plane, 1 + row] = (sums / divisor).astype(bf16)
            if plane in (1, 2):
                divisors[8 * (plane - 1) + row] = divisor
    for side in range(2):
        flag = side_flag[side]
        halo = (
            (3, 1, 1, 2, has_below),
            (0, 1, 0, 1, has_below),
            (2, 0, 1, 3, has_above),
            (1, 0, 0, 0, has_above),
        )
        for plane, (direct, vertical, at, theirs, vertical_flag) in enumerate(halo):
            corner = 2 * vertical + side
            both = jnp.logical_and(flag, vertical_flag)
            sums = jnp.where(flag, side_recv[side, direct].astype(f32), 0.0)
            sums = sums + jnp.where(both, corner_recv[corner, at].astype(f32), 0.0)
            kind = 6 if vertical == 0 else 8
            count = counts_in[4 + side, direct : direct + 1, :]
            count = count + counts_in[kind + side, theirs : theirs + 1, :]
            grid[plane, 9 * (1 - side)] = mean(sums, count).astype(bf16)

    lane = lax.broadcasted_iota(jnp.int32, (CH, X), 1)
    first_x = lane == 0
    last_x = lane == X - 1
    for z in range(CZ):
        stacked = jnp.concatenate(
            [
                jnp.concatenate([grid[z + u, v + y] for y in range(CY)], axis=1)
                for u in range(3)
                for v in range(3)
            ],
            axis=0,
        )
        patches[z] = stacked
        pre[...] = jnp.dot(wmat[...], stacked, preferred_element_type=f32)
        for y in range(CY):
            lanes = slice(128 * y, 128 * y + 128)
            low_x = pltpu.roll(pre[0:16, lanes], 1, 1)
            high_x = pltpu.roll(pre[32:48, lanes], X - 1, 1)
            value = (
                pre[16:32, lanes]
                + jnp.where(first_x, 0.0, low_x)
                + jnp.where(last_x, 0.0, high_x)
            )
            sigma = sigmoid(value)
            group = 4 * z + y // 2
            half = slice(128 * (y % 2), 128 * (y % 2) + 128)
            act[16 * group : 16 * group + 16, half] = (value * sigma).astype(bf16)
            cot_sum = acc_cot[16 * group : 16 * group + 16, half]
            gpad[z + 1, y + 1] = (cot_sum * sigma * (1.0 + value * (1.0 - sigma))).astype(bf16)

    def move(plane, row):
        value = gpad[plane, row]
        wide = value.astype(f32)
        gp3[plane, row, 0:16] = jnp.where(last_x, 0.0, pltpu.roll(wide, X - 1, 1)).astype(bf16)
        gp3[plane, row, 16:32] = value
        gp3[plane, row, 32:48] = jnp.where(first_x, 0.0, pltpu.roll(wide, 1, 1)).astype(bf16)

    wide_grad = jnp.zeros((48, 144), f32)
    for z in range(CZ):
        for y in range(CY):
            move(z + 1, y + 1)
        moved = jnp.concatenate([gp3[z + 1, y + 1] for y in range(CY)], axis=1)
        wide_grad += lax.dot_general(moved, patches[z], NT, preferred_element_type=f32)
    compact = jnp.zeros((CH, 128), f32)
    for col_k in range(3):
        kept = jnp.where(same_group, wide_grad[16 * col_k : 16 * col_k + 16], 0.0)
        compact += jnp.dot(
            kept.astype(bf16), spread[col_k].astype(bf16), preferred_element_type=f32
        )
    part[...] = compact.astype(bf16)

    def reduce_send(step, peers, source, target):
        if comm:
            for d, place in enumerate(peers):
                pltpu.make_async_remote_copy(
                    src_ref=source, dst_ref=target.at[d], send_sem=red_send.at[step],
                    recv_sem=red_recv.at[step], device_id=place, device_id_type=MESH,
                ).start()

    def reduce_wait(step, buffer):
        if comm:
            pltpu.make_async_copy(buffer, buffer, red_recv.at[step]).wait()
            wait_sent.append(pltpu.make_async_copy(buffer, buffer, red_send.at[step]).wait)

    reduce_send(0, peers_1, part, gather_1)
    second = (send_2, recv_2)
    finish_halo = []

    def send_2nd(src, dst, place, da, db):
        finish_halo.append(send(src, dst, second, place, da, db))

    send_2nd(gpad.at[1, pl.ds(1, 8)], gpad.at[3, pl.ds(1, 8)], 0, -1, 0)
    send_2nd(gpad.at[2, pl.ds(1, 8)], gpad.at[0, pl.ds(1, 8)], 1, 1, 0)
    send_2nd(gpad.at[pl.ds(1, 2), 1], gpad.at[pl.ds(1, 2), 9], 2, 0, -1)
    send_2nd(gpad.at[pl.ds(1, 2), 8], gpad.at[pl.ds(1, 2), 0], 3, 0, 1)
    send_2nd(gpad.at[1, 1], gpad.at[3, 9], 4, -1, -1)
    send_2nd(gpad.at[1, 8], gpad.at[3, 0], 5, -1, 1)
    send_2nd(gpad.at[2, 1], gpad.at[0, 9], 6, 1, -1)
    send_2nd(gpad.at[2, 8], gpad.at[0, 0], 7, 1, 1)


    def read_back(values, into):
        def body(k, carry):
            found = jnp.dot(values[...], onehots[k], preferred_element_type=f32)
            into[:, pl.ds(pl.multiple_of(k * S, 128), S)] = select(found, codes[k])
            return carry

        lax.fori_loop(0, ALL, body, 0, unroll=10)

    read_back(act, out_buf)

    reduce_wait(0, gather_1)
    total = compact
    for d in range(31):
        total = total + gather_1[d].astype(f32)
    plane_sum[...] = total.astype(bf16)
    reduce_send(1, peers_2, plane_sum, gather_2)

    for finish in finish_halo:
        finish()
    blank = jnp.zeros((CH, X), bf16)

    def clear(flag, places):
        @pl.when(flag)
        def _():
            for plane, row in places:
                gpad[plane, row] = blank

    clear(a == 0, [(0, row) for row in range(10)])
    clear(a == n_a - 1, [(3, row) for row in range(10)])
    clear(b == 0, [(plane, 0) for plane in range(4)])
    clear(b == n_b - 1, [(plane, 9) for plane in range(4)])
    for plane in range(4):
        for row in range(10):
            if plane in (0, 3) or row in (0, 9):
                move(plane, row)
    result = [None] * 16
    for plane in range(4):
        moved = jnp.concatenate([gp3[plane, row] for row in range(10)], axis=1)
        taps = lax.dot_general(
            wmat[...], moved, (((0,), (0,)), ((), ())), preferred_element_type=f32
        )
        for u in range(3):
            z = plane - 2 + u
            if z not in (0, 1):
                continue
            for v in range(3):
                rows = slice(16 * (3 * u + v), 16 * (3 * u + v) + 16)
                for y in range(CY):
                    source = y + 2 - v
                    term = taps[rows, 128 * source : 128 * source + 128]
                    i = 8 * z + y
                    result[i] = term if result[i] is None else result[i] + term
    for i in range(16):
        group = i // 2
        half = slice(128 * (i % 2), 128 * (i % 2) + 128)
        table[16 * group : 16 * group + 16, half] = (result[i] / divisors[i]).astype(bf16)
    read_back(table, grad_buf)

    reduce_wait(1, gather_2)
    for d in range(7):
        total = total + gather_2[d].astype(f32)
    for wait in wait_sent:
        wait()
    wgrad_ref[...] = total * (1.0 / math.sqrt(CZ * CY * X * n_a * n_b))


def copy_kernel(out, grad, total, out_hbm, grad_hbm, wgrad_hbm, wgrad, sem):
    copies = [
        pltpu.make_async_copy(src, dst, sem.at[i])
        for i, (src, dst) in enumerate(((out, out_hbm), (grad, grad_hbm), (wgrad, wgrad_hbm)))
    ]
    copies[0].start()
    copies[1].start()
    turned = total[...].T
    for i in range(27):
        wgrad[i] = turned[GRP * i : GRP * i + GRP]
    copies[2].start()
    for copy in copies:
        copy.wait()


def fused(feats, cot, cells, slots, count, weight, comm=True):
    hbm = pl.BlockSpec(memory_space=pltpu.HBM)
    vmem = pl.BlockSpec(memory_space=pltpu.VMEM)
    slots_all = ALL * S
    dma = pltpu.SemaphoreType.DMA
    shape = jax.ShapeDtypeStruct
    feats, cot, cells, slots, count, weight = (
        pltpu.with_memory_space_constraint(v, pltpu.HBM)
        for v in (feats, cot, cells, slots, count, weight)
    )
    parts = pl.pallas_call(
        functools.partial(kernel, comm=comm),
        out_shape=[
            shape((CH, slots_all), bf16),
            shape((CH, slots_all), bf16),
            shape((CH, 128), f32),
        ],
        in_specs=[hbm] * 6,
        out_specs=[vmem] * 3,
        scratch_shapes=[
            pltpu.VMEM((ALL, LO, S), bf16),
            pltpu.VMEM((ALL, 1, S), f32),
            pltpu.VMEM((128, LO), bf16),
            pltpu.VMEM((CH, OWN * S), bf16),
            pltpu.VMEM((CH, slots_all), bf16),
            pltpu.VMEM((112, 128), jnp.int32),
            pltpu.VMEM((1, 2, S), jnp.int32),
            pltpu.VMEM((1, 2), jnp.int32),
            pltpu.VMEM((27, GRP, CH), bf16),
            pltpu.VMEM((OWN, 1, S), f32),
            pltpu.VMEM((272, LO), f32),
            pltpu.VMEM((128, LO), f32),
            pltpu.VMEM((2, 1, S), f32),
            pltpu.VMEM((2, 1, S), f32),
            pltpu.VMEM((18, CH, 128), bf16),
            pltpu.VMEM((18, CH, 128), bf16),
            pltpu.VMEM((18, CH, 128), bf16),
            pltpu.VMEM((18, CH, 128), bf16),
            pltpu.VMEM((2, 5, CH, 128), bf16),
            pltpu.VMEM((2, 5, CH, 128), bf16),
            pltpu.VMEM((4, 3, CH, 128), bf16),
            pltpu.VMEM((4, 3, CH, 128), bf16),
            pltpu.VMEM((4, 10, CH, 128), bf16),
            pltpu.VMEM((4, 10, CH, 128), bf16),
            pltpu.VMEM((CZ, 144, CY * X), bf16),
            pltpu.VMEM((4, 10, 48, 128), bf16),
            pltpu.VMEM((128, LO), bf16),
            pltpu.VMEM((16, CH, 128), f32),
            pltpu.VMEM((48, 144), bf16),
            pltpu.VMEM((10, CH, 128), f32),
            pltpu.VMEM((48, CY * X), f32),
            pltpu.VMEM((CH, 128), bf16),
            pltpu.VMEM((31, CH, 128), bf16),
            pltpu.VMEM((CH, 128), bf16),
            pltpu.VMEM((7, CH, 128), bf16),
            dma((6,)),
            dma((10,)),
            dma((10,)),
            dma((8,)),
            dma((8,)),
            dma((2,)),
            dma((2,)),
        ],
        compiler_params=pltpu.CompilerParams(
            vmem_limit_bytes=30 << 20,
            **(dict(collective_id=0, has_side_effects=True) if comm else {}),
        ),
    )(feats, cot, cells, slots, count, weight)
    return pl.pallas_call(
        copy_kernel,
        out_shape=[
            shape((CH, slots_all), bf16),
            shape((CH, slots_all), bf16),
            shape((27, GRP, CH), f32),
        ],
        in_specs=[vmem] * 3,
        out_specs=[hbm] * 3,
        scratch_shapes=[pltpu.VMEM((27, GRP, CH), f32), dma((3,))],
    )(*(pltpu.with_memory_space_constraint(v, pltpu.VMEM) for v in parts))


def local(point_feats, cell_index, send_slots, send_count, conv_weight, point_cot):
    cells = cell_index.reshape(-1, 128)
    weight = conv_weight.transpose(2, 3, 4, 1, 0).reshape(27, GRP, CH)
    out, grad, wgrad = fused(point_feats, point_cot, cells, send_slots, send_count, weight)
    return out, grad, wgrad.reshape(3, 3, 3, GRP, CH).transpose(4, 3, 0, 1, 2)


def solution(mesh):
    placed = (
        P(None, ("gz", "gy")),
        P(("gz", "gy")),
        P(("gz", "gy"), None, None),
        P(("gz", "gy"), None),
        P(),
        P(None, ("gz", "gy")),
    )
    return jax.shard_map(
        local,
        mesh=mesh,
        in_specs=placed,
        out_specs=(P(None, ("gz", "gy")), P(None, ("gz", "gy")), P()),
        check_vma=False,
    )
```
